32 devices in a mesh: seq: 8 (over z, core), batch: 4 (over y, x).
Axes of the slice: x: 2, y: 2, z: 4, core: 2. Of those that a mesh axis runs over, the one named last changes fastest.
Arguments:
- tokens: bfloat16 [32, 2, 512, 576], P('batch', None, 'seq'), may hold values from -6 to 6
- assign: int32 [32], P('batch'), may hold values from 0 to 31, as said below
- lengths: int32 [32], replicated, may hold values from 128 to 1024, as said below
- gain_attn: bfloat16 [576], replicated, may hold values from 0.5 to 1.5
- query_weight: bfloat16 [576, 576], replicated, may hold values from -0.25 to 0.25
- key_weight: bfloat16 [576, 192], replicated, may hold values from -0.25 to 0.25
- value_weight: bfloat16 [576, 192], replicated, may hold values from -0.25 to 0.25
- out_weight: bfloat16 [576, 576], replicated, may hold values from -2 to 2
- gain_mlp: bfloat16 [576], replicated, may hold values from 0.5 to 1.5
- gate_weight: bfloat16 [576, 1536], replicated, may hold values from -0.25 to 0.25
- up_weight: bfloat16 [576, 1536], replicated, may hold values from -0.25 to 0.25
- down_weight: bfloat16 [1536, 576], replicated, may hold values from -0.15625 to 0.15625
- cotangent: bfloat16 [32, 2, 512, 576], P('batch', None, 'seq'), may hold values from -6 to 6
Outputs:
- block_out: bfloat16 [32, 2, 512, 576], P('batch', None, 'seq')
- input_grad: float32 [32, 2, 512, 576], P('batch', None, 'seq')
- grad_gain_attn: float32 [576], replicated
- grad_query: float32 [576, 576], replicated
- grad_key: float32 [576, 192], replicated
- grad_value: float32 [576, 192], replicated
- grad_out: float32 [576, 576], replicated
- grad_gain_mlp: float32 [576], replicated
- grad_gate: float32 [576, 1536], replicated
- grad_up: float32 [576, 1536], replicated
- grad_down: float32 [1536, 576], replicated
The draws below stay inside these ranges and needn't reach their ends.
Inputs may be any that keep to these rules, and one draw needn't show every extreme that they name: A permutation; batch slot s holds sequence assign[s]. `lengths`: in each block of 8 consecutive batch slots some slot holds a sequence of length 1024; some sequence has length 128.
All inputs are finite; a program needn't handle non-finite values.
Results may differ from the reference program's by a relative error of at most 0.015.
Values may be sent and summed in bfloat16 or wider, within the bound.
No kernel may reach another device: no remote copies, remote signals or barrier semaphores. Data moves between devices by JAX's collectives and lax.ppermute only.
A program may use at most 256 MiB of HBM per device.

```python
import jax
import jax.numpy as jnp
from jax import lax

D = 576
HEADS = 9
KV_HEADS = 3
HEAD_DIM = 64
FF = 1536
SEQS = 8
HALF = 512
SEQ_LEN = 1024
NSEQ_ALL = 32
MIN_LEN = 128


def sequence_layout(key):
    group_count = NSEQ_ALL // SEQS
    order = jax.random.permutation(jax.random.fold_in(key, 11), NSEQ_ALL).astype(jnp.int32)
    drawn = jax.random.randint(jax.random.fold_in(key, 12), (NSEQ_ALL,), MIN_LEN, SEQ_LEN + 1, dtype=jnp.int32)
    picks = jax.random.randint(jax.random.fold_in(key, 13), (group_count,), 0, SEQS, dtype=jnp.int32)
    starts = jnp.arange(group_count, dtype=jnp.int32) * SEQS
    longest = order[starts + picks]
    shortest = order[(picks[0] + 1) % SEQS]
    seq_lengths = drawn.at[shortest].set(MIN_LEN).at[longest].set(SEQ_LEN)
    return (order, seq_lengths)


def draw_assign(key, part):
    order, seq_lengths = sequence_layout(key)
    return order


def draw_lengths(key, part):
    order, seq_lengths = sequence_layout(key)
    return seq_lengths


def shard_levels(own_key, shape, shards, low, high):
    loudness, own = 1.0, jax.random.fold_in(own_key, 6)
    for dim, parts in shards:
        draws = jnp.exp(jax.random.uniform(jax.random.fold_in(own, dim), (parts,), jnp.float32, low / len(shards), high / len(shards)))
        loudness = loudness * jnp.repeat(draws, shape[dim] // parts).reshape([-1 if axis == dim else 1 for axis in range(len(shape))])
    return loudness


def centred(own_key, dims, width, most, split=(), kind=jnp.bfloat16):
    values = width * jax.random.normal(own_key, dims, jnp.float32)
    if split:
        values = values * shard_levels(own_key, dims, split, -0.22, 0.18)
    return jnp.clip(values, -most, most).astype(kind)


def setup_inputs(seed: int = 0) -> dict:
    splits = jax.random.split(jax.random.key(seed), 14)
    tokens = centred(splits[0], (NSEQ_ALL, 2, HALF, D), 1.0, 6.0, ((0, 4), (2, 8)))
    assign = draw_assign(jax.random.fold_in(splits[13], 71), 0)
    lengths = draw_lengths(jax.random.fold_in(splits[13], 71), 0)
    gain_attn = jnp.clip(1.0 + 0.1 * jax.random.normal(splits[3], (D,), jnp.float32), 0.5, 1.5).astype(jnp.bfloat16)
    query_weight = centred(splits[4], (D, D), D ** -0.5, 0.25)
    key_weight = centred(splits[5], (D, KV_HEADS * HEAD_DIM), D ** -0.5, 0.25)
    value_weight = centred(splits[6], (D, KV_HEADS * HEAD_DIM), D ** -0.5, 0.25)
    out_weight = centred(splits[7], (D, D), (D // 64) ** -0.5, 2.0)
    gain_mlp = jnp.clip(1.0 + 0.1 * jax.random.normal(splits[8], (D,), jnp.float32), 0.5, 1.5).astype(jnp.bfloat16)
    gate_weight = centred(splits[9], (D, FF), D ** -0.5, 0.25)
    up_weight = centred(splits[10], (D, FF), D ** -0.5, 0.25)
    down_weight = centred(splits[11], (FF, D), FF ** -0.5, 0.15625)
    cotangent = centred(splits[12], (NSEQ_ALL, 2, HALF, D), 1.0, 6.0, ((0, 4), (2, 8)))
    return dict(tokens=tokens, assign=assign, lengths=lengths, gain_attn=gain_attn, query_weight=query_weight, key_weight=key_weight, value_weight=value_weight, out_weight=out_weight, gain_mlp=gain_mlp, gate_weight=gate_weight, up_weight=up_weight, down_weight=down_weight, cotangent=cotangent)


epsilon = 1e-06
rope_base = 10000.0
masked_score = -1e+30
highest = lax.Precision.HIGHEST

@jax.custom_vjp
def low(v):
    return lax.optimization_barrier(v.astype(jnp.bfloat16)).astype(jnp.float32)

@jax.custom_vjp
def low_back(v):
    return v

def low_keep(v):
    return (low(v), None)

def low_pass(kept, grad):
    return (grad,)

def back_keep(v):
    return (v, None)

def back_low(kept, grad):
    return (low(grad),)
low.defvjp(low_keep, low_pass)
low_back.defvjp(back_keep, back_low)

def matmul(left, right):
    return jnp.einsum('...d,de->...e', left, right, precision=highest)

def rms_scale(values, gain):
    return values * lax.rsqrt(lax.optimization_barrier(jnp.mean(values * values, axis=-1, keepdims=True)) + epsilon) * gain

def rotate(tensor, cosine, sine):
    half_dim = tensor.shape[-1] // 2
    first_half = tensor[..., :half_dim]
    second_half = tensor[..., half_dim:]
    return jnp.concatenate([first_half * cosine - second_half * sine, second_half * cosine + first_half * sine], axis=-1)

def reference(tokens, assign, lengths, gain_attn, query_weight, key_weight, value_weight, out_weight, gain_mlp, gate_weight, up_weight, down_weight, cotangent):
    seq_lens = lengths[assign].astype(jnp.int32)
    row_index = jnp.arange(HALF, dtype=jnp.int32)
    positions = jnp.stack([row_index, SEQ_LEN - 1 - row_index])
    valid = (positions[None, :, :] < seq_lens[:, None, None]).astype(jnp.float32)[..., None]
    frequency = jnp.power(rope_base, -2.0 * jnp.arange(HEAD_DIM // 2, dtype=jnp.float32) / HEAD_DIM)
    angles = positions.astype(jnp.float32)[..., None] * frequency
    cosine = jnp.cos(angles)[:, :, None, :]
    sine = jnp.sin(angles)[:, :, None, :]
    flat_pos = positions.reshape(-1)
    group_size = HEADS // KV_HEADS
    lead_shape = tokens.shape[:3]

    def attend(inputs):
        query_s, key_s, value_s, length_s = inputs
        query_rows = query_s.reshape(SEQ_LEN, KV_HEADS, group_size, HEAD_DIM)
        key_rows = key_s.reshape(SEQ_LEN, KV_HEADS, HEAD_DIM)
        value_rows = value_s.reshape(SEQ_LEN, KV_HEADS, HEAD_DIM)
        raw_scores = jnp.einsum('qcgd,kcd->cgqk', query_rows, key_rows, precision=highest)
        allowed = (flat_pos[None, :] <= flat_pos[:, None]) & (flat_pos[None, :] < length_s)
        scores = jnp.where(allowed, low_back(raw_scores) * HEAD_DIM ** (-0.5), masked_score)
        soft_probs = low(jax.nn.softmax(scores, axis=-1))
        result = jnp.einsum('cgqk,kcd->qcgd', soft_probs, value_rows, precision=highest)
        return result.reshape(2, HALF, D)

    def forward(residual, attn_gain, w_query, w_key, w_value, w_out, mlp_gain, w_gate, w_up, w_down):
        normed = low(rms_scale(residual, attn_gain))
        query_heads = low(rotate(low_back(matmul(normed, w_query)).reshape(lead_shape + (HEADS, HEAD_DIM)), cosine, sine))
        key_heads = low(rotate(low_back(matmul(normed, w_key)).reshape(lead_shape + (KV_HEADS, HEAD_DIM)), cosine, sine))
        value_rows = low(low_back(matmul(normed, w_value)))
        attended = lax.map(jax.checkpoint(attend), (query_heads, key_heads, value_rows, seq_lens))
        attended = low(low_back(attended))
        middle = residual + low_back(matmul(attended, w_out))
        normed_mlp = low(rms_scale(middle, mlp_gain))
        gate_proj = low_back(matmul(normed_mlp, w_gate))
        up_proj = low_back(matmul(normed_mlp, w_up))
        activated = low(jax.nn.silu(gate_proj) * up_proj)
        return valid * (middle + low_back(matmul(activated, w_down)))
    primals = (tokens.astype(jnp.float32), gain_attn.astype(jnp.float32), query_weight.astype(jnp.float32), key_weight.astype(jnp.float32), value_weight.astype(jnp.float32), out_weight.astype(jnp.float32), gain_mlp.astype(jnp.float32), gate_weight.astype(jnp.float32), up_weight.astype(jnp.float32), down_weight.astype(jnp.float32))
    result, pullback = jax.vjp(forward, *primals)
    grads = pullback(cotangent.astype(jnp.float32))
    return (result.astype(jnp.bfloat16), grads[0], grads[1], grads[2], grads[3], grads[4], grads[5], grads[6], grads[7], grads[8], grads[9])
```

```python
import jax
import jax.numpy as jnp
from jax import lax
from jax.sharding import PartitionSpec as P

HEADS = 9
KV_HEADS = 3
HEAD_DIM = 64


epsilon = 1e-06
rope_base = 10000.0
masked_score = -1e30


def matmul(left, right):
    return jnp.dot(left, right, preferred_element_type=jnp.float32)


def weight_grad(left, right):
    return lax.dot_general(
        left, right, (((0,), (0,)), ((), ())), preferred_element_type=jnp.float32
    )


def through(left, right):
    return lax.dot_general(
        left, right, (((1,), (1,)), ((), ())), preferred_element_type=jnp.float32
    )


def rotate(tensor, cosine, sine):
    half_dim = tensor.shape[-1] // 2
    first_half = tensor[..., :half_dim]
    second_half = tensor[..., half_dim:]
    return jnp.concatenate(
        [first_half * cosine - second_half * sine, second_half * cosine + first_half * sine],
        axis=-1,
    )


def rotate_back(incoming, cosine, sine):
    half_dim = incoming.shape[-1] // 2
    first_half = incoming[..., :half_dim]
    second_half = incoming[..., half_dim:]
    return jnp.concatenate(
        [first_half * cosine + second_half * sine, second_half * cosine - first_half * sine],
        axis=-1,
    )


def angles_of(positions):
    frequency = jnp.power(rope_base, -2.0 * jnp.arange(HEAD_DIM // 2, dtype=jnp.float32) / HEAD_DIM)
    angles = positions.astype(jnp.float32)[..., None] * frequency
    return (jnp.cos(angles)[:, :, None, :], jnp.sin(angles)[:, :, None, :])


def norm_forward(values, gain):
    inverse = lax.rsqrt(jnp.mean(values * values, axis=-1, keepdims=True) + epsilon)
    return (inverse, (values * inverse * gain).astype(jnp.bfloat16))


def norm_backward(incoming, values, inverse, gain):
    scaled = incoming * gain
    gain_part = jnp.sum(incoming * values * inverse, axis=(0, 1, 2))
    value_part = inverse * scaled - values * inverse**3 * jnp.mean(
        scaled * values, axis=-1, keepdims=True
    )
    return (value_part, gain_part)


def scores_for(query_s, packed_s, length_s, query_pos, key_pos):
    group_size = HEADS // KV_HEADS
    key_width = KV_HEADS * HEAD_DIM
    query_rows = query_s.reshape(-1, KV_HEADS, group_size, HEAD_DIM)
    key_rows = packed_s[..., :key_width].reshape(-1, KV_HEADS, HEAD_DIM)
    value_rows = packed_s[..., key_width:].reshape(-1, KV_HEADS, HEAD_DIM)
    raw_scores = jnp.einsum(
        "qcgd,kcd->cgqk", query_rows, key_rows, preferred_element_type=jnp.float32
    )
    query_place = query_pos.reshape(-1)
    key_place = key_pos.reshape(-1)
    allowed = (key_place[None, :] <= query_place[:, None]) & (key_place[None, :] < length_s)
    scores = jnp.where(allowed, raw_scores * HEAD_DIM ** (-0.5), masked_score)
    return (scores, query_rows, key_rows, value_rows)


def attend_one(inputs, local_pos, key_pos):
    query_s, packed_s, length_s = inputs
    scores, query_rows, key_rows, value_rows = scores_for(
        query_s, packed_s, length_s, local_pos, key_pos
    )
    row_top = jnp.max(scores, axis=-1, keepdims=True)
    shifted = jnp.exp(scores - row_top)
    row_total = jnp.sum(shifted, axis=-1, keepdims=True)
    soft_probs = (shifted / row_total).astype(jnp.bfloat16)
    result = jnp.einsum(
        "cgqk,kcd->qcgd", soft_probs, value_rows, preferred_element_type=jnp.float32
    )
    return (result.reshape(query_s.shape[:2] + (-1,)), row_top + jnp.log(row_total))


def attend_back(inputs, query_pos, key_pos):
    query_s, packed_s, length_s, log_total, grad_attn = inputs[:5]
    scores, query_rows, key_rows, value_rows = scores_for(
        query_s, packed_s, length_s, query_pos, key_pos
    )
    soft_probs = jnp.exp(scores - log_total)
    grad_rows = grad_attn.reshape(query_rows.shape)
    grad_probs = jnp.einsum(
        "qcgd,kcd->cgqk", grad_rows, value_rows, preferred_element_type=jnp.float32
    )
    inner = jnp.sum(soft_probs * grad_probs, axis=-1, keepdims=True)
    grad_raw = (soft_probs * (grad_probs - inner) * HEAD_DIM ** (-0.5)).astype(jnp.bfloat16)
    results = ()
    grad_query = jnp.einsum(
        "cgqk,kcd->qcgd", grad_raw, key_rows, preferred_element_type=jnp.float32
    )
    results = results + (grad_query.reshape(query_s.shape),)
    grad_keys = jnp.einsum(
        "cgqk,qcgd->kcd", grad_raw, query_rows, preferred_element_type=jnp.float32
    )
    grad_values = jnp.einsum(
        "cgqk,qcgd->kcd",
        soft_probs.astype(jnp.bfloat16),
        grad_rows,
        preferred_element_type=jnp.float32,
    )
    key_count = key_rows.shape[0]
    grad_packed = jnp.concatenate(
        [grad_keys.reshape(key_count, -1), grad_values.reshape(key_count, -1)], axis=-1
    )
    results = results + (grad_packed.reshape(packed_s.shape),)
    return results


def front_half(residual, attn_gain, query_weight, key_weight, value_weight, cosine, sine):
    inverse, normed = norm_forward(residual, attn_gain)
    lead_shape = residual.shape[:3]
    flat_rows = normed.reshape(-1, residual.shape[-1])
    query_heads = rotate(
        matmul(flat_rows, query_weight).reshape(lead_shape + (HEADS, HEAD_DIM)), cosine, sine
    ).astype(jnp.bfloat16)
    key_heads = rotate(
        matmul(flat_rows, key_weight).reshape(lead_shape + (KV_HEADS, HEAD_DIM)), cosine, sine
    ).astype(jnp.bfloat16)
    value_rows = matmul(flat_rows, value_weight).astype(jnp.bfloat16)
    packed = jnp.concatenate(
        [key_heads.reshape(lead_shape + (-1,)), value_rows.reshape(lead_shape + (-1,))], axis=-1
    )
    return (inverse, flat_rows, query_heads, packed)


def rear_half(
    residual,
    query_heads,
    gathered,
    seq_lens,
    local_pos,
    key_pos,
    mlp_gain,
    out_weight,
    gate_weight,
    up_weight,
    down_weight,
):
    features = residual.shape[-1]
    attended, log_total = lax.map(
        lambda inputs: attend_one(inputs, local_pos, key_pos), (query_heads, gathered, seq_lens)
    )
    attn_rows = attended.astype(jnp.bfloat16).reshape(-1, features)
    middle = residual + matmul(attn_rows, out_weight).reshape(residual.shape)
    mlp_inverse, mlp_normed = norm_forward(middle, mlp_gain)
    mlp_rows = mlp_normed.reshape(-1, features)
    gate_proj = matmul(mlp_rows, gate_weight)
    up_proj = matmul(mlp_rows, up_weight)
    activated = (jax.nn.silu(gate_proj) * up_proj).astype(jnp.bfloat16)
    mlp_out = matmul(activated, down_weight).reshape(residual.shape)
    return (
        log_total,
        attn_rows,
        middle,
        mlp_inverse,
        mlp_rows,
        gate_proj,
        up_proj,
        activated,
        mlp_out,
    )


def shards(
    tokens,
    assign,
    lengths,
    gain_attn,
    query_weight,
    key_weight,
    value_weight,
    out_weight,
    gain_mlp,
    gate_weight,
    up_weight,
    down_weight,
    cotangent,
):
    span_len = tokens.shape[2]
    features = tokens.shape[3]
    key_width = KV_HEADS * HEAD_DIM
    half_len = span_len * lax.axis_size("seq")
    full_len = 2 * half_len
    my_index = lax.axis_index("seq")
    row_index = my_index * span_len + jnp.arange(span_len, dtype=jnp.int32)
    local_pos = jnp.stack([row_index, full_len - 1 - row_index])
    all_index = jnp.arange(half_len, dtype=jnp.int32)
    key_pos = jnp.stack([all_index, full_len - 1 - all_index])
    matches = assign[:, None] == jnp.arange(lengths.shape[0], dtype=jnp.int32)[None, :]
    seq_lens = jnp.sum(jnp.where(matches, lengths[None, :], 0), axis=1)
    valid = (local_pos[None, :, :] < seq_lens[:, None, None])[..., None]
    cosine, sine = angles_of(local_pos)
    attn_gain = gain_attn.astype(jnp.float32)
    mlp_gain = gain_mlp.astype(jnp.float32)
    residual = tokens.astype(jnp.float32)
    inverse, flat_rows, query_heads, packed = front_half(
        residual, attn_gain, query_weight, key_weight, value_weight, cosine, sine
    )
    gathered = lax.all_gather(packed, "seq", axis=2, tiled=True)
    log_total, attn_rows, middle, mlp_inverse, mlp_rows, gate_proj, up_proj, activated, mlp_out = (
        rear_half(
            residual,
            query_heads,
            gathered,
            seq_lens,
            local_pos,
            key_pos,
            mlp_gain,
            out_weight,
            gate_weight,
            up_weight,
            down_weight,
        )
    )
    block_out = jnp.where(valid, middle + mlp_out, 0.0).astype(jnp.bfloat16)
    incoming = jnp.where(valid, cotangent, jnp.zeros_like(cotangent))
    incoming_rows = incoming.reshape(-1, features)
    grad_down = weight_grad(activated, incoming_rows)
    grad_act = through(incoming_rows, down_weight)
    sigmoid_gate = jax.nn.sigmoid(gate_proj)
    back_gate = (
        grad_act * up_proj * sigmoid_gate * (1.0 + gate_proj * (1.0 - sigmoid_gate))
    ).astype(jnp.bfloat16)
    back_up = (grad_act * gate_proj * sigmoid_gate).astype(jnp.bfloat16)
    grad_gate = weight_grad(mlp_rows, back_gate)
    grad_up = weight_grad(mlp_rows, back_up)
    back_normed_mlp = through(back_gate, gate_weight) + through(back_up, up_weight)
    back_middle, grad_gain_mlp = norm_backward(
        back_normed_mlp.reshape(middle.shape), middle, mlp_inverse, mlp_gain
    )
    back_middle = back_middle + incoming.astype(jnp.float32)
    back_attn = back_middle.astype(jnp.bfloat16).reshape(-1, features)
    grad_out = weight_grad(attn_rows, back_attn)
    back_attended = through(back_attn, out_weight).astype(jnp.bfloat16).reshape(tokens.shape)
    back_query, back_packed_all = lax.map(
        lambda inputs: attend_back(inputs, local_pos, key_pos),
        (query_heads, gathered, seq_lens, log_total, back_attended),
    )
    back_packed = lax.psum_scatter(
        back_packed_all.astype(jnp.bfloat16), "seq", scatter_dimension=2, tiled=True
    ).astype(jnp.float32)
    lead_shape = tokens.shape[:3]
    back_keys = rotate_back(
        back_packed[..., :key_width].reshape(lead_shape + (KV_HEADS, HEAD_DIM)), cosine, sine
    )
    back_keys = back_keys.astype(jnp.bfloat16).reshape(-1, key_width)
    back_values = back_packed[..., key_width:].astype(jnp.bfloat16).reshape(-1, key_width)
    back_queries = rotate_back(back_query, cosine, sine).astype(jnp.bfloat16).reshape(-1, features)
    grad_query = weight_grad(flat_rows, back_queries)
    grad_key = weight_grad(flat_rows, back_keys)
    grad_value = weight_grad(flat_rows, back_values)
    back_normed = (
        through(back_queries, query_weight)
        + through(back_keys, key_weight)
        + through(back_values, value_weight)
    )
    back_input, grad_gain_attn = norm_backward(
        back_normed.reshape(residual.shape), residual, inverse, attn_gain
    )
    input_grad = back_input + back_middle
    names = (grad_query, grad_key, grad_value, grad_out, grad_gate, grad_up, grad_down)
    sums = lax.psum(tuple(g.astype(jnp.bfloat16) for g in names), ("seq", "batch"))
    grad_query, grad_key, grad_value, grad_out, grad_gate, grad_up, grad_down = (
        g.astype(jnp.float32) for g in sums
    )
    grad_gain_attn, grad_gain_mlp = lax.psum((grad_gain_attn, grad_gain_mlp), ("seq", "batch"))
    return (
        block_out,
        input_grad,
        grad_gain_attn,
        grad_query,
        grad_key,
        grad_value,
        grad_out,
        grad_gain_mlp,
        grad_gate,
        grad_up,
        grad_down,
    )


def solution(mesh):
    return jax.shard_map(
        shards,
        mesh=mesh,
        in_specs=(
            P("batch", None, "seq", None),
            P("batch"),
            P(),
            P(),
            P(),
            P(),
            P(),
            P(),
            P(),
            P(),
            P(),
            P(),
            P("batch", None, "seq", None),
        ),
        out_specs=(
            P("batch", None, "seq", None),
            P("batch", None, "seq", None),
            P(),
            P(),
            P(),
            P(),
            P(),
            P(),
            P(),
            P(),
            P(),
        ),
        check_vma=False,
    )
```

```python
import functools

import jax
import jax.numpy as jnp
from jax import lax
from jax.experimental import pallas as pl
from jax.experimental.pallas import tpu as pltpu
from jax.sharding import PartitionSpec as P

HEADS = 9
KV_HEADS = 3
HEAD_DIM = 64
GROUP = HEADS // KV_HEADS
KEY_WIDTH = KV_HEADS * HEAD_DIM
PACKED = 2 * KEY_WIDTH
LANES = 640
TILE = 256

epsilon = 1e-06
rope_base = 10000.0
bf16 = jnp.bfloat16
f32 = jnp.float32
MiB = 1 << 20

NN = (((1,), (0,)), ((), ()))
NT = (((1,), (1,)), ((), ()))
TN = (((0,), (0,)), ((), ()))


def dot(left, right, dims=NN):
    return lax.dot_general(left, right, dims, preferred_element_type=f32)


ME, CORE, LOW, HIGH, CHIP, FULL, LENGTHS = range(7)


def run(kernel, meta, grid, inputs, outputs, scratch, vmem, cost, name, after=()):
    kept = [at for at, out in enumerate(outputs) if out[2] is not None]
    hidden = [outputs[at][2] for at in kept] + list(after)
    count = len(inputs)

    def body(meta_ref, *refs):
        kernel(meta_ref, *refs[:count], *refs[count + len(hidden) :])

    return pl.pallas_call(
        body,
        grid_spec=pltpu.PrefetchScalarGridSpec(
            num_scalar_prefetch=1,
            grid=grid,
            in_specs=[spec for _, spec in inputs] + [pl.BlockSpec(memory_space=pl.ANY)] * len(hidden),
            out_specs=[spec for _, spec, _ in outputs],
            scratch_shapes=scratch,
        ),
        out_shape=[shape for shape, _, _ in outputs],
        input_output_aliases={1 + count + i: at for i, at in enumerate(kept)},
        compiler_params=pltpu.CompilerParams(
            vmem_limit_bytes=vmem * MiB, dimension_semantics=("arbitrary",) * len(grid)
        ),
        cost_estimate=pl.CostEstimate(flops=8 * cost[0], bytes_accessed=cost[1], transcendentals=cost[2]),
        name=name,
    )(meta, *[array for array, _ in inputs], *hidden)


def hold(meta, arrays, after):
    anywhere = pl.BlockSpec(memory_space=pl.ANY)
    out = run(
        lambda *refs: None, meta, (1,), [], [(like(a.shape, a.dtype), anywhere, a) for a in arrays],
        [], 16, (0, 0, 0), "hold", after,
    )
    return list(out)


def whole():
    return pl.BlockSpec(memory_space=pltpu.VMEM)


def like(shape, dtype):
    return jax.ShapeDtypeStruct(shape, dtype)


def seq_block(step, span, width, base=0):
    return pl.BlockSpec((step, 2, span, width), lambda s, meta: (s + base // step, 0, 0, 0))


def flat_block(step, span, width, base=0):
    return pl.BlockSpec((step * 2 * span, width), lambda s, meta: (s + base // step, 0))


def lane_of(shape):
    return lax.broadcasted_iota(jnp.int32, shape, len(shape) - 1)


def swap_halves(chunk):
    first = lane_of(chunk.shape) % HEAD_DIM < HEAD_DIM // 2
    return jnp.where(first, pltpu.roll(chunk, 96, 1), pltpu.roll(chunk, 32, 1))


def unit_rows(rows):
    return lax.rsqrt(jnp.mean(rows * rows, axis=-1, keepdims=True) + epsilon)


def front_kernel(meta, tok_ref, gain_ref, wq_ref, wk_ref, wv_ref, cos_ref, sin_ref, q_ref, kv_ref, n_ref):
    seqs, _, span, features = tok_ref.shape
    rows = tok_ref[...].reshape(seqs * 2 * span, features).astype(f32)
    normed = (rows * unit_rows(rows) * gain_ref[...].astype(f32)).astype(bf16)
    n_ref[...] = normed.reshape(n_ref.shape)
    cos = jnp.concatenate([cos_ref[...]] * seqs, axis=0)
    sin = jnp.concatenate([sin_ref[...]] * seqs, axis=0)
    turn = lambda chunk: chunk * cos + swap_halves(chunk) * sin
    queries = [turn(chunk).astype(bf16) for chunk in chunks_of(dot(normed, wq_ref[...]))]
    q_ref[...] = jnp.concatenate(queries, axis=1)[:, :features].reshape(q_ref.shape)
    weights = jnp.concatenate([wk_ref[...], wv_ref[...]], axis=0)
    lin = dot(normed, weights, NT)
    chunks = [lin[:, 128 * c : 128 * c + 128] for c in range(3)]
    chunks[0] = turn(chunks[0])
    chunks[1] = jnp.where(lane_of(chunks[1].shape) < HEAD_DIM, turn(chunks[1]), chunks[1])
    kv_ref[...] = jnp.concatenate([c.astype(bf16) for c in chunks], axis=1).reshape(kv_ref.shape)


def front(meta, chunk, tokens, gain, wq, wk, wv, cos, sin, after):
    base, seqs = chunk
    _, _, span, features = tokens.shape
    step = 2
    rows = seqs * 2 * span
    out = lambda width: (like((seqs, 2, span, width), bf16), seq_block(step, span, width), None)
    return run(
        front_kernel, meta, (seqs // step,),
        [(tokens, seq_block(step, span, features, base))]
        + [(a, whole()) for a in (gain, wq, wk, wv, cos, sin)],
        [out(features), out(PACKED), out(features)],
        [], 60, (2 * rows * features * 1024, rows * 4500 + 1200000, rows), "front", after,
    )


def head_rows(chunks, offset, scale):
    span = chunks[0].shape[0]
    zero = jnp.zeros((span, 128), bf16)
    lower = lane_of((span, 128)) < HEAD_DIM
    out = []
    for h in range(HEADS):
        place = h // GROUP + offset
        chunk = chunks[h // 2]
        if h % 2 != place % 2:
            chunk = pltpu.roll(chunk, HEAD_DIM, 1)
        keep = lower if place % 2 == 0 else jnp.logical_not(lower)
        piece = jnp.where(keep, chunk * scale, 0.0).astype(bf16)
        out.append(jnp.concatenate([piece, zero] if place < 2 else [zero, piece], axis=1))
    out.append(jnp.zeros((LANES - HEADS * span, 256), bf16))
    return jnp.concatenate(out, axis=0)


def chunks_of(rows):
    full = [rows[:, 128 * c : 128 * c + 128].astype(f32) for c in range(4)]
    last = rows[:, 512:576].astype(f32)
    return full + [jnp.concatenate([last, jnp.zeros_like(last)], axis=1)]


def heads_apart(turned):
    lane = lane_of((HEAD_DIM, LANES))
    width = GROUP * HEAD_DIM
    picked = jnp.where(
        lane < width,
        turned[:HEAD_DIM],
        jnp.where(lane < 2 * width, turned[HEAD_DIM : 2 * HEAD_DIM], turned[2 * HEAD_DIM :]),
    )
    out = []
    for c in range(5):
        flipped = picked[:, 128 * c : 128 * c + 128].T
        out.append(jnp.concatenate([flipped[:HEAD_DIM], flipped[HEAD_DIM:]], axis=1))
    return out


def score_bias(tile, place, length, full, t, span):
    row = tile * TILE + lax.broadcasted_iota(jnp.int32, (TILE, 128), 0)
    inner = row % span
    pos = jnp.where(row < full // 2, row, row - inner + (span - 1) - inner)
    own = place * span + lane_of((TILE, 128)) % span
    own = own if t == 0 else full - 1 - own
    return jnp.where((pos <= own) & (pos < length), 0.0, -1e30)


def place_of(slot, me, chips):
    m, j = slot % chips, slot // chips
    return ((me // 2) ^ m) * 2 + ((me % 2) ^ j)


def tiles_for(t, me, length, full, span):
    last = (me + 1) * span if t == 0 else full - me * span
    return pl.cdiv(jnp.minimum(last, length), TILE)


def fill_keys(kv_refs, kv_scr, me, full, span):
    chips = len(kv_refs) // 2
    for slot, ref in enumerate(kv_refs):
        place = place_of(slot, me, chips)
        kv_scr[pl.ds(pl.multiple_of(place * span, span), span), :] = ref[0, 0]
        kv_scr[pl.ds(pl.multiple_of(full - span - place * span, span), span), :] = ref[0, 1]


def forward_kernel(count, base, meta, q_ref, *refs):
    kv_refs = refs[:count]
    out_ref, lse_ref, kv_scr, turned_scr, score_scr, sum_scr = refs[count:]
    span = q_ref.shape[2]
    full = 2 * span * count
    me = meta[ME]
    length = meta[LENGTHS + base + pl.program_id(0)]

    def block(t):
        queries = head_rows(chunks_of(q_ref[0, t]), 0, HEAD_DIM**-0.5)
        tiles = tiles_for(t, me, length, full, span)

        def scores(tile, top):
            rows = pl.ds(pl.multiple_of(tile * TILE, TILE), TILE)
            bias = score_bias(tile, me, length, full, t, span)
            raw = dot(kv_scr[rows, 0:256], queries, NT) + jnp.concatenate([bias] * 5, axis=1)
            score_scr[rows, :] = raw
            return jnp.maximum(top, jnp.max(raw, axis=0, keepdims=True))

        top = lax.fori_loop(0, tiles, scores, jnp.full((1, LANES), -1e30, f32))
        sum_scr[...] = jnp.zeros_like(sum_scr)

        def values(tile, total):
            rows = pl.ds(pl.multiple_of(tile * TILE, TILE), TILE)
            probs = jnp.exp(score_scr[rows, :] - top)
            sum_scr[...] += dot(turned_scr[tile], probs.astype(bf16))
            return total + jnp.sum(probs, axis=0, keepdims=True)

        total = lax.fori_loop(0, tiles, values, jnp.zeros((1, LANES), f32))
        out = jnp.concatenate(heads_apart(sum_scr[...] / total), axis=1)
        out_ref[0, t] = out[:, : out_ref.shape[3]].astype(bf16)
        lse_ref[0, t : t + 1, :] = top + jnp.log(total)

    def blank(t):
        out_ref[0, t] = jnp.zeros(out_ref.shape[2:], bf16)
        lse_ref[0, t : t + 1, :] = jnp.zeros((1, LANES), f32)

    first = length > me * span
    second = length > full - (me + 1) * span

    @pl.when(first)
    def _():
        fill_keys(kv_refs, kv_scr, me, full, span)

        def turn(tile, carry):
            rows = pl.ds(pl.multiple_of(tile * TILE, TILE), TILE)
            turned_scr[tile] = kv_scr[rows, 128:PACKED].T[HEAD_DIM:]
            return carry

        most = jnp.where(second, tiles_for(1, me, length, full, span), tiles_for(0, me, length, full, span))
        lax.fori_loop(0, most, turn, 0)
        block(0)

    @pl.when(jnp.logical_not(first))
    def _():
        blank(0)

    @pl.when(second)
    def _():
        block(1)

    @pl.when(jnp.logical_not(second))
    def _():
        blank(1)


def attend(meta, chunk, queries, slots, begun, after):
    base, seqs = chunk
    _, _, span, features = queries.shape
    full = 2 * span * len(slots)
    tiles = seqs * full * 5 // 4 // TILE
    return run(
        functools.partial(forward_kernel, len(slots), base), meta, (seqs,),
        [(queries, seq_block(1, span, features))] + [(a, seq_block(1, span, PACKED)) for a in slots],
        [
            (like(begun[0].shape, bf16), seq_block(1, span, features, base), None if begun[1] else begun[0]),
            (like((seqs, 2, LANES), f32), pl.BlockSpec((1, 2, LANES), lambda s, meta: (s, 0, 0)), None),
        ],
        [
            pltpu.VMEM((full, PACKED), bf16),
            pltpu.VMEM((full // TILE, KEY_WIDTH, TILE), bf16),
            pltpu.VMEM((full, LANES), f32),
            pltpu.VMEM((KEY_WIDTH, LANES), f32),
        ],
        60, (tiles * 2 * 2 * 256 * TILE * LANES, seqs * full * PACKED * 2, tiles * TILE * LANES), "attend", after,
    )


def backward_kernel(count, base, meta, q_ref, o_ref, g_ref, lse_ref, cos_ref, sin_ref, *refs):
    kv_refs = refs[:count]
    dq_ref, near_ref, far_ref, kv_scr, turned_scr, dkv_scr, sum_scr = refs[count:]
    span = q_ref.shape[2]
    full = 2 * span * count
    chips = count // 2
    me = meta[ME]
    length = meta[LENGTHS + base + pl.program_id(0)]

    def block(t):
        queries = head_rows(chunks_of(q_ref[0, t]), 0, HEAD_DIM**-0.5)
        grad_chunks = chunks_of(g_ref[0, t])
        grads = head_rows(grad_chunks, 1, 1.0)
        inner = []
        for g, o in zip(grad_chunks, chunks_of(o_ref[0, t])):
            product = (g * o).T
            inner.append(jnp.sum(product[:HEAD_DIM], axis=0, keepdims=True))
            inner.append(jnp.sum(product[HEAD_DIM:], axis=0, keepdims=True))
        inner = jnp.concatenate(inner, axis=1)
        log_total = lse_ref[0, t : t + 1, :]
        sum_scr[...] = jnp.zeros_like(sum_scr)

        def one(tile, carry):
            rows = pl.ds(pl.multiple_of(tile * TILE, TILE), TILE)
            bias = score_bias(tile, me, length, full, t, span)
            raw = dot(kv_scr[rows, 0:256], queries, NT) + jnp.concatenate([bias] * 5, axis=1)
            probs = jnp.exp(raw - log_total)
            grad_probs = dot(kv_scr[rows, 128:PACKED], grads, NT)
            grad_raw = (probs * (grad_probs - inner)).astype(bf16)
            grad_values = dot(probs.astype(bf16), grads)
            grad_keys = dot(grad_raw, queries)
            dkv_scr[rows, 0:128] += grad_keys[:, :128]
            dkv_scr[rows, 128:256] += grad_keys[:, 128:] + grad_values[:, :128]
            dkv_scr[rows, 256:384] += grad_values[:, 128:]
            sum_scr[...] += dot(turned_scr[tile], grad_raw)
            return carry

        lax.fori_loop(0, tiles_for(t, me, length, full, span), one, 0)
        cos = cos_ref[pl.ds(t * span, span), :]
        sin = sin_ref[pl.ds(t * span, span), :]
        out = [
            chunk * cos - swap_halves(chunk) * sin
            for chunk in heads_apart(sum_scr[...] * HEAD_DIM**-0.5)
        ]
        dq_ref[0, t] = jnp.concatenate(out, axis=1)[:, : dq_ref.shape[3]].astype(bf16)

    def blank(t):
        dq_ref[0, t] = jnp.zeros(dq_ref.shape[2:], bf16)

    first = length > me * span
    second = length > full - (me + 1) * span

    @pl.when(first)
    def _():
        fill_keys(kv_refs, kv_scr, me, full, span)
        dkv_scr[...] = jnp.zeros_like(dkv_scr)

        def turn(tile, carry):
            rows = pl.ds(pl.multiple_of(tile * TILE, TILE), TILE)
            turned_scr[tile] = kv_scr[rows, 0:256].T[:KEY_WIDTH]
            return carry

        most = jnp.where(second, tiles_for(1, me, length, full, span), tiles_for(0, me, length, full, span))
        lax.fori_loop(0, most, turn, 0)
        block(0)

    @pl.when(second)
    def _():
        block(1)

    @pl.when(jnp.logical_not(second))
    def _():
        blank(1)

    @pl.when(first)
    def _():
        for slot in range(count):
            place = place_of(slot, me, chips)
            ref = (near_ref, far_ref)[slot // chips]
            m = slot % chips
            ref[m, 0, 0] = dkv_scr[pl.ds(pl.multiple_of(place * span, span), span), :].astype(bf16)
            ref[m, 0, 1] = dkv_scr[
                pl.ds(pl.multiple_of(full - span - place * span, span), span), :
            ].astype(bf16)

    @pl.when(jnp.logical_not(first))
    def _():
        blank(0)
        near_ref[...] = jnp.zeros_like(near_ref)
        far_ref[...] = jnp.zeros_like(far_ref)


def attend_back(meta, chunk, queries, attended, grads, lse, cos, sin, slots, begun, after):
    base, seqs = chunk
    _, _, span, features = queries.shape
    full = 2 * span * len(slots)
    chips = len(slots) // 2
    tiles = seqs * full * 5 // 4 // TILE
    far = seq_block(1, span, features, base)
    slot_block = pl.BlockSpec((chips, 1, 2, span, PACKED), lambda s, meta: (0, s, 0, 0, 0))
    slot_shape = like((chips, seqs, 2, span, PACKED), bf16)
    return run(
        functools.partial(backward_kernel, len(slots), base), meta, (seqs,),
        [(queries, seq_block(1, span, features)), (attended, far), (grads, far)]
        + [(lse, pl.BlockSpec((1, 2, LANES), lambda s, meta: (s, 0, 0))), (cos, whole()), (sin, whole())]
        + [(a, seq_block(1, span, PACKED)) for a in slots],
        [(like(attended.shape, bf16), far, begun), (slot_shape, slot_block, None), (slot_shape, slot_block, None)],
        [
            pltpu.VMEM((full, PACKED), bf16),
            pltpu.VMEM((full // TILE, KEY_WIDTH, TILE), bf16),
            pltpu.VMEM((full, PACKED), f32),
            pltpu.VMEM((KEY_WIDTH, LANES), f32),
        ],
        60, (tiles * 2 * 5 * 256 * TILE * LANES, seqs * full * PACKED * 4, tiles * TILE * LANES), "attend_back", after,
    )


def middle_kernel(
    base, meta, tok_ref, att_ref, cot_ref, gain_ref, wo_ref, wg_ref, wu_ref, wd_ref,
    out_ref, act_ref, cut_ref, gate_ref, up_ref, n_ref, dmid_ref, datt_ref, dhead_ref, dgain_ref,
):
    seqs, _, span, features = tok_ref.shape
    rows = seqs * 2 * span
    step = pl.program_id(0)
    flat = lambda ref: ref[...].reshape(rows, features)
    inner = lax.broadcasted_iota(jnp.int32, (2, span, 1), 1) + meta[ME] * span
    second = lax.broadcasted_iota(jnp.int32, (2, span, 1), 0) == 1
    pos = jnp.where(second, meta[FULL] - 1 - inner, inner).reshape(2 * span, 1)
    valid = jnp.concatenate(
        [(pos < meta[LENGTHS + base + seqs * step + s]).astype(f32) for s in range(seqs)], axis=0
    )
    gain = gain_ref[...].astype(f32)
    middle = flat(tok_ref).astype(f32) + dot(flat(att_ref), wo_ref[...])
    unit = unit_rows(middle)
    scaled = middle * unit
    normed = (scaled * gain).astype(bf16)
    cut = flat(cot_ref).astype(f32) * valid
    cut_low = cut.astype(bf16)
    n_ref[...] = normed
    cut_ref[...] = cut_low
    hidden = wg_ref.shape[1]
    mlp, d_normed = 0.0, 0.0
    for at in range(2):
        part = slice(at * hidden // 2, (at + 1) * hidden // 2)
        gate = dot(normed, wg_ref[:, part])
        up = dot(normed, wu_ref[:, part])
        d_act = dot(cut_low, wd_ref[:, part])
        sig = 0.5 * jnp.tanh(0.5 * gate) + 0.5
        silu = gate * sig
        act = (silu * up).astype(bf16)
        d_gate = (d_act * up * (sig + silu * (1.0 - sig))).astype(bf16)
        d_up = (d_act * silu).astype(bf16)
        act_ref[:, part] = act
        gate_ref[:, part] = d_gate
        up_ref[:, part] = d_up
        mlp += dot(act, wd_ref[:, part], NT)
        d_normed += dot(d_gate, wg_ref[:, part], NT) + dot(d_up, wu_ref[:, part], NT)
    out_ref[...] = (valid * (middle + mlp)).astype(bf16).reshape(out_ref.shape)
    dgain_ref[0:1] = jnp.sum(d_normed * scaled, axis=0, keepdims=True)
    dg = d_normed * gain
    d_middle = cut + unit * (dg - scaled * jnp.mean(dg * scaled, axis=-1, keepdims=True))
    d_att = d_middle.astype(bf16)
    dhead_ref[...] = dot(d_att, wo_ref[...], NT).astype(bf16).reshape(dhead_ref.shape)
    dmid_ref[...] = d_middle.reshape(dmid_ref.shape)
    datt_ref[...] = d_att


def middle(meta, chunk, tokens, attended, cotangent, gain, wo, wg, wu, wd, begun, after):
    base, seqs = chunk
    total, _, span, features = tokens.shape
    hidden = wg.shape[1]
    step = 2
    block = seq_block(step, span, features, base)
    low = lambda width: (like((total * 2 * span, width), bf16), flat_block(step, span, width, base))
    outs = [
        (like(tokens.shape, bf16), block), low(hidden), low(features), low(hidden), low(hidden), low(features),
        (like(tokens.shape, f32), block), low(features), (like(tokens.shape, bf16), block),
        (like((total // step * 8, features), f32), pl.BlockSpec((8, features), lambda s, meta: (s + base // step, 0))),
    ]
    begun = begun or [None] * len(outs)
    work = seqs * 2 * span * features
    return run(
        functools.partial(middle_kernel, base), meta, (seqs // step,),
        [(a, block) for a in (tokens, attended, cotangent)] + [(a, whole()) for a in (gain, wo, wg, wu, wd)],
        [out + (start,) for out, start in zip(outs, begun)],
        [], 60, (4 * work * (2 * features + 6 * hidden), 32 * work, work * 3), "middle", after,
    )


def last_kernel(
    count, begun, parted, meta, tok_ref, n_ref, dmid_ref, dq_ref, gain_ref, wq_ref, wk_ref, wv_ref, cos_ref, sin_ref, *refs
):
    part_refs, refs = refs[:count], refs[count:]
    before, refs = (refs[:2], refs[2:]) if begun else ((), refs)
    in_ref, *out_refs, grad_scr, gain_scr = refs
    step, steps = pl.program_id(0), pl.num_programs(0)
    seqs, _, span, features = tok_ref.shape
    rows = seqs * 2 * span
    packed = sum(ref[...].reshape(rows, PACKED).astype(f32) for ref in part_refs)
    cos = jnp.concatenate([cos_ref[...]] * seqs, axis=0)
    sin = jnp.concatenate([sin_ref[...]] * seqs, axis=0)
    chunks = [packed[:, 128 * c : 128 * c + 128] for c in range(3)]
    turned = [c * cos - swap_halves(c) * sin for c in chunks[:2]]
    turned[1] = jnp.where(lane_of((rows, 128)) < HEAD_DIM, turned[1], chunks[1])
    dkv = jnp.concatenate(turned + [chunks[2]], axis=1).astype(bf16)
    dq = dq_ref[...].reshape(rows, features)
    weights = jnp.concatenate([wk_ref[...], wv_ref[...]], axis=0)
    d_normed = dot(dq, wq_ref[...], NT) + dot(dkv, weights)
    values = tok_ref[...].reshape(rows, features).astype(f32)
    unit = unit_rows(values)
    scaled = values * unit
    gain_part = jnp.sum(d_normed * scaled, axis=0, keepdims=True)
    fill = jnp.zeros((rows, grad_scr.shape[1] - features - PACKED), bf16)
    grad_part = dot(n_ref[...].reshape(rows, features), jnp.concatenate([dq, dkv, fill], axis=1), TN)

    @pl.when(step == 0)
    def _():
        if begun:
            grad_scr[...] = before[0][...] + grad_part
            gain_scr[...] = before[1][...]
            gain_scr[0:1, :] += gain_part
        else:
            grad_scr[...] = grad_part
            gain_scr[...] = jnp.zeros_like(gain_scr)
            gain_scr[0:1, :] = gain_part

    @pl.when(step > 0)
    def _():
        grad_scr[...] += grad_part
        gain_scr[0:1, :] += gain_part

    dg = d_normed * gain_ref[...].astype(f32)
    back = unit * (dg - scaled * jnp.mean(dg * scaled, axis=-1, keepdims=True))
    in_ref[...] = dmid_ref[...] + back.reshape(in_ref.shape)

    @pl.when(step == steps - 1)
    def _():
        if parted:
            used = features + PACKED
            both = jnp.concatenate(
                [grad_scr[:, :used], gain_scr[...].T[:, : grad_scr.shape[1] - used]], axis=1
            )
            width = both.shape[1] // 4
            for c in range(4):
                place = lambda ref, f, s: ref.at[f, s, c ^ meta[CHIP]]
                put_parts(meta, both[:, width * c : width * c + width], place, *out_refs)
        else:
            out_refs[0][...] = grad_scr[...]
            out_refs[1][...] = gain_scr[...]


def last(meta, chunk, parted, tokens, normed, d_middle, dq, gain, wq, wk, wv, cos, sin, parts, begun, after):
    base, seqs = chunk
    _, _, span, features = tokens.shape
    step = 2
    rows = seqs * 2 * span
    far = seq_block(step, span, features, base)
    if parted:
        shape = (2, 2, 4, features // 8, 256)
        more = [(like(shape, bf16), pl.BlockSpec(shape, lambda s, meta: (0,) * 5), None)] * 2
    else:
        more = [
            (like((height, width), f32), pl.BlockSpec((height, width), lambda s, meta: (0, 0)), None)
            for height, width in ((features, 1024), (128, features))
        ]
    return run(
        functools.partial(last_kernel, len(parts), begun is not None, parted), meta, (seqs // step,),
        [(tokens, far), (normed, seq_block(step, span, features)), (d_middle, far), (dq, far)]
        + [(a, whole()) for a in (gain, wq, wk, wv, cos, sin)]
        + [(a, seq_block(step, span, PACKED)) for a in parts]
        + ([(a, whole()) for a in begun[1:]] if begun else []),
        [(like(tokens.shape, f32), far, begun[0] if begun else None)] + more,
        [pltpu.VMEM((features, 1024), f32), pltpu.VMEM((128, features), f32)],
        60, (2 * rows * features * 2048, rows * 13000, rows), "last", after,
    )


def put_parts(meta, value, place, keep_ref, send_ref):
    core, low, high = meta[CORE], meta[LOW], meta[HIGH]
    rows = value.shape[0] // 8
    for owner in range(2):
        def write(ref):
            for at in range(4):
                x, y = (at % 2) ^ low, (at // 2) ^ high
                first, second = (x, y) if owner == 0 else (y, x)
                start = (owner * 4 + at) * rows
                place(ref, first, second)[...] = value[start : start + rows].astype(bf16)

        pl.when(core == owner)(lambda: write(keep_ref))
        pl.when(core != owner)(lambda: write(send_ref))


def down_gate_kernel(meta, cut_ref, act_ref, n_ref, gate_ref, keep_ref, send_ref, turned_scr):
    step = pl.program_id(0)
    place = lambda ref, f, s: ref.at[f, s, 0]

    @pl.when(step == 0)
    def _():
        turned_scr[...] = cut_ref[...].T

    @pl.when(step == 2)
    def _():
        turned_scr[...] = n_ref[...].T

    @pl.when(step < 2)
    def _():
        put_parts(meta, dot(turned_scr[...], act_ref[...]), place, keep_ref, send_ref)

    @pl.when(step >= 2)
    def _():
        put_parts(meta, dot(turned_scr[...], gate_ref[...]), place, keep_ref, send_ref)


def up_out_kernel(meta, n_ref, up_ref, att_ref, datt_ref, gain_ref, keep_ref, send_ref, turned_scr):
    step = pl.program_id(0)
    width = keep_ref.shape[-1]
    features = turned_scr.shape[0]
    place = lambda ref, f, s: ref.at[f, s, 0]

    @pl.when(step == 0)
    def _():
        turned_scr[...] = n_ref[...].T

    @pl.when(step < 3)
    def _():
        value = dot(turned_scr[...], up_ref[...])
        value = jnp.concatenate([value, jnp.zeros((features, width - value.shape[1]), f32)], axis=1)
        put_parts(meta, value, place, keep_ref, send_ref)

    @pl.when(step == 3)
    def _():
        value = dot(att_ref[...].T, datt_ref[...])
        gains = jnp.sum(gain_ref[...].reshape(-1, 8, features)[:, 0], axis=0, keepdims=True)
        gains = jnp.broadcast_to(gains, (128, features)).T
        value = jnp.concatenate([value, gains[:, : width - features]], axis=1)
        put_parts(meta, value, place, keep_ref, send_ref)


def grads_in_parts(kernel, meta, width, inputs, name, after):
    rows, features = inputs[0][0].shape
    shape = (2, 2, 4, features // 8, width)
    block = pl.BlockSpec((2, 2, 1) + shape[3:], lambda s, meta: (0, 0, s ^ meta[CHIP], 0, 0))
    return run(
        kernel, meta, (4,), inputs, [(like(shape, bf16), block, None)] * 2,
        [pltpu.VMEM((features, rows), bf16)], 60,
        (8 * rows * features * width, 8 * (rows + features) * width, 0), name, after,
    )


def columns(rows, width, index):
    return pl.BlockSpec((rows, width), lambda s, meta: (0, index(s)))


def across(value, kind):
    seq, batch = lax.axis_size("seq"), lax.axis_size("batch")
    pairs = []
    for s in range(seq):
        mask = 1 + (s % 2 ^ kind)
        pairs += [(s * batch + b, s * batch + (b ^ mask)) for b in range(batch)]
    return lax.ppermute(value, ("seq", "batch"), pairs)


def add_up(*values):
    return sum(v.astype(f32) for v in values).astype(bf16)


class Total:
    def __init__(self, meta, keep, send):
        self.meta, self.keep, self.send = meta, keep, send

    def held(self, arrays, after):
        return hold(self.meta, arrays, after) if after else arrays

    def core(self, after=()):
        (self.got,) = self.held([swap_with(self.send, "seq", 1)], after)
        self.now = add_up(self.keep[1], self.got[1])

    def first(self, after=()):
        (self.one,) = self.held([across(self.now, 0)], after)
        self.now = add_up(self.keep[0, 1], self.got[0, 1], self.one[1])

    def second(self, after=()):
        (two,) = self.held([across(self.now, 1)], after)
        self.mine = [(self.keep[0, 0, z], self.got[0, 0, z], self.one[0, z], two[z]) for z in range(4)]
        self.now = [add_up(*self.mine[z]) for z in range(1, 4)]

    def chips(self, after=()):
        there = self.held([swap_with(self.now[z - 1], "seq", 2 * z) for z in range(1, 4)], after)
        self.now = add_up(*self.mine[0], *there)

    def back_chips(self, after=()):
        done = [self.now] + self.held([swap_with(self.now, "seq", 2 * z) for z in range(1, 4)], after)
        self.now = jnp.stack(done)

    def rest(self):
        second = across(self.now, 1)
        ours = [self.now, second, across(self.now, 0), across(second, 0)]
        return ours + [swap_with(part, "seq", 1) for part in ours]


def row_block(meta, j):
    core = meta[CORE] if j < 4 else 1 - meta[CORE]
    first, second = (j % 4) // 2, j % 2
    x = jnp.where(core == 0, first, second) ^ meta[LOW]
    y = jnp.where(core == 0, second, first) ^ meta[HIGH]
    return core * 4 + y * 2 + x


def place_rows(meta, refs, out_ref, width):
    for j, ref in enumerate(refs):
        rows = ref.shape[-2]
        start = pl.multiple_of(row_block(meta, j) * rows, 8)
        out_ref[pl.ds(start, rows), :] = ref[0, :, :width].astype(f32)


def join_down_gate_kernel(meta, *refs):
    step = pl.program_id(0)
    pl.when(step < 2)(lambda: place_rows(meta, refs[:8], refs[8], refs[8].shape[1]))
    pl.when(step >= 2)(lambda: place_rows(meta, refs[:8], refs[9], refs[9].shape[1]))


def join_up_out_kernel(meta, *refs):
    step = pl.program_id(0)
    up_ref, out_ref, gain_ref, scr = refs[8:]
    features = out_ref.shape[1]
    pl.when(step < 3)(lambda: place_rows(meta, refs[:8], up_ref, up_ref.shape[1]))

    @pl.when(step == 3)
    def _():
        place_rows(meta, refs[:8], scr, scr.shape[1])
        out_ref[...] = scr[:, :features]
        gain_ref[...] = scr[:, features - 64 :].T[64:65]


def join_last_kernel(meta, *refs):
    query_ref, key_ref, value_ref, gain_ref, scr = refs[8:]
    features = query_ref.shape[1]
    width = scr.shape[1] // 4
    for z in range(4):
        for j, ref in enumerate(refs[:8]):
            rows = ref.shape[-2]
            start = pl.multiple_of(row_block(meta, j) * rows, 8)
            scr[pl.ds(start, rows), width * z : width * z + width] = ref[z ^ meta[CHIP]].astype(f32)
    query_ref[...] = scr[:, :features]
    turned = scr[:, 512:].T
    start = features - 512
    key_ref[...] = turned[start : start + KEY_WIDTH]
    value_ref[...] = turned[start + KEY_WIDTH : start + PACKED]
    gain_ref[...] = turned[start + PACKED : start + PACKED + 1]


def join(meta, kernel, parts, grid, outs, scratch, name):
    _, rows, width = parts[0].shape
    spec = pl.BlockSpec((1, rows, width), lambda s, meta: (s ^ meta[CHIP], 0, 0)) if grid else whole()
    return run(
        kernel, meta, grid, [(a, spec) for a in parts], [(like(shape, f32), spec, None) for shape, spec in outs],
        scratch, 32, (0, 8 * 4 * rows * width * 6, 0), name,
    )


def swap_with(value, axis, mask):
    size = lax.axis_size(axis)
    return lax.ppermute(value, axis, [(s, s ^ mask) for s in range(size)])


def gather_chips(packed):
    return [packed] + [swap_with(packed, "seq", 2 * m) for m in range(1, lax.axis_size("seq") // 2)]


def gather_cores(same):
    return same + [swap_with(part, "seq", 1) for part in same]


def scatter_cores(meta, near, far, after):
    (other,) = hold(meta, [swap_with(far, "seq", 1)], after)
    return [add_up(near[m], other[m]) for m in range(near.shape[0])]


def scatter_chips(parts):
    return [parts[0]] + [swap_with(part, "seq", 2 * m) for m, part in enumerate(parts) if m]


def shards(
    tokens, assign, lengths, gain_attn, query_weight, key_weight, value_weight, out_weight,
    gain_mlp, gate_weight, up_weight, down_weight, cotangent,
):
    seqs, _, span, features = tokens.shape
    half = span * lax.axis_size("seq")
    full = 2 * half
    me = lax.axis_index("seq")
    matches = assign[:, None] == jnp.arange(lengths.shape[0], dtype=jnp.int32)[None, :]
    seq_lens = jnp.sum(jnp.where(matches, lengths[None, :], 0), axis=1)
    column = lax.axis_index("batch")
    head = jnp.stack([me, me % 2, column % 2, column // 2, me // 2, jnp.full_like(me, full)])
    meta = jnp.concatenate([head.astype(jnp.int32), seq_lens])
    parted = lax.axis_size("batch") == 4 and lax.axis_size("seq") == 8
    key_weight, value_weight, down_weight = key_weight.T, value_weight.T, down_weight.T
    row = me * span + jnp.arange(span, dtype=jnp.int32)
    pos = jnp.concatenate([row, full - 1 - row]).astype(f32)
    frequency = jnp.power(rope_base, -2.0 * jnp.arange(HEAD_DIM // 2, dtype=f32) / HEAD_DIM)
    angles = pos[:, None] * frequency
    cos, sin = jnp.cos(angles), jnp.sin(angles)
    cos = jnp.concatenate([cos] * 4, axis=1)
    sin = jnp.concatenate([-sin, sin] * 2, axis=1)
    gain_attn = gain_attn.reshape(1, -1)
    gain_mlp = gain_mlp.reshape(1, -1)

    one, two = (0, seqs // 2), (seqs // 2, seqs - seqs // 2)
    first_weights = (gain_attn, query_weight, key_weight, value_weight, cos, sin)
    mlp_weights = (gain_mlp, out_weight, gate_weight, up_weight, down_weight)
    blank = like(tokens.shape, bf16)

    q_one, kv_one, n_one = front(meta, one, tokens, *first_weights, ())
    chips_one = gather_chips(kv_one)
    q_two, kv_two, n_two = front(meta, two, tokens, *first_weights, chips_one[1:])
    chips_two = gather_chips(kv_two)
    slots_one = gather_cores(chips_one)
    attended, lse_one = attend(meta, one, q_one, slots_one, (blank, True), (q_two,))
    mid = middle(meta, one, tokens, attended, cotangent, *mlp_weights, None, ())
    dq, near_one, far_one = attend_back(
        meta, one, q_one, attended, mid[8], lse_one, cos, sin, slots_one, None, ()
    )
    slots_two = gather_cores([kv_two] + hold(meta, chips_two[1:], (dq,)))
    attended, lse_two = attend(meta, two, q_two, slots_two, (attended, False), (dq,))
    parts_one = scatter_cores(meta, near_one, far_one, (lse_two,))
    block_out, act, cut, d_gate, d_up, n_mlp, d_middle, d_att, d_heads, gain_parts = middle(
        meta, two, tokens, attended, cotangent, *mlp_weights, mid, parts_one[1:]
    )
    parts_one = scatter_chips(parts_one)
    flat_attended = attended.reshape(-1, features)
    rows, hidden = act.shape
    pieces = []
    if parted:
        wide = hidden // 2
        keep, send = grads_in_parts(
            down_gate_kernel, meta, wide,
            [
                (cut, whole()), (act, columns(rows, wide, lambda s: jnp.minimum(s, 1))),
                (n_mlp, whole()), (d_gate, columns(rows, wide, lambda s: jnp.maximum(s - 2, 0))),
            ],
            "down_gate", (),
        )
        piece_one = Total(meta, keep, send)
        pieces = [keep]
    dq, near_two, far_two = attend_back(
        meta, two, q_two, attended, d_heads, lse_two, cos, sin, slots_two, dq, pieces
    )
    if parted:
        piece_one.core((dq,))
        third = hidden // 3
        keep, send = grads_in_parts(
            up_out_kernel, meta, features + 64,
            [
                (n_mlp, whole()), (d_up, columns(rows, third, lambda s: jnp.minimum(s, 2))),
                (flat_attended, whole()), (d_att, whole()), (gain_parts, whole()),
            ],
            "up_out", (piece_one.now,),
        )
        piece_two = Total(meta, keep, send)
        pieces = [keep]
        piece_one.first((keep,))
        parts_two = scatter_cores(meta, near_two, far_two, (keep,))
        pieces = [piece_one.now]
    else:
        parts_two = scatter_cores(meta, near_two, far_two, (d_heads,))
    parts_one = parts_one[:1] + hold(meta, parts_one[1:], pieces + [parts_two[1]])
    tail = last(meta, one, False, tokens, n_one, d_middle, dq, *first_weights, parts_one, None, parts_two[1:])
    parts_two = scatter_chips(parts_two)
    pieces = []
    if parted:
        piece_one.second(tail[:1])
        piece_two.core(tail[:1])
        piece_one.chips()
        piece_two.first()
        piece_one.back_chips()
        piece_two.second()
        piece_two.chips()
        piece_two.back_chips()
    input_grad, *tail = last(
        meta, two, parted, tokens, n_two, d_middle, dq, *first_weights, parts_two, tail, pieces
    )
    if parted:
        piece_three = Total(meta, *tail)
        for stage in ("core", "first", "second", "chips", "back_chips"):
            getattr(piece_three, stage)()
        square = (features, features)
        row = ((1, features), pl.BlockSpec((1, features), lambda s, meta: (0, 0)))
        grad_down, grad_gate = join(
            meta, join_down_gate_kernel, piece_one.rest(), (4,),
            [
                ((features, hidden), columns(features, wide, lambda s: jnp.minimum(s, 1))),
                ((features, hidden), columns(features, wide, lambda s: jnp.maximum(s - 2, 0))),
            ],
            [], "join_down_gate",
        )
        grad_up, grad_out, d_gain_mlp = join(
            meta, join_up_out_kernel, piece_two.rest(), (4,),
            [
                ((features, hidden), columns(features, third, lambda s: jnp.minimum(s, 2))),
                (square, columns(features, features, lambda s: 0)), row,
            ],
            [pltpu.VMEM((features, features + 64), f32)], "join_up_out",
        )
        grad_query, grad_key, grad_value, d_gain_attn = join(
            meta, join_last_kernel, piece_three.rest(), (),
            [(square, whole()), ((KEY_WIDTH, features), whole()), ((KEY_WIDTH, features), whole()), ((1, features), whole())],
            [pltpu.VMEM((features, 1024), f32)], "join_query_key_value",
        )
    else:
        gain_rows = gain_parts.reshape(-1, 8, features)[:, 0].sum(axis=0, keepdims=True)
        grad_down, grad_gate, grad_up, grad_out, grad_packed, d_gain_attn, d_gain_mlp = lax.psum(
            (
                dot(cut, act, TN), dot(n_mlp, d_gate, TN), dot(n_mlp, d_up, TN),
                dot(flat_attended, d_att, TN), tail[0], tail[1][0], gain_rows,
            ),
            ("seq", "batch"),
        )
        grad_query = grad_packed[:, :features]
        grad_key = grad_packed[:, features : features + KEY_WIDTH].T
        grad_value = grad_packed[:, features + KEY_WIDTH : features + PACKED].T
    return (
        block_out,
        input_grad,
        d_gain_attn.reshape(-1),
        grad_query,
        grad_key.T,
        grad_value.T,
        grad_out,
        d_gain_mlp.reshape(-1),
        grad_gate,
        grad_up,
        grad_down.T,
    )


def solution(mesh):
    rows = P("batch", None, "seq", None)
    return jax.shard_map(
        shards,
        mesh=mesh,
        in_specs=(rows, P("batch")) + (P(),) * 10 + (rows,),
        out_specs=(rows, rows) + (P(),) * 9,
        check_vma=False,
    )
```

```python
import functools

import jax
import jax.numpy as jnp
from jax import lax
from jax.experimental import pallas as pl
from jax.experimental.pallas import tpu as pltpu
from jax.sharding import PartitionSpec as P

HEADS = 9
KV_HEADS = 3
HEAD_DIM = 64
GROUP = HEADS // KV_HEADS
KEY_WIDTH = KV_HEADS * HEAD_DIM
PACKED = 2 * KEY_WIDTH
LANES = 640
TILE = 256

epsilon = 1e-06
rope_base = 10000.0
bf16 = jnp.bfloat16
f32 = jnp.float32
MiB = 1 << 20

NN = (((1,), (0,)), ((), ()))
NT = (((1,), (1,)), ((), ()))
TN = (((0,), (0,)), ((), ()))


def dot(left, right, dims=NN):
    return lax.dot_general(left, right, dims, preferred_element_type=f32)


ME, CORE, LOW, HIGH, CHIP, FULL, LENGTHS = range(7)


def run(kernel, meta, grid, inputs, outputs, scratch, vmem, cost, name, after=()):
    kept = [at for at, out in enumerate(outputs) if out[2] is not None]
    hidden = [outputs[at][2] for at in kept] + list(after)
    count = len(inputs)

    def body(meta_ref, *refs):
        kernel(meta_ref, *refs[:count], *refs[count + len(hidden) :])

    return pl.pallas_call(
        body,
        grid_spec=pltpu.PrefetchScalarGridSpec(
            num_scalar_prefetch=1,
            grid=grid,
            in_specs=[spec for _, spec in inputs] + [pl.BlockSpec(memory_space=pl.ANY)] * len(hidden),
            out_specs=[spec for _, spec, _ in outputs],
            scratch_shapes=scratch,
        ),
        out_shape=[shape for shape, _, _ in outputs],
        input_output_aliases={1 + count + i: at for i, at in enumerate(kept)},
        compiler_params=pltpu.CompilerParams(
            vmem_limit_bytes=vmem * MiB, dimension_semantics=("arbitrary",) * len(grid)
        ),
        cost_estimate=pl.CostEstimate(flops=8 * cost[0], bytes_accessed=cost[1], transcendentals=cost[2]),
        name=name,
    )(meta, *[array for array, _ in inputs], *hidden)


def hold(meta, arrays, after):
    anywhere = pl.BlockSpec(memory_space=pl.ANY)
    out = run(
        lambda *refs: None, meta, (1,), [], [(like(a.shape, a.dtype), anywhere, a) for a in arrays],
        [], 16, (0, 0, 0), "hold", after,
    )
    return list(out)


def whole():
    return pl.BlockSpec(memory_space=pltpu.VMEM)


def like(shape, dtype):
    return jax.ShapeDtypeStruct(shape, dtype)


def seq_block(step, span, width, base=0):
    return pl.BlockSpec((step, 2, span, width), lambda s, meta: (s + base // step, 0, 0, 0))


def flat_block(step, span, width, base=0):
    return pl.BlockSpec((step * 2 * span, width), lambda s, meta: (s + base // step, 0))


def lane_of(shape):
    return lax.broadcasted_iota(jnp.int32, shape, len(shape) - 1)


def swap_halves(chunk):
    first = lane_of(chunk.shape) % HEAD_DIM < HEAD_DIM // 2
    return jnp.where(first, pltpu.roll(chunk, 96, 1), pltpu.roll(chunk, 32, 1))


def unit_rows(rows):
    return lax.rsqrt(jnp.mean(rows * rows, axis=-1, keepdims=True) + epsilon)


def front_kernel(
    packing, meta, tok_ref, gain_ref, wq_ref, wk_ref, wv_ref, cos_ref, sin_ref, q_ref, kv_ref, n_ref, *message_refs
):
    seqs, _, span, features = tok_ref.shape
    rows = tok_ref[...].reshape(seqs * 2 * span, features).astype(f32)
    normed = (rows * unit_rows(rows) * gain_ref[...].astype(f32)).astype(bf16)
    n_ref[...] = normed.reshape(n_ref.shape)
    cos = jnp.concatenate([cos_ref[...]] * seqs, axis=0)
    sin = jnp.concatenate([sin_ref[...]] * seqs, axis=0)
    turn = lambda chunk: chunk * cos + swap_halves(chunk) * sin
    weights = jnp.concatenate([wk_ref[...], wv_ref[...]], axis=0)
    lin = dot(normed, weights, NT)
    chunks = [lin[:, 128 * c : 128 * c + 128] for c in range(3)]
    chunks[0] = turn(chunks[0])
    chunks[1] = jnp.where(lane_of(chunks[1].shape) < HEAD_DIM, turn(chunks[1]), chunks[1])
    packed = jnp.concatenate([c.astype(bf16) for c in chunks], axis=1)
    kv_ref[...] = packed.reshape(kv_ref.shape)
    if packing:
        for e in range(seqs):
            low = packed[2 * e * span : (2 * e + 1) * span]
            high = packed[(2 * e + 1) * span : (2 * e + 2) * span]
            rank = rank_of(meta, seqs * pl.program_id(0) + e)
            put_message(meta, rank, message_refs, low, high)
    queries = [turn(chunk).astype(bf16) for chunk in chunks_of(dot(normed, wq_ref[...]))]
    q_ref[...] = jnp.concatenate(queries, axis=1)[:, :features].reshape(q_ref.shape)


def front(meta, packing, tokens, gain, wq, wk, wv, cos, sin):
    seqs, _, span, features = tokens.shape
    step = 2
    rows = seqs * 2 * span
    out = lambda width: (like((seqs, 2, span, width), bf16), seq_block(step, span, width), None)
    message = lambda count: (
        like((count, span, PACKED), bf16), pl.BlockSpec((count, span, PACKED), lambda s, meta: (0, 0, 0)), None
    )
    return run(
        functools.partial(front_kernel, packing), meta, (seqs // step,),
        [(tokens, seq_block(step, span, features))] + [(a, whole()) for a in (gain, wq, wk, wv, cos, sin)],
        [out(features), out(PACKED), out(features)] + ([message(8)] * 3 + [message(4)] if packing else []),
        [], 60, (2 * rows * features * 1024, rows * 4500 + 1200000, rows), "front",
    )


LONG, LONGER = 4, 6


def rank_of(meta, s):
    return meta[LENGTHS + 8 + s]


def put_message(meta, rank, refs, low, high):
    chip = meta[CHIP]
    for m in range(1, 4):
        later = (chip ^ m) > chip

        @pl.when(later)
        def _():
            refs[m - 1][rank] = low

        @pl.when(jnp.logical_not(later) & (rank < LONG))
        def _():
            refs[m - 1][2 * rank] = low
            refs[m - 1][2 * rank + 1] = high

    @pl.when((rank >= LONG) & (rank < LONGER))
    def _():
        refs[3][2 * (rank - LONG)] = low
        refs[3][2 * (rank - LONG) + 1] = high


def message_specs(array, m, span, later, s_of):
    def index(add):
        def at(s, meta):
            rank = rank_of(meta, s_of(s))
            chip = meta[CHIP]
            pairs = ((chip ^ m) > chip) == later
            return (jnp.where(pairs, jnp.minimum(2 * rank + add, 6 + add), rank), 0, 0)

        return at

    return [(array, pl.BlockSpec((1, span, PACKED), index(add))) for add in (0, 1)]


def extra_spec(array, span, s_of):
    def at(s, meta):
        return (jnp.clip(rank_of(meta, s_of(s)) - LONG, 0, 1), 0, 0)

    return (array, pl.BlockSpec((2, span, PACKED), at))


class Dense:
    def __init__(self, packed):
        same = [packed] + [swap_with(packed, "seq", 2 * m) for m in range(1, lax.axis_size("seq") // 2)]
        self.slots = same + [swap_with(part, "seq", 1) for part in same]
        self.chips = len(same)
        self.seqs, _, self.span, _ = packed.shape
        self.full = 2 * self.span * len(self.slots)

    def inputs(self):
        return [(a, seq_block(1, self.span, PACKED)) for a in self.slots]

    def rows(self, place, t):
        span = self.span
        start = place * span if t == 0 else self.full - span - place * span
        return pl.ds(pl.multiple_of(start, span), span)

    def fill(self, meta, refs, kv_scr):
        for slot, ref in enumerate(refs):
            place = place_of(slot, meta[ME], self.chips)
            for t in range(2):
                kv_scr[self.rows(place, t), :] = ref[0, t]

    def outputs(self):
        shape = like((self.chips, self.seqs, 2, self.span, PACKED), bf16)
        spec = pl.BlockSpec((self.chips, 1, 2, self.span, PACKED), lambda s, meta: (0, s, 0, 0, 0))
        return [(shape, spec, None)] * 2

    def store(self, meta, refs, grads):
        for slot in range(2 * self.chips):
            place = place_of(slot, meta[ME], self.chips)
            for t in range(2):
                refs[slot // self.chips][slot % self.chips, 0, t] = grads(self.rows(place, t))

    def cores(self, outs):
        near, far = outs
        other = swap_with(far, "seq", 1)
        self.sums = [add_up(near[m], other[m]) for m in range(self.chips)]
        return self.sums

    def finish(self):
        self.parts = [self.sums[0]] + [swap_with(part, "seq", 2 * m) for m, part in enumerate(self.sums) if m]

    def last_inputs(self, step):
        return [(a, seq_block(step, self.span, PACKED)) for a in self.parts]

    def collect(self, meta, refs, step):
        return sum(ref[...].reshape(step * 2 * self.span, PACKED).astype(f32) for ref in refs)


class Ragged(Dense):
    def __init__(self, packed, messages):
        self.seqs, _, self.span, _ = packed.shape
        self.full = 2 * self.span * lax.axis_size("seq")
        chips = [swap_with(a, "seq", 2 * m + 2) for m, a in enumerate(messages[:3])]
        chips += [self.between(messages[3], 1, -1), self.between(messages[3], 2, -1)]
        near = [packed] + chips
        self.sets = [near, [swap_with(a, "seq", 1) for a in near]]

    def between(self, value, far, way):
        pairs = ((3, 2), (2, 1)) if far == 1 else ((3, 1),)
        pairs = [p if way < 0 else p[::-1] for p in pairs]
        return lax.ppermute(value, "seq", [(2 * p + c, 2 * q + c) for p, q in pairs for c in range(2)])

    def inputs(self):
        out = []
        for own, *rest in self.sets:
            out.append((own, seq_block(1, self.span, PACKED)))
            for m in range(1, 4):
                out += message_specs(rest[m - 1], m, self.span, True, lambda s: s)
            out += [extra_spec(a, self.span, lambda s: s) for a in rest[3:]]
        return out

    def fill(self, meta, refs, kv_scr):
        chip, rank = meta[CHIP], rank_of(meta, pl.program_id(0))
        for j in range(2):
            own, *rest = refs[9 * j : 9 * j + 9]
            core = meta[CORE] ^ j

            def put(y, t, value):
                kv_scr[self.rows(2 * y + core, t), :] = value

            for t in range(2):
                put(chip, t, own[0, t])
            for m in range(1, 4):
                y = chip ^ m
                one, two = rest[2 * m - 2], rest[2 * m - 1]

                @pl.when((y < chip) | (rank < LONG))
                def _():
                    put(y, 0, one[0])

                @pl.when((y > chip) & (rank < LONG))
                def _():
                    put(y, 1, two[0])

                for far in (1, 2):
                    @pl.when((y == chip + far) & (rank >= LONG) & (rank < LONGER))
                    def _():
                        for t in range(2):
                            put(y, t, rest[5 + far][t])

    def outputs(self):
        own = (like((self.seqs, 2, self.span, PACKED), bf16), seq_block(1, self.span, PACKED), None)
        shape = (32, self.span, PACKED)
        message = (like(shape, bf16), pl.BlockSpec(shape, lambda s, meta: (0, 0, 0)), None)
        return [own, own, message, message]

    def store(self, meta, refs, grads):
        chip, rank = meta[CHIP], rank_of(meta, pl.program_id(0))
        for j in range(2):
            own, out = refs[j], refs[2 + j]
            core = meta[CORE] ^ j
            value = lambda y, t: grads(self.rows(2 * y + core, t))
            for t in range(2):
                own[0, t] = value(chip, t)
            for m in range(1, 4):
                y = chip ^ m
                start = 8 * (m - 1)

                @pl.when(y < chip)
                def _():
                    out[start + rank] = value(y, 0)

                @pl.when((y > chip) & (rank < LONG))
                def _():
                    out[start + 2 * rank] = value(y, 0)
                    out[start + 2 * rank + 1] = value(y, 1)

                for far in (1, 2):
                    @pl.when((y == chip + far) & (rank >= LONG) & (rank < LONGER))
                    def _():
                        for t in range(2):
                            out[20 + 4 * far + 2 * (rank - LONG) + t] = value(y, t)

    def cores(self, outs):
        own, own_far, near, far = outs
        other_own, other = (swap_with(own_far, "seq", 1), swap_with(far, "seq", 1))
        cut = [(0, 8), (8, 16), (16, 24), (24, 28), (28, 32)]
        self.sums = [add_up(own, other_own)] + [add_up(near[a:b], other[a:b]) for a, b in cut]
        return self.sums

    def finish(self):
        own, *rest = self.sums
        self.parts = [own] + [swap_with(a, "seq", 2 * m + 2) for m, a in enumerate(rest[:3])]
        self.parts += [self.between(rest[3], 1, 1), self.between(rest[4], 2, 1)]

    def last_inputs(self, step):
        own, *rest = self.parts
        out = [(own, seq_block(step, self.span, PACKED))]
        for e in range(step):
            s_of = lambda s, e=e: step * s + e
            for m in range(1, 4):
                out += message_specs(rest[m - 1], m, self.span, False, s_of)
            out += [extra_spec(a, self.span, s_of) for a in rest[3:]]
        return out

    def collect(self, meta, refs, step):
        own, *rest = refs
        chip = meta[CHIP]
        out = []
        for e in range(step):
            rank = rank_of(meta, step * pl.program_id(0) + e)
            mine = rest[8 * e : 8 * e + 8]
            both = [own[e, t].astype(f32) for t in range(2)]
            for m in range(1, 4):
                y = chip ^ m
                both[0] += jnp.where((y > chip) | (rank < LONG), mine[2 * m - 2][0].astype(f32), 0.0)
                both[1] += jnp.where((y < chip) & (rank < LONG), mine[2 * m - 1][0].astype(f32), 0.0)
            extra = (rank >= LONG) & (rank < LONGER)
            for t in range(2):
                both[t] += jnp.where(extra, mine[6][t].astype(f32) + mine[7][t].astype(f32), 0.0)
            out += both
        return jnp.concatenate(out, axis=0)


def head_rows(chunks, offset, scale):
    span = chunks[0].shape[0]
    zero = jnp.zeros((span, 128), bf16)
    lower = lane_of((span, 128)) < HEAD_DIM
    out = []
    for h in range(HEADS):
        place = h // GROUP + offset
        chunk = chunks[h // 2]
        if h % 2 != place % 2:
            chunk = pltpu.roll(chunk, HEAD_DIM, 1)
        keep = lower if place % 2 == 0 else jnp.logical_not(lower)
        piece = jnp.where(keep, chunk * scale, 0.0).astype(bf16)
        out.append(jnp.concatenate([piece, zero] if place < 2 else [zero, piece], axis=1))
    out.append(jnp.zeros((LANES - HEADS * span, 256), bf16))
    return jnp.concatenate(out, axis=0)


def chunks_of(rows):
    full = [rows[:, 128 * c : 128 * c + 128].astype(f32) for c in range(4)]
    last = rows[:, 512:576].astype(f32)
    return full + [jnp.concatenate([last, jnp.zeros_like(last)], axis=1)]


def heads_apart(turned):
    lane = lane_of((HEAD_DIM, LANES))
    width = GROUP * HEAD_DIM
    picked = jnp.where(
        lane < width,
        turned[:HEAD_DIM],
        jnp.where(lane < 2 * width, turned[HEAD_DIM : 2 * HEAD_DIM], turned[2 * HEAD_DIM :]),
    )
    out = []
    for c in range(5):
        flipped = picked[:, 128 * c : 128 * c + 128].T
        out.append(jnp.concatenate([flipped[:HEAD_DIM], flipped[HEAD_DIM:]], axis=1))
    return out


def score_bias(tile, place, length, full, t, span):
    row = tile * TILE + lax.broadcasted_iota(jnp.int32, (TILE, 128), 0)
    inner = row % span
    pos = jnp.where(row < full // 2, row, row - inner + (span - 1) - inner)
    own = place * span + lane_of((TILE, 128)) % span
    own = own if t == 0 else full - 1 - own
    return jnp.where((pos <= own) & (pos < length), 0.0, -1e30)


def place_of(slot, me, chips):
    m, j = slot % chips, slot // chips
    return ((me // 2) ^ m) * 2 + ((me % 2) ^ j)


def tiles_for(t, me, length, full, span):
    last = (me + 1) * span if t == 0 else full - me * span
    return pl.cdiv(jnp.minimum(last, length), TILE)


def row_bias(tile, place, length, full, t, span):
    column = tile * TILE + lane_of((span, TILE))
    inner = column % span
    pos = jnp.where(column < full // 2, column, column - inner + (span - 1) - inner)
    own = place * span + lax.broadcasted_iota(jnp.int32, (span, TILE), 0)
    own = own if t == 0 else full - 1 - own
    return jnp.where((pos <= own) & (pos < length), 0.0, -1e30)


def heads_together(rows):
    span = rows.shape[0] // HEADS
    lower = lane_of((span, 128)) < HEAD_DIM
    out = []
    for pair in range(5):
        halves = []
        for h in (2 * pair, 2 * pair + 1):
            if h < HEADS:
                place = h // GROUP + 1
                piece = rows[h * span : (h + 1) * span, 128 * (place // 2) : 128 * (place // 2) + 128]
                halves.append(pltpu.roll(piece, HEAD_DIM, 1) if place % 2 != h % 2 else piece)
        out.append(jnp.where(lower, *halves) if len(halves) == 2 else halves[0])
    return jnp.concatenate(out, axis=1)[:, : HEADS * HEAD_DIM]


def each_count(t, tiles, full, work):
    half = full // 2 // TILE
    for n in range(1 + t * half, half + 1 + t * half):
        pl.when(tiles == n)(functools.partial(work, n))


def forward_kernel(keys, count, meta, q_ref, *refs):
    kv_refs = refs[:count]
    out_ref, lse_ref, kv_scr = refs[count:]
    span, full = keys.span, keys.full
    me = meta[ME]
    length = meta[LENGTHS + pl.program_id(0)]

    def block(t):
        def work(n):
            queries = head_rows(chunks_of(q_ref[0, t]), 0, HEAD_DIM**-0.5)[: HEADS * span]
            scores = []
            for tile in range(n):
                bias = row_bias(tile, me, length, full, t, span)
                raw = dot(queries, kv_scr[tile * TILE : (tile + 1) * TILE, 0:256], NT)
                scores.append(raw + jnp.concatenate([bias] * HEADS, axis=0))
            top = scores[0]
            for score in scores[1:]:
                top = jnp.maximum(top, score)
            top = jnp.max(top, axis=1, keepdims=True)
            total, out = 0.0, 0.0
            for tile, score in enumerate(scores):
                probs = jnp.exp(score - top)
                total += jnp.sum(probs, axis=1, keepdims=True)
                out += dot(probs.astype(bf16), kv_scr[tile * TILE : (tile + 1) * TILE, 128:PACKED])
            out_ref[0, t] = heads_together(out / total).astype(bf16)
            column = jnp.broadcast_to(top + jnp.log(total), (HEADS * span, 128))
            row = jnp.concatenate([column, jnp.zeros((LANES - HEADS * span, 128), f32)], axis=0).T
            lse_ref[0, t : t + 1, :] = row[0:1]

        each_count(t, tiles_for(t, me, length, full, span), full, work)

    def blank(t):
        out_ref[0, t] = jnp.zeros(out_ref.shape[2:], bf16)
        lse_ref[0, t : t + 1, :] = jnp.zeros((1, LANES), f32)

    first = length > me * span
    second = length > full - (me + 1) * span

    @pl.when(pl.program_id(0) == 0)
    def _():
        kv_scr[...] = jnp.zeros_like(kv_scr)

    @pl.when(first)
    def _():
        keys.fill(meta, kv_refs, kv_scr)
        block(0)

    @pl.when(jnp.logical_not(first))
    def _():
        blank(0)

    @pl.when(second)
    def _():
        block(1)

    @pl.when(jnp.logical_not(second))
    def _():
        blank(1)


def attend(meta, queries, keys):
    seqs, _, span, features = queries.shape
    full = keys.full
    tiles = seqs * full * 5 // 4 // TILE
    inputs = keys.inputs()
    return run(
        functools.partial(forward_kernel, keys, len(inputs)), meta, (seqs,),
        [(queries, seq_block(1, span, features))] + inputs,
        [
            (like(queries.shape, bf16), seq_block(1, span, features), None),
            (like((seqs, 2, LANES), f32), pl.BlockSpec((1, 2, LANES), lambda s, meta: (s, 0, 0)), None),
        ],
        [pltpu.VMEM((full, PACKED), bf16)],
        60, (tiles * 2 * 2 * 256 * TILE * LANES, seqs * full * PACKED * 2, tiles * TILE * LANES), "attend",
    )


def backward_kernel(keys, count, meta, q_ref, o_ref, g_ref, lse_ref, cos_ref, sin_ref, *refs):
    kv_refs = refs[:count]
    dq_ref, *store_refs, kv_scr, turned_scr, dkv_scr, sum_scr = refs[count:]
    span, full = keys.span, keys.full
    me = meta[ME]
    length = meta[LENGTHS + pl.program_id(0)]

    def block(t):
        queries = head_rows(chunks_of(q_ref[0, t]), 0, HEAD_DIM**-0.5)
        grad_chunks = chunks_of(g_ref[0, t])
        grads = head_rows(grad_chunks, 1, 1.0)
        inner = []
        for g, o in zip(grad_chunks, chunks_of(o_ref[0, t])):
            product = (g * o).T
            inner.append(jnp.sum(product[:HEAD_DIM], axis=0, keepdims=True))
            inner.append(jnp.sum(product[HEAD_DIM:], axis=0, keepdims=True))
        inner = jnp.concatenate(inner, axis=1)
        log_total = lse_ref[0, t : t + 1, :]

        def one(tile):
            rows = slice(tile * TILE, (tile + 1) * TILE)
            bias = score_bias(tile, me, length, full, t, span)
            raw = dot(kv_scr[rows, 0:256], queries, NT) + jnp.concatenate([bias] * 5, axis=1)
            probs = jnp.exp(raw - log_total)
            grad_probs = dot(kv_scr[rows, 128:PACKED], grads, NT)
            grad_raw = (probs * (grad_probs - inner)).astype(bf16)
            grad_values = dot(probs.astype(bf16), grads)
            grad_keys = dot(grad_raw, queries)
            dkv_scr[rows, 0:128] += grad_keys[:, :128]
            dkv_scr[rows, 128:256] += grad_keys[:, 128:] + grad_values[:, :128]
            dkv_scr[rows, 256:384] += grad_values[:, 128:]
            return dot(turned_scr[tile], grad_raw)

        def work(n):
            sum_scr[...] = sum(one(tile) for tile in range(n))

        each_count(t, tiles_for(t, me, length, full, span), full, work)
        cos = cos_ref[pl.ds(t * span, span), :]
        sin = sin_ref[pl.ds(t * span, span), :]
        out = [
            chunk * cos - swap_halves(chunk) * sin
            for chunk in heads_apart(sum_scr[...] * HEAD_DIM**-0.5)
        ]
        dq_ref[0, t] = jnp.concatenate(out, axis=1)[:, : dq_ref.shape[3]].astype(bf16)

    def blank(t):
        dq_ref[0, t] = jnp.zeros(dq_ref.shape[2:], bf16)

    first = length > me * span
    second = length > full - (me + 1) * span

    @pl.when(pl.program_id(0) == 0)
    def _():
        kv_scr[...] = jnp.zeros_like(kv_scr)

    @pl.when(first)
    def _():
        keys.fill(meta, kv_refs, kv_scr)
        dkv_scr[...] = jnp.zeros_like(dkv_scr)

        def turn(tile, carry):
            rows = pl.ds(pl.multiple_of(tile * TILE, TILE), TILE)
            turned_scr[tile] = kv_scr[rows, 0:256].T[:KEY_WIDTH]
            return carry

        most = jnp.where(second, tiles_for(1, me, length, full, span), tiles_for(0, me, length, full, span))
        lax.fori_loop(0, most, turn, 0)
        block(0)

    @pl.when(second)
    def _():
        block(1)

    @pl.when(jnp.logical_not(second))
    def _():
        blank(1)

    @pl.when(first)
    def _():
        keys.store(meta, store_refs, lambda rows: dkv_scr[rows, :].astype(bf16))

    @pl.when(jnp.logical_not(first))
    def _():
        blank(0)
        keys.store(meta, store_refs, lambda rows: jnp.zeros((span, PACKED), bf16))


def attend_back(meta, queries, attended, grads, lse, cos, sin, keys, after):
    seqs, _, span, features = queries.shape
    full = keys.full
    tiles = seqs * full * 5 // 4 // TILE
    block = seq_block(1, span, features)
    inputs = keys.inputs()
    return run(
        functools.partial(backward_kernel, keys, len(inputs)), meta, (seqs,),
        [(queries, block), (attended, block), (grads, block)]
        + [(lse, pl.BlockSpec((1, 2, LANES), lambda s, meta: (s, 0, 0))), (cos, whole()), (sin, whole())]
        + inputs,
        [(like(attended.shape, bf16), block, None)] + keys.outputs(),
        [
            pltpu.VMEM((full, PACKED), bf16),
            pltpu.VMEM((full // TILE, KEY_WIDTH, TILE), bf16),
            pltpu.VMEM((full, PACKED), f32),
            pltpu.VMEM((KEY_WIDTH, LANES), f32),
        ],
        60, (tiles * 2 * 5 * 256 * TILE * LANES, seqs * full * PACKED * 4, tiles * TILE * LANES), "attend_back", after,
    )


def middle_kernel(
    meta, tok_ref, att_ref, cot_ref, gain_ref, wo_ref, wg_ref, wu_ref, wd_ref,
    out_ref, act_ref, cut_ref, gate_ref, up_ref, n_ref, dmid_ref, datt_ref, dhead_ref, dgain_ref,
):
    seqs, _, span, features = tok_ref.shape
    rows = seqs * 2 * span
    step = pl.program_id(0)
    flat = lambda ref: ref[...].reshape(rows, features)
    inner = lax.broadcasted_iota(jnp.int32, (2, span, 1), 1) + meta[ME] * span
    second = lax.broadcasted_iota(jnp.int32, (2, span, 1), 0) == 1
    pos = jnp.where(second, meta[FULL] - 1 - inner, inner).reshape(2 * span, 1)
    valid = jnp.concatenate(
        [(pos < meta[LENGTHS + seqs * step + s]).astype(f32) for s in range(seqs)], axis=0
    )
    gain = gain_ref[...].astype(f32)
    middle = flat(tok_ref).astype(f32) + dot(flat(att_ref), wo_ref[...])
    unit = unit_rows(middle)
    scaled = middle * unit
    normed = (scaled * gain).astype(bf16)
    cut = flat(cot_ref).astype(f32) * valid
    cut_low = cut.astype(bf16)
    n_ref[...] = normed
    cut_ref[...] = cut_low
    hidden = wg_ref.shape[1]
    mlp, d_normed = 0.0, 0.0
    for at in range(2):
        part = slice(at * hidden // 2, (at + 1) * hidden // 2)
        gate = dot(normed, wg_ref[:, part])
        up = dot(normed, wu_ref[:, part])
        d_act = dot(cut_low, wd_ref[:, part])
        sig = 0.5 * jnp.tanh(0.5 * gate) + 0.5
        silu = gate * sig
        act = (silu * up).astype(bf16)
        d_gate = (d_act * up * (sig + silu * (1.0 - sig))).astype(bf16)
        d_up = (d_act * silu).astype(bf16)
        act_ref[:, part] = act
        gate_ref[:, part] = d_gate
        up_ref[:, part] = d_up
        mlp += dot(act, wd_ref[:, part], NT)
        d_normed += dot(d_gate, wg_ref[:, part], NT) + dot(d_up, wu_ref[:, part], NT)
    out_ref[...] = (valid * (middle + mlp)).astype(bf16).reshape(out_ref.shape)
    dgain_ref[0:1] = jnp.sum(d_normed * scaled, axis=0, keepdims=True)
    dg = d_normed * gain
    d_middle = cut + unit * (dg - scaled * jnp.mean(dg * scaled, axis=-1, keepdims=True))
    d_att = d_middle.astype(bf16)
    dhead_ref[...] = dot(d_att, wo_ref[...], NT).astype(bf16).reshape(dhead_ref.shape)
    dmid_ref[...] = d_middle.reshape(dmid_ref.shape)
    datt_ref[...] = d_att


def middle(meta, tokens, attended, cotangent, gain, wo, wg, wu, wd):
    seqs, _, span, features = tokens.shape
    hidden = wg.shape[1]
    step = 2
    block = seq_block(step, span, features)
    low = lambda width: (like((seqs * 2 * span, width), bf16), flat_block(step, span, width), None)
    work = seqs * 2 * span * features
    return run(
        middle_kernel, meta, (seqs // step,),
        [(a, block) for a in (tokens, attended, cotangent)] + [(a, whole()) for a in (gain, wo, wg, wu, wd)],
        [
            (like(tokens.shape, bf16), block, None), low(hidden), low(features), low(hidden), low(hidden), low(features),
            (like(tokens.shape, f32), block, None), low(features), (like(tokens.shape, bf16), block, None),
            (like((seqs // step * 8, features), f32), pl.BlockSpec((8, features), lambda s, meta: (s, 0)), None),
        ],
        [], 60, (4 * work * (2 * features + 6 * hidden), 32 * work, work * 3), "middle",
    )


def last_kernel(
    keys, count, parted, meta, tok_ref, n_ref, dmid_ref, dq_ref, gain_ref, wq_ref, wk_ref, wv_ref, cos_ref, sin_ref, *refs
):
    part_refs, refs = refs[:count], refs[count:]
    in_ref, *out_refs, grad_scr, gain_scr = refs
    step, steps = pl.program_id(0), pl.num_programs(0)
    seqs, _, span, features = tok_ref.shape
    rows = seqs * 2 * span
    packed = keys.collect(meta, part_refs, seqs)
    cos = jnp.concatenate([cos_ref[...]] * seqs, axis=0)
    sin = jnp.concatenate([sin_ref[...]] * seqs, axis=0)
    chunks = [packed[:, 128 * c : 128 * c + 128] for c in range(3)]
    turned = [c * cos - swap_halves(c) * sin for c in chunks[:2]]
    turned[1] = jnp.where(lane_of((rows, 128)) < HEAD_DIM, turned[1], chunks[1])
    dkv = jnp.concatenate(turned + [chunks[2]], axis=1).astype(bf16)
    dq = dq_ref[...].reshape(rows, features)
    weights = jnp.concatenate([wk_ref[...], wv_ref[...]], axis=0)
    d_normed = dot(dq, wq_ref[...], NT) + dot(dkv, weights)
    values = tok_ref[...].reshape(rows, features).astype(f32)
    unit = unit_rows(values)
    scaled = values * unit
    gain_part = jnp.sum(d_normed * scaled, axis=0, keepdims=True)
    fill = jnp.zeros((rows, grad_scr.shape[1] - features - PACKED), bf16)
    grad_part = dot(n_ref[...].reshape(rows, features), jnp.concatenate([dq, dkv, fill], axis=1), TN)

    @pl.when(step == 0)
    def _():
        grad_scr[...] = grad_part
        gain_scr[...] = jnp.zeros_like(gain_scr)
        gain_scr[0:1, :] = gain_part

    @pl.when(step > 0)
    def _():
        grad_scr[...] += grad_part
        gain_scr[0:1, :] += gain_part

    dg = d_normed * gain_ref[...].astype(f32)
    back = unit * (dg - scaled * jnp.mean(dg * scaled, axis=-1, keepdims=True))
    in_ref[...] = dmid_ref[...] + back.reshape(in_ref.shape)

    @pl.when(step == steps - 1)
    def _():
        if parted:
            used = features + PACKED
            both = jnp.concatenate(
                [grad_scr[:, :used], gain_scr[...].T[:, : grad_scr.shape[1] - used]], axis=1
            )
            width = both.shape[1] // 4
            for c in range(4):
                place = lambda ref, f, s: ref.at[f, s, c]
                put_parts(meta, both[:, width * c : width * c + width], place, *out_refs)
        else:
            out_refs[0][...] = grad_scr[...]
            out_refs[1][...] = gain_scr[...]


def last(meta, parted, tokens, normed, d_middle, dq, gain, wq, wk, wv, cos, sin, keys, after):
    seqs, _, span, features = tokens.shape
    step = 2
    rows = seqs * 2 * span
    block = seq_block(step, span, features)
    if parted:
        shape = (2, 2, 4, features // 8, 256)
        more = [(like(shape, bf16), pl.BlockSpec(shape, lambda s, meta: (0,) * 5), None)] * 2
    else:
        more = [
            (like((height, width), f32), pl.BlockSpec((height, width), lambda s, meta: (0, 0)), None)
            for height, width in ((features, 1024), (128, features))
        ]
    inputs = keys.last_inputs(step)
    return run(
        functools.partial(last_kernel, keys, len(inputs), parted), meta, (seqs // step,),
        [(a, block) for a in (tokens, normed, d_middle, dq)]
        + [(a, whole()) for a in (gain, wq, wk, wv, cos, sin)] + inputs,
        [(like(tokens.shape, f32), block, None)] + more,
        [pltpu.VMEM((features, 1024), f32), pltpu.VMEM((128, features), f32)],
        60, (2 * rows * features * 2048, rows * 13000, rows), "last", after,
    )


def put_parts(meta, value, place, keep_ref, send_ref):
    core, low, high = meta[CORE], meta[LOW], meta[HIGH]
    rows = value.shape[0] // 8
    for owner in range(2):
        def write(ref):
            for at in range(4):
                x, y = (at % 2) ^ low, (at // 2) ^ high
                first, second = (x, y) if owner == 0 else (y, x)
                start = (owner * 4 + at) * rows
                place(ref, first, second)[...] = value[start : start + rows].astype(bf16)

        pl.when(core == owner)(lambda: write(keep_ref))
        pl.when(core != owner)(lambda: write(send_ref))


def down_gate_kernel(meta, cut_ref, act_ref, n_ref, gate_ref, keep_ref, send_ref, turned_scr):
    step = pl.program_id(0)
    place = lambda ref, f, s: ref.at[f, s, 0]

    @pl.when(step == 0)
    def _():
        turned_scr[...] = cut_ref[...].T

    @pl.when(step == 2)
    def _():
        turned_scr[...] = n_ref[...].T

    @pl.when(step < 2)
    def _():
        put_parts(meta, dot(turned_scr[...], act_ref[...]), place, keep_ref, send_ref)

    @pl.when(step >= 2)
    def _():
        put_parts(meta, dot(turned_scr[...], gate_ref[...]), place, keep_ref, send_ref)


def up_out_kernel(meta, n_ref, up_ref, att_ref, datt_ref, gain_ref, keep_ref, send_ref, turned_scr):
    step = pl.program_id(0)
    width = keep_ref.shape[-1]
    features = turned_scr.shape[0]
    place = lambda ref, f, s: ref.at[f, s, 0]

    @pl.when(step == 0)
    def _():
        turned_scr[...] = n_ref[...].T

    @pl.when(step < 3)
    def _():
        value = dot(turned_scr[...], up_ref[...])
        value = jnp.concatenate([value, jnp.zeros((features, width - value.shape[1]), f32)], axis=1)
        put_parts(meta, value, place, keep_ref, send_ref)

    @pl.when(step == 3)
    def _():
        value = dot(att_ref[...].T, datt_ref[...])
        gains = jnp.sum(gain_ref[...].reshape(-1, 8, features)[:, 0], axis=0, keepdims=True)
        gains = jnp.broadcast_to(gains, (128, features)).T
        value = jnp.concatenate([value, gains[:, : width - features]], axis=1)
        put_parts(meta, value, place, keep_ref, send_ref)


def grads_in_parts(kernel, meta, width, inputs, name, after):
    rows, features = inputs[0][0].shape
    shape = (2, 2, 4, features // 8, width)
    block = pl.BlockSpec((2, 2, 1) + shape[3:], lambda s, meta: (0, 0, s ^ meta[CHIP], 0, 0))
    return run(
        kernel, meta, (4,), inputs, [(like(shape, bf16), block, None)] * 2,
        [pltpu.VMEM((features, rows), bf16)], 60,
        (8 * rows * features * width, 8 * (rows + features) * width, 0), name, after,
    )


def columns(rows, width, index):
    return pl.BlockSpec((rows, width), lambda s, meta: (0, index(s)))


def across(value, kind):
    seq, batch = lax.axis_size("seq"), lax.axis_size("batch")
    pairs = []
    for s in range(seq):
        mask = 1 + (s % 2 ^ kind)
        pairs += [(s * batch + b, s * batch + (b ^ mask)) for b in range(batch)]
    return lax.ppermute(value, ("seq", "batch"), pairs)


def add_up(*values):
    return sum(v.astype(f32) for v in values).astype(bf16)


class Total:
    def __init__(self, meta, *pieces):
        self.meta, self.pieces = meta, pieces

    def held(self, arrays, after):
        return hold(self.meta, arrays, after) if after else arrays

    def mine(self, at):
        sums = [keep[at].astype(f32) + got[at].astype(f32) for (keep, _), got in zip(self.pieces, self.got)]
        return jnp.concatenate(sums, axis=-1)

    def core(self):
        self.got = [swap_with(send, "seq", 1) for _, send in self.pieces]
        self.now = self.mine(1).astype(bf16)

    def first(self, after=()):
        (self.one,) = self.held([across(self.now, 0)], after)
        self.now = (self.mine((0, 1)) + self.one[1].astype(f32)).astype(bf16)

    def second(self, after=()):
        (self.two,) = self.held([across(self.now, 1)], after)
        self.now = [self.third(z).astype(bf16) for z in range(1, 4)]

    def third(self, z):
        return self.mine((0, 0, z)) + self.one[0, z].astype(f32) + self.two[z].astype(f32)

    def chips(self, after=()):
        there = self.held([swap_with(self.now[z - 1], "seq", 2 * z) for z in range(1, 4)], after)
        done = self.third(0) + sum(part.astype(f32) for part in there)
        self.now = done.astype(bf16)

    def back_chips(self, after=()):
        done = [self.now] + self.held([swap_with(self.now, "seq", 2 * z) for z in range(1, 4)], after)
        self.now = jnp.stack(done)

    def second_whole(self):
        self.two = across(self.now, 1)
        self.part = self.mine((0, 0)) + self.one[0].astype(f32) + self.two.astype(f32)
        self.now = self.part.astype(bf16)

    def all_chips(self):
        there = [self.now] + [swap_with(self.now, "seq", 2 * z) for z in range(1, 4)]
        there = [part.astype(f32) for part in there]
        self.now = ((there[0] + there[1]) + (there[2] + there[3])).astype(bf16)


def spread(meta, value):
    both = jnp.stack([value, across(value, 1)])
    ours = [both, across(both, 0)]
    return ours + [swap_with(part, "seq", 1) for part in ours]


def row_block(meta, j):
    core = meta[CORE] if j < 4 else 1 - meta[CORE]
    first, second = (j % 4) // 2, j % 2
    x = jnp.where(core == 0, first, second) ^ meta[LOW]
    y = jnp.where(core == 0, second, first) ^ meta[HIGH]
    return core * 4 + y * 2 + x


def place_rows(meta, refs, out_ref, start, width):
    for j in range(8):
        part = refs[j // 2]
        rows = part.shape[-2]
        row = pl.multiple_of(row_block(meta, j) * rows, 8)
        out_ref[pl.ds(row, rows), :] = part[j % 2, 0, :, start : start + width].astype(f32)


def join_kernel(meta, *refs):
    step = pl.program_id(0)
    refs, (down_ref, gate_ref, up_ref, out_ref, query_ref, key_ref, value_ref, mlp_ref, att_ref, scr, last_scr) = (
        refs[:4], refs[4:]
    )
    wide, third, features = down_ref.shape[1], up_ref.shape[1], out_ref.shape[1]
    narrow = wide + features + 64
    pl.when(step < 2)(lambda: place_rows(meta, refs, down_ref, 0, wide))
    pl.when(step >= 2)(lambda: place_rows(meta, refs, gate_ref, 0, wide))
    pl.when(step < 3)(lambda: place_rows(meta, refs, up_ref, wide, third))
    place_rows(meta, refs, last_scr.at[step ^ meta[CHIP]], narrow, last_scr.shape[2])

    @pl.when(step == 3)
    def _():
        place_rows(meta, refs, scr, wide, scr.shape[1])
        out_ref[...] = scr[:, :features]
        mlp_ref[...] = scr[:, features - 64 :].T[64:65]
        query_ref[...] = jnp.concatenate([last_scr[z] for z in range(3)], axis=1)[:, :features]
        turned = jnp.concatenate([last_scr[2], last_scr[3]], axis=1).T
        start = features - 512
        key_ref[...] = turned[start : start + KEY_WIDTH]
        value_ref[...] = turned[start + KEY_WIDTH : start + PACKED]
        att_ref[...] = turned[start + PACKED : start + PACKED + 1]


def join(meta, parts, outs, scratch):
    _, _, rows, width = parts[0].shape
    spec = pl.BlockSpec((2, 1, rows, width), lambda s, meta: (0, s ^ meta[CHIP], 0, 0))
    return run(
        join_kernel, meta, (4,), [(a, spec) for a in parts], [(like(shape, f32), out, None) for shape, out in outs],
        scratch, 60, (0, 8 * 4 * rows * width * 6, 0), "join",
    )


def swap_with(value, axis, mask):
    size = lax.axis_size(axis)
    return lax.ppermute(value, axis, [(s, s ^ mask) for s in range(size)])


def shards(
    tokens, assign, lengths, gain_attn, query_weight, key_weight, value_weight, out_weight,
    gain_mlp, gate_weight, up_weight, down_weight, cotangent,
):
    seqs, _, span, features = tokens.shape
    half = span * lax.axis_size("seq")
    full = 2 * half
    me = lax.axis_index("seq")
    matches = assign[:, None] == jnp.arange(lengths.shape[0], dtype=jnp.int32)[None, :]
    seq_lens = jnp.sum(jnp.where(matches, lengths[None, :], 0), axis=1)
    column = lax.axis_index("batch")
    head = jnp.stack([me, me % 2, column % 2, column // 2, me // 2, jnp.full_like(me, full)])
    index = jnp.arange(seqs)
    longer = (seq_lens[None, :] > seq_lens[:, None]) | (
        (seq_lens[None, :] == seq_lens[:, None]) & (index[None, :] < index[:, None])
    )
    ranks = jnp.sum(longer, axis=1, dtype=jnp.int32)
    meta = jnp.concatenate([head.astype(jnp.int32), seq_lens, ranks])
    parted = lax.axis_size("batch") == 4 and lax.axis_size("seq") == 8
    key_weight, value_weight, down_weight = key_weight.T, value_weight.T, down_weight.T
    row = me * span + jnp.arange(span, dtype=jnp.int32)
    pos = jnp.concatenate([row, full - 1 - row]).astype(f32)
    frequency = jnp.power(rope_base, -2.0 * jnp.arange(HEAD_DIM // 2, dtype=f32) / HEAD_DIM)
    angles = pos[:, None] * frequency
    cos, sin = jnp.cos(angles), jnp.sin(angles)
    cos = jnp.concatenate([cos] * 4, axis=1)
    sin = jnp.concatenate([-sin, sin] * 2, axis=1)
    gain_attn = gain_attn.reshape(1, -1)
    gain_mlp = gain_mlp.reshape(1, -1)

    first_weights = (gain_attn, query_weight, key_weight, value_weight, cos, sin)
    mlp_weights = (gain_mlp, out_weight, gate_weight, up_weight, down_weight)
    parted = parted and seqs == 8
    queries, packed, normed, *messages = front(meta, parted, tokens, *first_weights)
    given = (meta, tokens, cotangent, queries, packed, normed, messages, first_weights, mlp_weights)
    if not parted:
        return whole_layer(False, False, *given)
    many = jnp.sum(seq_lens > full - 2 * span) > LONG
    many = many | (jnp.sum(seq_lens > full - 6 * span) > LONGER)
    many = jnp.full((8, 128), many, f32)
    for other in [swap_with(many, "batch", m) for m in range(1, lax.axis_size("batch"))]:
        many = jnp.maximum(many, other)
    return lax.cond(
        many[0, 0] > 0.5, functools.partial(whole_layer, True, False), functools.partial(whole_layer, True, True), *given
    )


def whole_layer(parted, ragged, meta, tokens, cotangent, queries, packed, normed, messages, first_weights, mlp_weights):
    features = tokens.shape[3]
    cos, sin = first_weights[4:]
    keys = Ragged(packed, messages) if ragged else Dense(packed)
    attended, lse = attend(meta, queries, keys)
    block_out, act, cut, d_gate, d_up, n_mlp, d_middle, d_att, d_heads, gain_parts = middle(
        meta, tokens, attended, cotangent, *mlp_weights
    )
    flat_attended = attended.reshape(-1, features)
    rows, hidden = act.shape
    wide, third = hidden // 2, hidden // 3
    after = []
    if parted:
        one = grads_in_parts(
            down_gate_kernel, meta, wide,
            [
                (cut, whole()), (act, columns(rows, wide, lambda s: jnp.minimum(s, 1))),
                (n_mlp, whole()), (d_gate, columns(rows, wide, lambda s: jnp.maximum(s - 2, 0))),
            ],
            "down_gate", (),
        )
        two = grads_in_parts(
            up_out_kernel, meta, features + 64,
            [
                (n_mlp, whole()), (d_up, columns(rows, third, lambda s: jnp.minimum(s, 2))),
                (flat_attended, whole()), (d_att, whole()), (gain_parts, whole()),
            ],
            "up_out", one[:1],
        )
        large = Total(meta, one, two)
        large.core()
        after = [large.now]
    dq, *sent = attend_back(meta, queries, attended, d_heads, lse, cos, sin, keys, after)
    after = []
    if parted:
        large.first([dq])
        sent = hold(meta, sent, [large.now])
        large.second()
    keys.cores(sent)
    keys.finish()
    if parted:
        after = large.now = hold(meta, large.now, keys.parts[1:])
    input_grad, *tail = last(
        meta, parted, tokens, normed, d_middle, dq, *first_weights, keys, after
    )
    if parted:
        large.chips([input_grad])
        small = Total(meta, hold(meta, tail, [large.now]))
        small.core()
        small.first()
        small.second_whole()
        large.back_chips([small.now])
        small.all_chips()
        block = lambda width, index: ((features, hidden), columns(features, width, index))
        fixed = lambda height: ((height, features), columns(height, features, lambda s: 0))
        grad_down, grad_gate, grad_up, grad_out, grad_query, grad_key, grad_value, d_gain_mlp, d_gain_attn = join(
            meta, spread(meta, jnp.concatenate([large.now, small.now], axis=-1)),
            [
                block(wide, lambda s: jnp.minimum(s, 1)), block(wide, lambda s: jnp.maximum(s - 2, 0)),
                block(third, lambda s: jnp.minimum(s, 2)),
                fixed(features), fixed(features), fixed(KEY_WIDTH), fixed(KEY_WIDTH), fixed(1), fixed(1),
            ],
            [pltpu.VMEM((features, features + 64), f32), pltpu.VMEM((4, features, 256), f32)],
        )
    else:
        gain_rows = gain_parts.reshape(-1, 8, features)[:, 0].sum(axis=0, keepdims=True)
        grad_down, grad_gate, grad_up, grad_out, grad_packed, d_gain_attn, d_gain_mlp = lax.psum(
            (
                dot(cut, act, TN), dot(n_mlp, d_gate, TN), dot(n_mlp, d_up, TN),
                dot(flat_attended, d_att, TN), tail[0], tail[1][0], gain_rows,
            ),
            ("seq", "batch"),
        )
        grad_query = grad_packed[:, :features]
        grad_key = grad_packed[:, features : features + KEY_WIDTH].T
        grad_value = grad_packed[:, features + KEY_WIDTH : features + PACKED].T
    return (
        block_out,
        input_grad,
        d_gain_attn.reshape(-1),
        grad_query,
        grad_key.T,
        grad_value.T,
        grad_out,
        d_gain_mlp.reshape(-1),
        grad_gate,
        grad_up,
        grad_down.T,
    )


def solution(mesh):
    rows = P("batch", None, "seq", None)
    return jax.shard_map(
        shards,
        mesh=mesh,
        in_specs=(rows, P("batch")) + (P(),) * 10 + (rows,),
        out_specs=(rows, rows) + (P(),) * 9,
        check_vma=False,
    )
```

```python
import functools

import jax
import jax.numpy as jnp
from jax import lax
from jax.experimental import pallas as pl
from jax.experimental.pallas import tpu as pltpu
from jax.sharding import PartitionSpec as P

HEADS = 9
KV_HEADS = 3
HEAD_DIM = 64
GROUP = HEADS // KV_HEADS
KEY_WIDTH = KV_HEADS * HEAD_DIM
PACKED = 2 * KEY_WIDTH
LANES = 640
TILE = 256

epsilon = 1e-06
rope_base = 10000.0
bf16 = jnp.bfloat16
f32 = jnp.float32
MiB = 1 << 20

NN = (((1,), (0,)), ((), ()))
NT = (((1,), (1,)), ((), ()))
TN = (((0,), (0,)), ((), ()))


def dot(left, right, dims=NN):
    return lax.dot_general(left, right, dims, preferred_element_type=f32)


ME, CORE, LOW, HIGH, CHIP, FULL, LENGTHS = range(7)


def run(kernel, meta, grid, inputs, outputs, scratch, vmem, cost, name, after=()):
    kept = [at for at, out in enumerate(outputs) if out[2] is not None]
    hidden = [outputs[at][2] for at in kept] + list(after)
    count = len(inputs)

    def body(meta_ref, *refs):
        kernel(meta_ref, *refs[:count], *refs[count + len(hidden) :])

    return pl.pallas_call(
        body,
        grid_spec=pltpu.PrefetchScalarGridSpec(
            num_scalar_prefetch=1,
            grid=grid,
            in_specs=[spec for _, spec in inputs] + [pl.BlockSpec(memory_space=pl.ANY)] * len(hidden),
            out_specs=[spec for _, spec, _ in outputs],
            scratch_shapes=scratch,
        ),
        out_shape=[shape for shape, _, _ in outputs],
        input_output_aliases={1 + count + i: at for i, at in enumerate(kept)},
        compiler_params=pltpu.CompilerParams(
            vmem_limit_bytes=vmem * MiB, dimension_semantics=("arbitrary",) * len(grid)
        ),
        cost_estimate=pl.CostEstimate(flops=8 * cost[0], bytes_accessed=cost[1], transcendentals=cost[2]),
        name=name,
    )(meta, *[array for array, _ in inputs], *hidden)


def hold(meta, arrays, after):
    anywhere = pl.BlockSpec(memory_space=pl.ANY)
    out = run(
        lambda *refs: None, meta, (1,), [], [(like(a.shape, a.dtype), anywhere, a) for a in arrays],
        [], 16, (0, 0, 0), "hold", after,
    )
    return list(out)


def whole():
    return pl.BlockSpec(memory_space=pltpu.VMEM)


def like(shape, dtype):
    return jax.ShapeDtypeStruct(shape, dtype)


def seq_block(step, span, width, base=0):
    return pl.BlockSpec((step, 2, span, width), lambda s, meta: (s + base // step, 0, 0, 0))


def flat_block(step, span, width, base=0):
    return pl.BlockSpec((step * 2 * span, width), lambda s, meta: (s + base // step, 0))


def lane_of(shape):
    return lax.broadcasted_iota(jnp.int32, shape, len(shape) - 1)


def swap_halves(chunk):
    first = lane_of(chunk.shape) % HEAD_DIM < HEAD_DIM // 2
    return jnp.where(first, pltpu.roll(chunk, 96, 1), pltpu.roll(chunk, 32, 1))


def unit_rows(rows):
    return lax.rsqrt(jnp.mean(rows * rows, axis=-1, keepdims=True) + epsilon)


def front_kernel(
    packing, meta, tok_ref, gain_ref, wq_ref, wk_ref, wv_ref, cos_ref, sin_ref, q_ref, kv_ref, n_ref, *message_refs
):
    seqs, _, span, features = tok_ref.shape
    rows = tok_ref[...].reshape(seqs * 2 * span, features).astype(f32)
    normed = (rows * unit_rows(rows) * gain_ref[...].astype(f32)).astype(bf16)
    n_ref[...] = normed.reshape(n_ref.shape)
    cos = jnp.concatenate([cos_ref[...]] * seqs, axis=0)
    sin = jnp.concatenate([sin_ref[...]] * seqs, axis=0)
    turn = lambda chunk: chunk * cos + swap_halves(chunk) * sin
    weights = jnp.concatenate([wk_ref[...], wv_ref[...]], axis=0)
    lin = dot(normed, weights, NT)
    chunks = [lin[:, 128 * c : 128 * c + 128] for c in range(3)]
    chunks[0] = turn(chunks[0])
    chunks[1] = jnp.where(lane_of(chunks[1].shape) < HEAD_DIM, turn(chunks[1]), chunks[1])
    packed = jnp.concatenate([c.astype(bf16) for c in chunks], axis=1)
    kv_ref[...] = packed.reshape(kv_ref.shape)
    if packing:
        for e in range(seqs):
            low = packed[2 * e * span : (2 * e + 1) * span]
            high = packed[(2 * e + 1) * span : (2 * e + 2) * span]
            rank = rank_of(meta, seqs * pl.program_id(0) + e)
            put_message(meta, rank, message_refs, low, high)
    queries = [turn(chunk).astype(bf16) for chunk in chunks_of(dot(normed, wq_ref[...]))]
    q_ref[...] = jnp.concatenate(queries, axis=1)[:, :features].reshape(q_ref.shape)


def front(meta, packing, tokens, gain, wq, wk, wv, cos, sin):
    seqs, _, span, features = tokens.shape
    step = 4 if seqs % 4 == 0 else 1
    rows = seqs * 2 * span
    out = lambda width: (like((seqs, 2, span, width), bf16), seq_block(step, span, width), None)
    message = lambda count: (
        like((count, span, PACKED), bf16), pl.BlockSpec((count, span, PACKED), lambda s, meta: (0, 0, 0)), None
    )
    return run(
        functools.partial(front_kernel, packing), meta, (seqs // step,),
        [(tokens, seq_block(step, span, features))] + [(a, whole()) for a in (gain, wq, wk, wv, cos, sin)],
        [out(features), out(PACKED), out(features)] + ([message(8)] * 3 + [message(4)] if packing else []),
        [], 60, (2 * rows * features * 1024, rows * 4500 + 1200000, rows), "front",
    )


LONG, LONGER = 4, 6


def rank_of(meta, s):
    return meta[LENGTHS + 8 + s]


def put_message(meta, rank, refs, low, high):
    chip = meta[CHIP]
    for m in range(1, 4):
        later = (chip ^ m) > chip

        @pl.when(later)
        def _():
            refs[m - 1][rank] = low

        @pl.when(jnp.logical_not(later) & (rank < LONG))
        def _():
            refs[m - 1][2 * rank] = low
            refs[m - 1][2 * rank + 1] = high

    @pl.when((rank >= LONG) & (rank < LONGER))
    def _():
        refs[3][2 * (rank - LONG)] = low
        refs[3][2 * (rank - LONG) + 1] = high


def message_specs(array, m, span, later, s_of):
    def index(add):
        def at(s, meta):
            rank = rank_of(meta, s_of(s))
            chip = meta[CHIP]
            pairs = ((chip ^ m) > chip) == later
            return (jnp.where(pairs, jnp.minimum(2 * rank + add, 6 + add), rank), 0, 0)

        return at

    return [(array, pl.BlockSpec((1, span, PACKED), index(add))) for add in (0, 1)]


def extra_spec(array, span, s_of):
    def at(s, meta):
        return (jnp.clip(rank_of(meta, s_of(s)) - LONG, 0, 1), 0, 0)

    return (array, pl.BlockSpec((2, span, PACKED), at))


class Dense:
    rolled = True

    def __init__(self, packed):
        same = [packed] + [swap_with(packed, "seq", 2 * m) for m in range(1, lax.axis_size("seq") // 2)]
        self.slots = same + [swap_with(part, "seq", 1) for part in same]
        self.chips = len(same)
        self.seqs, _, self.span, _ = packed.shape
        self.full = 2 * self.span * len(self.slots)

    def inputs(self):
        return [(a, seq_block(1, self.span, PACKED)) for a in self.slots]

    def rows(self, place, t):
        span = self.span
        start = place * span if t == 0 else self.full - span - place * span
        return pl.ds(pl.multiple_of(start, span), span)

    def fill(self, meta, refs, kv_scr):
        for slot, ref in enumerate(refs):
            place = place_of(slot, meta[ME], self.chips)
            for t in range(2):
                kv_scr[self.rows(place, t), :] = ref[0, t]

    def outputs(self):
        shape = like((self.chips, self.seqs, 2, self.span, PACKED), bf16)
        spec = pl.BlockSpec((self.chips, 1, 2, self.span, PACKED), lambda s, meta: (0, s, 0, 0, 0))
        return [(shape, spec, None)] * 2

    def store(self, meta, refs, grads):
        for slot in range(2 * self.chips):
            place = place_of(slot, meta[ME], self.chips)
            for t in range(2):
                refs[slot // self.chips][slot % self.chips, 0, t] = grads(self.rows(place, t))

    def cores(self, outs):
        near, far = outs
        other = swap_with(far, "seq", 1)
        self.sums = [add_up(near[m], other[m]) for m in range(self.chips)]
        return self.sums

    def finish(self):
        self.parts = [self.sums[0]] + [swap_with(part, "seq", 2 * m) for m, part in enumerate(self.sums) if m]

    def last_inputs(self, step):
        return [(a, seq_block(step, self.span, PACKED)) for a in self.parts]

    def collect(self, meta, refs, step):
        return sum(ref[...].reshape(step * 2 * self.span, PACKED).astype(f32) for ref in refs)


class Ragged(Dense):
    rolled = False

    def __init__(self, packed, messages):
        self.seqs, _, self.span, _ = packed.shape
        self.full = 2 * self.span * lax.axis_size("seq")
        chips = [swap_with(a, "seq", 2 * m + 2) for m, a in enumerate(messages[:3])]
        chips += [self.between(messages[3], 1, -1), self.between(messages[3], 2, -1)]
        near = [packed] + chips
        self.sets = [near, [swap_with(a, "seq", 1) for a in near]]

    def between(self, value, far, way):
        pairs = ((3, 2), (2, 1)) if far == 1 else ((3, 1),)
        pairs = [p if way < 0 else p[::-1] for p in pairs]
        return lax.ppermute(value, "seq", [(2 * p + c, 2 * q + c) for p, q in pairs for c in range(2)])

    def inputs(self):
        return [(a, whole()) for arrays in self.sets for a in arrays]

    def fill(self, meta, refs, kv_scr):
        s = pl.program_id(0)
        chip, rank = meta[CHIP], rank_of(meta, s)
        for j in range(2):
            own, *mains, near_extra, far_extra = refs[6 * j : 6 * j + 6]
            core = meta[CORE] ^ j

            def put(y, t, value):
                kv_scr[self.rows(2 * y + core, t), :] = value

            for t in range(2):
                put(chip, t, own[s, t])
            for m in range(1, 4):
                y = chip ^ m
                main = mains[m - 1]

                @pl.when(y < chip)
                def _():
                    put(y, 0, main[rank])

                @pl.when((y > chip) & (rank < LONG))
                def _():
                    put(y, 0, main[2 * rank])
                    put(y, 1, main[2 * rank + 1])

                for far, extra in ((1, near_extra), (2, far_extra)):
                    @pl.when((y == chip + far) & (rank >= LONG) & (rank < LONGER))
                    def _():
                        for t in range(2):
                            put(y, t, extra[2 * (rank - LONG) + t])

    def outputs(self):
        own = (like((self.seqs, 2, self.span, PACKED), bf16), seq_block(1, self.span, PACKED), None)
        shape = (32, self.span, PACKED)
        message = (like(shape, bf16), pl.BlockSpec(shape, lambda s, meta: (0, 0, 0)), None)
        return [own, own, message, message]

    def store(self, meta, refs, grads):
        chip, rank = meta[CHIP], rank_of(meta, pl.program_id(0))
        for j in range(2):
            own, out = refs[j], refs[2 + j]
            core = meta[CORE] ^ j
            value = lambda y, t: grads(self.rows(2 * y + core, t))
            for t in range(2):
                own[0, t] = value(chip, t)
            for m in range(1, 4):
                y = chip ^ m
                start = 8 * (m - 1)

                @pl.when(y < chip)
                def _():
                    out[start + rank] = value(y, 0)

                @pl.when((y > chip) & (rank < LONG))
                def _():
                    out[start + 2 * rank] = value(y, 0)
                    out[start + 2 * rank + 1] = value(y, 1)

                for far in (1, 2):
                    @pl.when((y == chip + far) & (rank >= LONG) & (rank < LONGER))
                    def _():
                        for t in range(2):
                            out[20 + 4 * far + 2 * (rank - LONG) + t] = value(y, t)

    def cores(self, outs):
        own, own_far, near, far = outs
        other_own, other = (swap_with(own_far, "seq", 1), swap_with(far, "seq", 1))
        cut = [(0, 8), (8, 16), (16, 24), (24, 28), (28, 32)]
        self.sums = [add_up(own, other_own)] + [add_up(near[a:b], other[a:b]) for a, b in cut]
        return self.sums

    def finish(self):
        own, *rest = self.sums
        self.parts = [own] + [swap_with(a, "seq", 2 * m + 2) for m, a in enumerate(rest[:3])]
        self.parts += [self.between(rest[3], 1, 1), self.between(rest[4], 2, 1)]

    def last_inputs(self, step):
        own, *rest = self.parts
        out = [(own, seq_block(step, self.span, PACKED))]
        for e in range(step):
            s_of = lambda s, e=e: step * s + e
            for m in range(1, 4):
                out += message_specs(rest[m - 1], m, self.span, False, s_of)
            out += [extra_spec(a, self.span, s_of) for a in rest[3:]]
        return out

    def collect(self, meta, refs, step):
        own, *rest = refs
        chip = meta[CHIP]
        out = []
        for e in range(step):
            rank = rank_of(meta, step * pl.program_id(0) + e)
            mine = rest[8 * e : 8 * e + 8]
            both = [own[e, t].astype(f32) for t in range(2)]
            for m in range(1, 4):
                y = chip ^ m
                both[0] += jnp.where((y > chip) | (rank < LONG), mine[2 * m - 2][0].astype(f32), 0.0)
                both[1] += jnp.where((y < chip) & (rank < LONG), mine[2 * m - 1][0].astype(f32), 0.0)
            extra = (rank >= LONG) & (rank < LONGER)
            for t in range(2):
                both[t] += jnp.where(extra, mine[6][t].astype(f32) + mine[7][t].astype(f32), 0.0)
            out += both
        return jnp.concatenate(out, axis=0)


def head_rows(chunks, offset, scale):
    span = chunks[0].shape[0]
    zero = jnp.zeros((span, 128), bf16)
    lower = lane_of((span, 128)) < HEAD_DIM
    out = []
    for h in range(HEADS):
        place = h // GROUP + offset
        chunk = chunks[h // 2]
        if h % 2 != place % 2:
            chunk = pltpu.roll(chunk, HEAD_DIM, 1)
        keep = lower if place % 2 == 0 else jnp.logical_not(lower)
        piece = jnp.where(keep, chunk * scale, 0.0).astype(bf16)
        out.append(jnp.concatenate([piece, zero] if place < 2 else [zero, piece], axis=1))
    out.append(jnp.zeros((LANES - HEADS * span, 256), bf16))
    return jnp.concatenate(out, axis=0)


def chunks_of(rows):
    full = [rows[:, 128 * c : 128 * c + 128].astype(f32) for c in range(4)]
    last = rows[:, 512:576].astype(f32)
    return full + [jnp.concatenate([last, jnp.zeros_like(last)], axis=1)]


def heads_apart(turned):
    lane = lane_of((HEAD_DIM, LANES))
    width = GROUP * HEAD_DIM
    picked = jnp.where(
        lane < width,
        turned[:HEAD_DIM],
        jnp.where(lane < 2 * width, turned[HEAD_DIM : 2 * HEAD_DIM], turned[2 * HEAD_DIM :]),
    )
    out = []
    for c in range(5):
        flipped = picked[:, 128 * c : 128 * c + 128].T
        out.append(jnp.concatenate([flipped[:HEAD_DIM], flipped[HEAD_DIM:]], axis=1))
    return out


def score_bias(tile, place, length, full, t, span):
    row = tile * TILE + lax.broadcasted_iota(jnp.int32, (TILE, 128), 0)
    inner = row % span
    pos = jnp.where(row < full // 2, row, row - inner + (span - 1) - inner)
    own = place * span + lane_of((TILE, 128)) % span
    own = own if t == 0 else full - 1 - own
    return jnp.where((pos <= own) & (pos < length), 0.0, -1e30)


def place_of(slot, me, chips):
    m, j = slot % chips, slot // chips
    return ((me // 2) ^ m) * 2 + ((me % 2) ^ j)


def tiles_for(t, me, length, full, span):
    last = (me + 1) * span if t == 0 else full - me * span
    return pl.cdiv(jnp.minimum(last, length), TILE)


def row_bias(tile, place, length, full, t, span):
    column = tile * TILE + lane_of((span, TILE))
    inner = column % span
    pos = jnp.where(column < full // 2, column, column - inner + (span - 1) - inner)
    own = place * span + lax.broadcasted_iota(jnp.int32, (span, TILE), 0)
    own = own if t == 0 else full - 1 - own
    return jnp.where((pos <= own) & (pos < length), 0.0, -1e30)


def heads_together(rows):
    span = rows.shape[0] // HEADS
    lower = lane_of((span, 128)) < HEAD_DIM
    out = []
    for pair in range(5):
        halves = []
        for h in (2 * pair, 2 * pair + 1):
            if h < HEADS:
                place = h // GROUP + 1
                piece = rows[h * span : (h + 1) * span, 128 * (place // 2) : 128 * (place // 2) + 128]
                halves.append(pltpu.roll(piece, HEAD_DIM, 1) if place % 2 != h % 2 else piece)
        out.append(jnp.where(lower, *halves) if len(halves) == 2 else halves[0])
    return jnp.concatenate(out, axis=1)[:, : HEADS * HEAD_DIM]


def each_count(t, tiles, full, work):
    half = full // 2 // TILE
    for n in range(1 + t * half, half + 1 + t * half):
        pl.when(tiles == n)(functools.partial(work, n))


def forward_kernel(keys, count, meta, q_ref, *refs):
    kv_refs = refs[:count]
    out_ref, lse_ref, kv_scr, *more_scr = refs[count:]
    span, full = keys.span, keys.full
    me = meta[ME]
    length = meta[LENGTHS + pl.program_id(0)]

    def block(t):
        def work(n):
            queries = head_rows(chunks_of(q_ref[0, t]), 0, HEAD_DIM**-0.5)[: HEADS * span]
            scores = []
            for tile in range(n):
                bias = row_bias(tile, me, length, full, t, span)
                raw = dot(queries, kv_scr[tile * TILE : (tile + 1) * TILE, 0:256], NT)
                scores.append(raw + jnp.concatenate([bias] * HEADS, axis=0))
            top = scores[0]
            for score in scores[1:]:
                top = jnp.maximum(top, score)
            top = jnp.max(top, axis=1, keepdims=True)
            total, out = 0.0, 0.0
            for tile, score in enumerate(scores):
                probs = jnp.exp(score - top)
                total += jnp.sum(probs, axis=1, keepdims=True)
                out += dot(probs.astype(bf16), kv_scr[tile * TILE : (tile + 1) * TILE, 128:PACKED])
            finish(out, top, total)

        def finish(out, top, total):
            out_ref[0, t] = heads_together(out / total).astype(bf16)
            column = jnp.broadcast_to(top + jnp.log(total), (HEADS * span, 128))
            row = jnp.concatenate([column, jnp.zeros((LANES - HEADS * span, 128), f32)], axis=0).T
            lse_ref[0, t : t + 1, :] = row[0:1]

        def rolled():
            queries = head_rows(chunks_of(q_ref[0, t]), 0, HEAD_DIM**-0.5)[: HEADS * span]
            top_scr, total_scr, sum_scr = more_scr
            top_scr[...] = jnp.full_like(top_scr, -1e30)
            total_scr[...] = jnp.zeros_like(total_scr)
            sum_scr[...] = jnp.zeros_like(sum_scr)

            def one(tile, carry):
                rows = pl.ds(pl.multiple_of(tile * TILE, TILE), TILE)
                bias = row_bias(tile, me, length, full, t, span)
                score = dot(queries, kv_scr[rows, 0:256], NT) + jnp.concatenate([bias] * HEADS, axis=0)
                before = top_scr[:, 0:1]
                top = jnp.maximum(before, jnp.max(score, axis=1, keepdims=True))
                probs = jnp.exp(score - top)
                shrink = jnp.exp(before - top)
                total_scr[...] = total_scr[...] * shrink + jnp.sum(probs, axis=1, keepdims=True)
                sum_scr[...] = sum_scr[...] * shrink + dot(probs.astype(bf16), kv_scr[rows, 128:PACKED])
                top_scr[...] = jnp.broadcast_to(top, top_scr.shape)
                return carry

            lax.fori_loop(0, tiles_for(t, me, length, full, span), one, 0)
            finish(sum_scr[...], top_scr[:, 0:1], total_scr[:, 0:1])

        if keys.rolled:
            rolled()
        else:
            each_count(t, tiles_for(t, me, length, full, span), full, work)

    def blank(t):
        out_ref[0, t] = jnp.zeros(out_ref.shape[2:], bf16)
        lse_ref[0, t : t + 1, :] = jnp.zeros((1, LANES), f32)

    first = length > me * span
    second = length > full - (me + 1) * span

    @pl.when(pl.program_id(0) == 0)
    def _():
        kv_scr[...] = jnp.zeros_like(kv_scr)

    @pl.when(first)
    def _():
        keys.fill(meta, kv_refs, kv_scr)
        block(0)

    @pl.when(jnp.logical_not(first))
    def _():
        blank(0)

    @pl.when(second)
    def _():
        block(1)

    @pl.when(jnp.logical_not(second))
    def _():
        blank(1)


def attend(meta, queries, keys):
    seqs, _, span, features = queries.shape
    full = keys.full
    tiles = seqs * full * 5 // 4 // TILE
    inputs = keys.inputs()
    return run(
        functools.partial(forward_kernel, keys, len(inputs)), meta, (seqs,),
        [(queries, seq_block(1, span, features))] + inputs,
        [
            (like(queries.shape, bf16), seq_block(1, span, features), None),
            (like((seqs, 2, LANES), f32), pl.BlockSpec((1, 2, LANES), lambda s, meta: (s, 0, 0)), None),
        ],
        [pltpu.VMEM((full, PACKED), bf16)]
        + [pltpu.VMEM((HEADS * span, width), f32) for width in ((128, 128, 256) if keys.rolled else ())],
        60, (tiles * 2 * 2 * 256 * TILE * LANES, seqs * full * PACKED * 2, tiles * TILE * LANES), "attend",
    )


def backward_kernel(keys, count, meta, q_ref, o_ref, g_ref, lse_ref, cos_ref, sin_ref, *refs):
    kv_refs = refs[:count]
    dq_ref, *store_refs, kv_scr, turned_scr, dkv_scr, sum_scr = refs[count:]
    span, full = keys.span, keys.full
    me = meta[ME]
    length = meta[LENGTHS + pl.program_id(0)]

    def block(t):
        queries = head_rows(chunks_of(q_ref[0, t]), 0, HEAD_DIM**-0.5)
        grad_chunks = chunks_of(g_ref[0, t])
        grads = head_rows(grad_chunks, 1, 1.0)
        inner = []
        for g, o in zip(grad_chunks, chunks_of(o_ref[0, t])):
            product = (g * o).T
            inner.append(jnp.sum(product[:HEAD_DIM], axis=0, keepdims=True))
            inner.append(jnp.sum(product[HEAD_DIM:], axis=0, keepdims=True))
        inner = jnp.concatenate(inner, axis=1)
        log_total = lse_ref[0, t : t + 1, :]

        def one(tile):
            rows = pl.ds(pl.multiple_of(tile * TILE, TILE), TILE) if keys.rolled else slice(tile * TILE, (tile + 1) * TILE)
            bias = score_bias(tile, me, length, full, t, span)
            raw = dot(kv_scr[rows, 0:256], queries, NT) + jnp.concatenate([bias] * 5, axis=1)
            probs = jnp.exp(raw - log_total)
            grad_probs = dot(kv_scr[rows, 128:PACKED], grads, NT)
            grad_raw = (probs * (grad_probs - inner)).astype(bf16)
            grad_values = dot(probs.astype(bf16), grads)
            grad_keys = dot(grad_raw, queries)
            dkv_scr[rows, 0:128] += grad_keys[:, :128]
            dkv_scr[rows, 128:256] += grad_keys[:, 128:] + grad_values[:, :128]
            dkv_scr[rows, 256:384] += grad_values[:, 128:]
            return dot(turned_scr[tile], grad_raw)

        def work(n):
            sum_scr[...] = sum(one(tile) for tile in range(n))

        def rolled(tile, carry):
            sum_scr[...] += one(tile)
            return carry

        if keys.rolled:
            sum_scr[...] = jnp.zeros_like(sum_scr)
            lax.fori_loop(0, tiles_for(t, me, length, full, span), rolled, 0)
        else:
            each_count(t, tiles_for(t, me, length, full, span), full, work)
        cos = cos_ref[pl.ds(t * span, span), :]
        sin = sin_ref[pl.ds(t * span, span), :]
        out = [
            chunk * cos - swap_halves(chunk) * sin
            for chunk in heads_apart(sum_scr[...] * HEAD_DIM**-0.5)
        ]
        dq_ref[0, t] = jnp.concatenate(out, axis=1)[:, : dq_ref.shape[3]].astype(bf16)

    def blank(t):
        dq_ref[0, t] = jnp.zeros(dq_ref.shape[2:], bf16)

    first = length > me * span
    second = length > full - (me + 1) * span

    @pl.when(pl.program_id(0) == 0)
    def _():
        kv_scr[...] = jnp.zeros_like(kv_scr)

    @pl.when(first)
    def _():
        keys.fill(meta, kv_refs, kv_scr)
        dkv_scr[...] = jnp.zeros_like(dkv_scr)

        def turn(tile, carry):
            rows = pl.ds(pl.multiple_of(tile * TILE, TILE), TILE)
            turned_scr[tile] = kv_scr[rows, 0:256].T[:KEY_WIDTH]
            return carry

        most = jnp.where(second, tiles_for(1, me, length, full, span), tiles_for(0, me, length, full, span))
        lax.fori_loop(0, most, turn, 0)
        block(0)

    @pl.when(second)
    def _():
        block(1)

    @pl.when(jnp.logical_not(second))
    def _():
        blank(1)

    @pl.when(first)
    def _():
        keys.store(meta, store_refs, lambda rows: dkv_scr[rows, :].astype(bf16))

    @pl.when(jnp.logical_not(first))
    def _():
        blank(0)
        keys.store(meta, store_refs, lambda rows: jnp.zeros((span, PACKED), bf16))


def attend_back(meta, queries, attended, grads, lse, cos, sin, keys, after):
    seqs, _, span, features = queries.shape
    full = keys.full
    tiles = seqs * full * 5 // 4 // TILE
    block = seq_block(1, span, features)
    inputs = keys.inputs()
    return run(
        functools.partial(backward_kernel, keys, len(inputs)), meta, (seqs,),
        [(queries, block), (attended, block), (grads, block)]
        + [(lse, pl.BlockSpec((1, 2, LANES), lambda s, meta: (s, 0, 0))), (cos, whole()), (sin, whole())]
        + inputs,
        [(like(attended.shape, bf16), block, None)] + keys.outputs(),
        [
            pltpu.VMEM((full, PACKED), bf16),
            pltpu.VMEM((full // TILE, KEY_WIDTH, TILE), bf16),
            pltpu.VMEM((full, PACKED), f32),
            pltpu.VMEM((KEY_WIDTH, LANES), f32),
        ],
        60, (tiles * 2 * 5 * 256 * TILE * LANES, seqs * full * PACKED * 4, tiles * TILE * LANES), "attend_back", after,
    )


def middle_kernel(
    meta, tok_ref, att_ref, cot_ref, gain_ref, wo_ref, wg_ref, wu_ref, wd_ref,
    out_ref, act_ref, cut_ref, gate_ref, up_ref, n_ref, dmid_ref, datt_ref, dhead_ref, dgain_ref,
):
    seqs, _, span, features = tok_ref.shape
    rows = seqs * 2 * span
    step = pl.program_id(0)
    flat = lambda ref: ref[...].reshape(rows, features)
    inner = lax.broadcasted_iota(jnp.int32, (2, span, 1), 1) + meta[ME] * span
    second = lax.broadcasted_iota(jnp.int32, (2, span, 1), 0) == 1
    pos = jnp.where(second, meta[FULL] - 1 - inner, inner).reshape(2 * span, 1)
    valid = jnp.concatenate(
        [(pos < meta[LENGTHS + seqs * step + s]).astype(f32) for s in range(seqs)], axis=0
    )
    gain = gain_ref[...].astype(f32)
    middle = flat(tok_ref).astype(f32) + dot(flat(att_ref), wo_ref[...])
    unit = unit_rows(middle)
    scaled = middle * unit
    normed = (scaled * gain).astype(bf16)
    cut = flat(cot_ref).astype(f32) * valid
    cut_low = cut.astype(bf16)
    n_ref[...] = normed
    cut_ref[...] = cut_low
    hidden = wg_ref.shape[1]
    mlp, d_normed = 0.0, 0.0
    for at in range(2):
        part = slice(at * hidden // 2, (at + 1) * hidden // 2)
        gate = dot(normed, wg_ref[:, part])
        up = dot(normed, wu_ref[:, part])
        d_act = dot(cut_low, wd_ref[:, part])
        sig = 0.5 * jnp.tanh(0.5 * gate) + 0.5
        silu = gate * sig
        act = (silu * up).astype(bf16)
        d_gate = (d_act * up * (sig + silu * (1.0 - sig))).astype(bf16)
        d_up = (d_act * silu).astype(bf16)
        act_ref[:, part] = act
        gate_ref[:, part] = d_gate
        up_ref[:, part] = d_up
        mlp += dot(act, wd_ref[:, part], NT)
        d_normed += dot(d_gate, wg_ref[:, part], NT) + dot(d_up, wu_ref[:, part], NT)
    out_ref[...] = (valid * (middle + mlp)).astype(bf16).reshape(out_ref.shape)
    dgain_ref[0:1] = jnp.sum(d_normed * scaled, axis=0, keepdims=True)
    dg = d_normed * gain
    d_middle = cut + unit * (dg - scaled * jnp.mean(dg * scaled, axis=-1, keepdims=True))
    d_att = d_middle.astype(bf16)
    dhead_ref[...] = dot(d_att, wo_ref[...], NT).astype(bf16).reshape(dhead_ref.shape)
    dmid_ref[...] = d_middle.reshape(dmid_ref.shape)
    datt_ref[...] = d_att


def middle(meta, tokens, attended, cotangent, gain, wo, wg, wu, wd):
    seqs, _, span, features = tokens.shape
    hidden = wg.shape[1]
    step = 2
    block = seq_block(step, span, features)
    low = lambda width: (like((seqs * 2 * span, width), bf16), flat_block(step, span, width), None)
    work = seqs * 2 * span * features
    return run(
        middle_kernel, meta, (seqs // step,),
        [(a, block) for a in (tokens, attended, cotangent)] + [(a, whole()) for a in (gain, wo, wg, wu, wd)],
        [
            (like(tokens.shape, bf16), block, None), low(hidden), low(features), low(hidden), low(hidden), low(features),
            (like(tokens.shape, f32), block, None), low(features), (like(tokens.shape, bf16), block, None),
            (like((seqs // step * 8, features), f32), pl.BlockSpec((8, features), lambda s, meta: (s, 0)), None),
        ],
        [], 60, (4 * work * (2 * features + 6 * hidden), 32 * work, work * 3), "middle",
    )


def last_kernel(
    keys, count, parted, meta, tok_ref, n_ref, dmid_ref, dq_ref, gain_ref, wq_ref, wk_ref, wv_ref, cos_ref, sin_ref, *refs
):
    part_refs, refs = refs[:count], refs[count:]
    in_ref, *out_refs, grad_scr, gain_scr = refs
    step, steps = pl.program_id(0), pl.num_programs(0)
    seqs, _, span, features = tok_ref.shape
    rows = seqs * 2 * span
    packed = keys.collect(meta, part_refs, seqs)
    cos = jnp.concatenate([cos_ref[...]] * seqs, axis=0)
    sin = jnp.concatenate([sin_ref[...]] * seqs, axis=0)
    chunks = [packed[:, 128 * c : 128 * c + 128] for c in range(3)]
    turned = [c * cos - swap_halves(c) * sin for c in chunks[:2]]
    turned[1] = jnp.where(lane_of((rows, 128)) < HEAD_DIM, turned[1], chunks[1])
    dkv = jnp.concatenate(turned + [chunks[2]], axis=1).astype(bf16)
    dq = dq_ref[...].reshape(rows, features)
    weights = jnp.concatenate([wk_ref[...], wv_ref[...]], axis=0)
    d_normed = dot(dq, wq_ref[...], NT) + dot(dkv, weights)
    values = tok_ref[...].reshape(rows, features).astype(f32)
    unit = unit_rows(values)
    scaled = values * unit
    gain_part = jnp.sum(d_normed * scaled, axis=0, keepdims=True)
    fill = jnp.zeros((rows, grad_scr.shape[1] - features - PACKED), bf16)
    grad_part = dot(n_ref[...].reshape(rows, features), jnp.concatenate([dq, dkv, fill], axis=1), TN)

    @pl.when(step == 0)
    def _():
        grad_scr[...] = grad_part
        gain_scr[...] = jnp.zeros_like(gain_scr)
        gain_scr[0:1, :] = gain_part

    @pl.when(step > 0)
    def _():
        grad_scr[...] += grad_part
        gain_scr[0:1, :] += gain_part

    dg = d_normed * gain_ref[...].astype(f32)
    back = unit * (dg - scaled * jnp.mean(dg * scaled, axis=-1, keepdims=True))
    in_ref[...] = dmid_ref[...] + back.reshape(in_ref.shape)

    @pl.when(step == steps - 1)
    def _():
        if parted:
            used = features + PACKED
            both = jnp.concatenate(
                [grad_scr[:, :used], gain_scr[...].T[:, : grad_scr.shape[1] - used]], axis=1
            )
            width = both.shape[1] // 4
            for c in range(4):
                place = lambda ref, f, s: ref.at[f, s, c]
                put_parts(meta, both[:, width * c : width * c + width], place, *out_refs)
        else:
            out_refs[0][...] = grad_scr[...]
            out_refs[1][...] = gain_scr[...]


def last(meta, parted, tokens, normed, d_middle, dq, gain, wq, wk, wv, cos, sin, keys, after):
    seqs, _, span, features = tokens.shape
    step = 2
    rows = seqs * 2 * span
    block = seq_block(step, span, features)
    if parted:
        shape = (2, 2, 4, features // 8, 256)
        more = [(like(shape, bf16), pl.BlockSpec(shape, lambda s, meta: (0,) * 5), None)] * 2
    else:
        more = [
            (like((height, width), f32), pl.BlockSpec((height, width), lambda s, meta: (0, 0)), None)
            for height, width in ((features, 1024), (128, features))
        ]
    inputs = keys.last_inputs(step)
    return run(
        functools.partial(last_kernel, keys, len(inputs), parted), meta, (seqs // step,),
        [(a, block) for a in (tokens, normed, d_middle, dq)]
        + [(a, whole()) for a in (gain, wq, wk, wv, cos, sin)] + inputs,
        [(like(tokens.shape, f32), block, None)] + more,
        [pltpu.VMEM((features, 1024), f32), pltpu.VMEM((128, features), f32)],
        60, (2 * rows * features * 2048, rows * 13000, rows), "last", after,
    )


def put_parts(meta, value, place, keep_ref, send_ref):
    core, low, high = meta[CORE], meta[LOW], meta[HIGH]
    rows = value.shape[0] // 8
    for owner in range(2):
        def write(ref):
            for at in range(4):
                x, y = (at % 2) ^ low, (at // 2) ^ high
                first, second = (x, y) if owner == 0 else (y, x)
                start = (owner * 4 + at) * rows
                place(ref, first, second)[...] = value[start : start + rows].astype(bf16)

        pl.when(core == owner)(lambda: write(keep_ref))
        pl.when(core != owner)(lambda: write(send_ref))


def down_gate_kernel(meta, cut_ref, act_ref, n_ref, gate_ref, keep_ref, send_ref, turned_scr):
    step = pl.program_id(0)
    place = lambda ref, f, s: ref.at[f, s, 0]

    @pl.when(step == 0)
    def _():
        turned_scr[...] = cut_ref[...].T

    @pl.when(step == 2)
    def _():
        turned_scr[...] = n_ref[...].T

    @pl.when(step < 2)
    def _():
        put_parts(meta, dot(turned_scr[...], act_ref[...]), place, keep_ref, send_ref)

    @pl.when(step >= 2)
    def _():
        put_parts(meta, dot(turned_scr[...], gate_ref[...]), place, keep_ref, send_ref)


def up_out_kernel(meta, n_ref, up_ref, att_ref, datt_ref, gain_ref, keep_ref, send_ref, turned_scr):
    step = pl.program_id(0)
    width = keep_ref.shape[-1]
    features = turned_scr.shape[0]
    place = lambda ref, f, s: ref.at[f, s, 0]

    @pl.when(step == 0)
    def _():
        turned_scr[...] = n_ref[...].T

    @pl.when(step < 3)
    def _():
        value = dot(turned_scr[...], up_ref[...])
        value = jnp.concatenate([value, jnp.zeros((features, width - value.shape[1]), f32)], axis=1)
        put_parts(meta, value, place, keep_ref, send_ref)

    @pl.when(step == 3)
    def _():
        value = dot(att_ref[...].T, datt_ref[...])
        gains = jnp.sum(gain_ref[...].reshape(-1, 8, features)[:, 0], axis=0, keepdims=True)
        gains = jnp.broadcast_to(gains, (128, features)).T
        value = jnp.concatenate([value, gains[:, : width - features]], axis=1)
        put_parts(meta, value, place, keep_ref, send_ref)


def grads_in_parts(kernel, meta, width, inputs, name, after):
    rows, features = inputs[0][0].shape
    shape = (2, 2, 4, features // 8, width)
    block = pl.BlockSpec((2, 2, 1) + shape[3:], lambda s, meta: (0, 0, s ^ meta[CHIP], 0, 0))
    return run(
        kernel, meta, (4,), inputs, [(like(shape, bf16), block, None)] * 2,
        [pltpu.VMEM((features, rows), bf16)], 60,
        (8 * rows * features * width, 8 * (rows + features) * width, 0), name, after,
    )


def columns(rows, width, index):
    return pl.BlockSpec((rows, width), lambda s, meta: (0, index(s)))


def across(value, kind):
    seq, batch = lax.axis_size("seq"), lax.axis_size("batch")
    pairs = []
    for s in range(seq):
        mask = 3 if kind == 2 else 1 + (s % 2 ^ kind)
        pairs += [(s * batch + b, s * batch + (b ^ mask)) for b in range(batch)]
    return lax.ppermute(value, ("seq", "batch"), pairs)


def add_up(*values):
    return sum(v.astype(f32) for v in values).astype(bf16)


class Total:
    def __init__(self, meta, *pieces):
        self.meta, self.pieces = meta, pieces

    def held(self, arrays, after):
        return hold(self.meta, arrays, after) if after else arrays

    def mine(self, at):
        sums = [keep[at].astype(f32) + got[at].astype(f32) for (keep, _), got in zip(self.pieces, self.got)]
        return jnp.concatenate(sums, axis=-1)

    def core(self):
        self.got = [swap_with(send, "seq", 1) for _, send in self.pieces]

    def toward_first(self):
        self.now = self.mine(1).astype(bf16)

    def first(self, after=()):
        (self.one,) = self.held([across(self.now, 0)], after)
        self.now = (self.mine((0, 1)) + self.one[1].astype(f32)).astype(bf16)

    def second(self, after=()):
        (self.two,) = self.held([across(self.now, 1)], after)
        self.now = [self.third(z).astype(bf16) for z in range(1, 4)]

    def third(self, z):
        return self.mine((0, 0, z)) + self.one[0, z].astype(f32) + self.two[z].astype(f32)

    def chips(self, after=()):
        there = self.held([swap_with(self.now[z - 1], "seq", 2 * z) for z in range(1, 4)], after)
        done = self.third(0) + sum(part.astype(f32) for part in there)
        self.now = done.astype(bf16)

    def back_chips(self, after=()):
        done = [self.now] + self.held([swap_with(self.now, "seq", 2 * z) for z in range(1, 4)], after)
        self.now = jnp.stack(done)

    def batch_at_once(self):
        there = [across(self.mine(at).astype(bf16), kind) for kind, at in ((2, (1, 1)), (0, (1, 0)), (1, (0, 1)))]
        self.now = (self.mine((0, 0)) + sum(part.astype(f32) for part in there)).astype(bf16)

    def all_chips(self):
        there = [self.now] + [swap_with(self.now, "seq", 2 * z) for z in range(1, 4)]
        there = [part.astype(f32) for part in there]
        self.now = ((there[0] + there[1]) + (there[2] + there[3])).astype(bf16)


def spread(meta, value):
    both = jnp.stack([value, across(value, 1)])
    ours = [both, across(both, 0)]
    return ours + [swap_with(part, "seq", 1) for part in ours]


def row_block(meta, j):
    core = meta[CORE] if j < 4 else 1 - meta[CORE]
    first, second = (j % 4) // 2, j % 2
    x = jnp.where(core == 0, first, second) ^ meta[LOW]
    y = jnp.where(core == 0, second, first) ^ meta[HIGH]
    return core * 4 + y * 2 + x


def place_rows(meta, refs, out_ref, start, width):
    for j in range(8):
        part = refs[j // 2]
        rows = part.shape[-2]
        row = pl.multiple_of(row_block(meta, j) * rows, 8)
        out_ref[pl.ds(row, rows), :] = part[j % 2, 0, :, start : start + width].astype(f32)


def join_kernel(meta, *refs):
    step = pl.program_id(0)
    refs, (down_ref, gate_ref, up_ref, out_ref, query_ref, key_ref, value_ref, mlp_ref, att_ref, scr, last_scr) = (
        refs[:4], refs[4:]
    )
    wide, third, features = down_ref.shape[1], up_ref.shape[1], out_ref.shape[1]
    narrow = wide + features + 64
    pl.when(step < 2)(lambda: place_rows(meta, refs, down_ref, 0, wide))
    pl.when(step >= 2)(lambda: place_rows(meta, refs, gate_ref, 0, wide))
    pl.when(step < 3)(lambda: place_rows(meta, refs, up_ref, wide, third))
    place_rows(meta, refs, last_scr.at[step ^ meta[CHIP]], narrow, last_scr.shape[2])

    @pl.when(step == 3)
    def _():
        place_rows(meta, refs, scr, wide, scr.shape[1])
        out_ref[...] = scr[:, :features]
        mlp_ref[...] = scr[:, features - 64 :].T[64:65]
        query_ref[...] = jnp.concatenate([last_scr[z] for z in range(3)], axis=1)[:, :features]
        turned = jnp.concatenate([last_scr[2], last_scr[3]], axis=1).T
        start = features - 512
        key_ref[...] = turned[start : start + KEY_WIDTH]
        value_ref[...] = turned[start + KEY_WIDTH : start + PACKED]
        att_ref[...] = turned[start + PACKED : start + PACKED + 1]


def join(meta, parts, outs, scratch):
    _, _, rows, width = parts[0].shape
    spec = pl.BlockSpec((2, 1, rows, width), lambda s, meta: (0, s ^ meta[CHIP], 0, 0))
    return run(
        join_kernel, meta, (4,), [(a, spec) for a in parts], [(like(shape, f32), out, None) for shape, out in outs],
        scratch, 60, (0, 8 * 4 * rows * width * 6, 0), "join",
    )


def swap_with(value, axis, mask):
    size = lax.axis_size(axis)
    return lax.ppermute(value, axis, [(s, s ^ mask) for s in range(size)])


def shards(
    tokens, assign, lengths, gain_attn, query_weight, key_weight, value_weight, out_weight,
    gain_mlp, gate_weight, up_weight, down_weight, cotangent,
):
    seqs, _, span, features = tokens.shape
    half = span * lax.axis_size("seq")
    full = 2 * half
    me = lax.axis_index("seq")
    matches = assign[:, None] == jnp.arange(lengths.shape[0], dtype=jnp.int32)[None, :]
    seq_lens = jnp.sum(jnp.where(matches, lengths[None, :], 0), axis=1)
    column = lax.axis_index("batch")
    head = jnp.stack([me, me % 2, column % 2, column // 2, me // 2, jnp.full_like(me, full)])
    index = jnp.arange(seqs)
    longer = (seq_lens[None, :] > seq_lens[:, None]) | (
        (seq_lens[None, :] == seq_lens[:, None]) & (index[None, :] < index[:, None])
    )
    ranks = jnp.sum(longer, axis=1, dtype=jnp.int32)
    meta = jnp.concatenate([head.astype(jnp.int32), seq_lens, ranks])
    parted = lax.axis_size("batch") == 4 and lax.axis_size("seq") == 8
    key_weight, value_weight, down_weight = key_weight.T, value_weight.T, down_weight.T
    row = me * span + jnp.arange(span, dtype=jnp.int32)
    pos = jnp.concatenate([row, full - 1 - row]).astype(f32)
    frequency = jnp.power(rope_base, -2.0 * jnp.arange(HEAD_DIM // 2, dtype=f32) / HEAD_DIM)
    angles = pos[:, None] * frequency
    cos, sin = jnp.cos(angles), jnp.sin(angles)
    cos = jnp.concatenate([cos] * 4, axis=1)
    sin = jnp.concatenate([-sin, sin] * 2, axis=1)
    gain_attn = gain_attn.reshape(1, -1)
    gain_mlp = gain_mlp.reshape(1, -1)

    first_weights = (gain_attn, query_weight, key_weight, value_weight, cos, sin)
    mlp_weights = (gain_mlp, out_weight, gate_weight, up_weight, down_weight)
    parted = parted and seqs == 8
    queries, packed, normed, *messages = front(meta, parted, tokens, *first_weights)
    given = (meta, tokens, cotangent, queries, packed, normed, messages, first_weights, mlp_weights)
    if not parted:
        return whole_layer(False, False, *given)
    many = jnp.sum(seq_lens > full - 2 * span) > LONG
    many = many | (jnp.sum(seq_lens > full - 6 * span) > LONGER)
    many = jnp.full((8, 128), many, f32)
    for other in [swap_with(many, "batch", m) for m in range(1, lax.axis_size("batch"))]:
        many = jnp.maximum(many, other)
    return lax.cond(
        many[0, 0] > 0.5, functools.partial(whole_layer, True, False), functools.partial(whole_layer, True, True), *given
    )


def whole_layer(parted, ragged, meta, tokens, cotangent, queries, packed, normed, messages, first_weights, mlp_weights):
    features = tokens.shape[3]
    cos, sin = first_weights[4:]
    keys = Ragged(packed, messages) if ragged else Dense(packed)
    attended, lse = attend(meta, queries, keys)
    block_out, act, cut, d_gate, d_up, n_mlp, d_middle, d_att, d_heads, gain_parts = middle(
        meta, tokens, attended, cotangent, *mlp_weights
    )
    flat_attended = attended.reshape(-1, features)
    rows, hidden = act.shape
    wide, third = hidden // 2, hidden // 3
    after = []
    if parted:
        one = grads_in_parts(
            down_gate_kernel, meta, wide,
            [
                (cut, whole()), (act, columns(rows, wide, lambda s: jnp.minimum(s, 1))),
                (n_mlp, whole()), (d_gate, columns(rows, wide, lambda s: jnp.maximum(s - 2, 0))),
            ],
            "down_gate", (),
        )
        two = grads_in_parts(
            up_out_kernel, meta, features + 64,
            [
                (n_mlp, whole()), (d_up, columns(rows, third, lambda s: jnp.minimum(s, 2))),
                (flat_attended, whole()), (d_att, whole()), (gain_parts, whole()),
            ],
            "up_out", one[:1],
        )
        large = Total(meta, one, two)
        large.core()
        large.toward_first()
        after = [large.now]
    dq, *sent = attend_back(meta, queries, attended, d_heads, lse, cos, sin, keys, after)
    after = []
    if parted:
        large.first([dq])
        sent = sent[:-1] + hold(meta, sent[-1:], [large.one])
        large.second()
    keys.cores(sent)
    keys.finish()
    if parted:
        after = large.now = hold(meta, large.now, keys.parts[1:])
    input_grad, *tail = last(
        meta, parted, tokens, normed, d_middle, dq, *first_weights, keys, after
    )
    if parted:
        large.chips([input_grad])
        small = Total(meta, hold(meta, tail, [large.now]))
        small.core()
        small.batch_at_once()
        large.back_chips([small.now])
        small.all_chips()
        block = lambda width, index: ((features, hidden), columns(features, width, index))
        fixed = lambda height: ((height, features), columns(height, features, lambda s: 0))
        grad_down, grad_gate, grad_up, grad_out, grad_query, grad_key, grad_value, d_gain_mlp, d_gain_attn = join(
            meta, spread(meta, jnp.concatenate([large.now, small.now], axis=-1)),
            [
                block(wide, lambda s: jnp.minimum(s, 1)), block(wide, lambda s: jnp.maximum(s - 2, 0)),
                block(third, lambda s: jnp.minimum(s, 2)),
                fixed(features), fixed(features), fixed(KEY_WIDTH), fixed(KEY_WIDTH), fixed(1), fixed(1),
            ],
            [pltpu.VMEM((features, features + 64), f32), pltpu.VMEM((4, features, 256), f32)],
        )
    else:
        gain_rows = gain_parts.reshape(-1, 8, features)[:, 0].sum(axis=0, keepdims=True)
        grad_down, grad_gate, grad_up, grad_out, grad_packed, d_gain_attn, d_gain_mlp = lax.psum(
            (
                dot(cut, act, TN), dot(n_mlp, d_gate, TN), dot(n_mlp, d_up, TN),
                dot(flat_attended, d_att, TN), tail[0], tail[1][0], gain_rows,
            ),
            ("seq", "batch"),
        )
        grad_query = grad_packed[:, :features]
        grad_key = grad_packed[:, features : features + KEY_WIDTH].T
        grad_value = grad_packed[:, features + KEY_WIDTH : features + PACKED].T
    return (
        block_out,
        input_grad,
        d_gain_attn.reshape(-1),
        grad_query,
        grad_key.T,
        grad_value.T,
        grad_out,
        d_gain_mlp.reshape(-1),
        grad_gate,
        grad_up,
        grad_down.T,
    )


def solution(mesh):
    rows = P("batch", None, "seq", None)
    return jax.shard_map(
        shards,
        mesh=mesh,
        in_specs=(rows, P("batch")) + (P(),) * 10 + (rows,),
        out_specs=(rows, rows) + (P(),) * 9,
        check_vma=False,
    )
```

```python
import functools

import jax
import jax.numpy as jnp
from jax import lax
from jax.experimental import pallas as pl
from jax.experimental.pallas import tpu as pltpu
from jax.sharding import PartitionSpec as P

HEADS = 9
KV_HEADS = 3
HEAD_DIM = 64
GROUP = HEADS // KV_HEADS
KEY_WIDTH = KV_HEADS * HEAD_DIM
PACKED = 2 * KEY_WIDTH
LANES = 640
TILE = 256

epsilon = 1e-06
rope_base = 10000.0
bf16 = jnp.bfloat16
f32 = jnp.float32
MiB = 1 << 20

NN = (((1,), (0,)), ((), ()))
NT = (((1,), (1,)), ((), ()))
TN = (((0,), (0,)), ((), ()))


def dot(left, right, dims=NN):
    return lax.dot_general(left, right, dims, preferred_element_type=f32)


ME, CORE, LOW, HIGH, CHIP, FULL, LENGTHS = range(7)


def run(kernel, meta, grid, inputs, outputs, scratch, vmem, cost, name, after=()):
    kept = [at for at, out in enumerate(outputs) if out[2] is not None]
    hidden = [outputs[at][2] for at in kept] + list(after)
    count = len(inputs)

    def body(meta_ref, *refs):
        kernel(meta_ref, *refs[:count], *refs[count + len(hidden) :])

    return pl.pallas_call(
        body,
        grid_spec=pltpu.PrefetchScalarGridSpec(
            num_scalar_prefetch=1,
            grid=grid,
            in_specs=[spec for _, spec in inputs] + [pl.BlockSpec(memory_space=pl.ANY)] * len(hidden),
            out_specs=[spec for _, spec, _ in outputs],
            scratch_shapes=scratch,
        ),
        out_shape=[shape for shape, _, _ in outputs],
        input_output_aliases={1 + count + i: at for i, at in enumerate(kept)},
        compiler_params=pltpu.CompilerParams(
            vmem_limit_bytes=vmem * MiB, dimension_semantics=("arbitrary",) * len(grid)
        ),
        cost_estimate=pl.CostEstimate(flops=8 * cost[0], bytes_accessed=cost[1], transcendentals=cost[2]),
        name=name,
    )(meta, *[array for array, _ in inputs], *hidden)


def hold(meta, arrays, after):
    anywhere = pl.BlockSpec(memory_space=pl.ANY)
    out = run(
        lambda *refs: None, meta, (1,), [], [(like(a.shape, a.dtype), anywhere, a) for a in arrays],
        [], 16, (0, 0, 0), "hold", after,
    )
    return list(out)


def whole():
    return pl.BlockSpec(memory_space=pltpu.VMEM)


def like(shape, dtype):
    return jax.ShapeDtypeStruct(shape, dtype)


def seq_block(step, span, width, base=0):
    return pl.BlockSpec((step, 2, span, width), lambda s, meta: (s + base // step, 0, 0, 0))


def flat_block(step, span, width, base=0):
    return pl.BlockSpec((step * 2 * span, width), lambda s, meta: (s + base // step, 0))


def lane_of(shape):
    return lax.broadcasted_iota(jnp.int32, shape, len(shape) - 1)


def swap_halves(chunk):
    first = lane_of(chunk.shape) % HEAD_DIM < HEAD_DIM // 2
    return jnp.where(first, pltpu.roll(chunk, 96, 1), pltpu.roll(chunk, 32, 1))


def unit_rows(rows):
    return lax.rsqrt(jnp.mean(rows * rows, axis=-1, keepdims=True) + epsilon)


def front_kernel(
    packing, meta, tok_ref, gain_ref, wq_ref, wk_ref, wv_ref, cos_ref, sin_ref, q_ref, kv_ref, n_ref, *message_refs
):
    seqs, _, span, features = tok_ref.shape
    rows = tok_ref[...].reshape(seqs * 2 * span, features).astype(f32)
    normed = (rows * unit_rows(rows) * gain_ref[...].astype(f32)).astype(bf16)
    n_ref[...] = normed.reshape(n_ref.shape)
    cos = jnp.concatenate([cos_ref[...]] * seqs, axis=0)
    sin = jnp.concatenate([sin_ref[...]] * seqs, axis=0)
    turn = lambda chunk: chunk * cos + swap_halves(chunk) * sin
    weights = jnp.concatenate([wk_ref[...], wv_ref[...]], axis=0)
    lin = dot(normed, weights, NT)
    chunks = [lin[:, 128 * c : 128 * c + 128] for c in range(3)]
    chunks[0] = turn(chunks[0])
    chunks[1] = jnp.where(lane_of(chunks[1].shape) < HEAD_DIM, turn(chunks[1]), chunks[1])
    packed = jnp.concatenate([c.astype(bf16) for c in chunks], axis=1)
    kv_ref[...] = packed.reshape(kv_ref.shape)
    if packing:
        for e in range(seqs):
            low = packed[2 * e * span : (2 * e + 1) * span]
            high = packed[(2 * e + 1) * span : (2 * e + 2) * span]
            rank = rank_of(meta, seqs * pl.program_id(0) + e)
            put_message(meta, rank, message_refs, low, high)
    queries = [turn(chunk).astype(bf16) for chunk in chunks_of(dot(normed, wq_ref[...]))]
    q_ref[...] = jnp.concatenate(queries, axis=1)[:, :features].reshape(q_ref.shape)


def front(meta, packing, tokens, gain, wq, wk, wv, cos, sin):
    seqs, _, span, features = tokens.shape
    step = 4 if seqs % 4 == 0 else 1
    rows = seqs * 2 * span
    out = lambda width: (like((seqs, 2, span, width), bf16), seq_block(step, span, width), None)
    message = lambda count: (
        like((count, span, PACKED), bf16), pl.BlockSpec((count, span, PACKED), lambda s, meta: (0, 0, 0)), None
    )
    return run(
        functools.partial(front_kernel, packing), meta, (seqs // step,),
        [(tokens, seq_block(step, span, features))] + [(a, whole()) for a in (gain, wq, wk, wv, cos, sin)],
        [out(features), out(PACKED), out(features)] + ([message(8)] * 3 + [message(4)] if packing else []),
        [], 60, (2 * rows * features * 1024, rows * 4500 + 1200000, rows), "front",
    )


LONG, LONGER = 4, 6


def rank_of(meta, s):
    return meta[LENGTHS + 8 + s]


def put_message(meta, rank, refs, low, high):
    chip = meta[CHIP]
    for m in range(1, 4):
        later = (chip ^ m) > chip

        @pl.when(later)
        def _():
            refs[m - 1][rank] = low

        @pl.when(jnp.logical_not(later) & (rank < LONG))
        def _():
            refs[m - 1][2 * rank] = low
            refs[m - 1][2 * rank + 1] = high

    @pl.when((rank >= LONG) & (rank < LONGER))
    def _():
        refs[3][2 * (rank - LONG)] = low
        refs[3][2 * (rank - LONG) + 1] = high


def message_specs(array, m, span, later, s_of):
    def index(add):
        def at(s, meta):
            rank = rank_of(meta, s_of(s))
            chip = meta[CHIP]
            pairs = ((chip ^ m) > chip) == later
            return (jnp.where(pairs, jnp.minimum(2 * rank + add, 6 + add), rank), 0, 0)

        return at

    return [(array, pl.BlockSpec((1, span, PACKED), index(add))) for add in (0, 1)]


def extra_spec(array, span, s_of):
    def at(s, meta):
        return (jnp.clip(rank_of(meta, s_of(s)) - LONG, 0, 1), 0, 0)

    return (array, pl.BlockSpec((2, span, PACKED), at))


class Dense:
    def __init__(self, packed):
        same = [packed] + [swap_with(packed, "seq", 2 * m) for m in range(1, lax.axis_size("seq") // 2)]
        self.slots = same + [swap_with(part, "seq", 1) for part in same]
        self.chips = len(same)
        self.seqs, _, self.span, _ = packed.shape
        self.full = 2 * self.span * len(self.slots)

    def inputs(self):
        return [(a, seq_block(1, self.span, PACKED)) for a in self.slots]

    def rows(self, place, t):
        span = self.span
        start = place * span if t == 0 else self.full - span - place * span
        return pl.ds(pl.multiple_of(start, span), span)

    def fill(self, meta, refs, kv_scr):
        for slot, ref in enumerate(refs):
            place = place_of(slot, meta[ME], self.chips)
            for t in range(2):
                kv_scr[self.rows(place, t), :] = ref[0, t]

    def outputs(self):
        shape = like((self.chips, self.seqs, 2, self.span, PACKED), bf16)
        spec = pl.BlockSpec((self.chips, 1, 2, self.span, PACKED), lambda s, meta: (0, s, 0, 0, 0))
        return [(shape, spec, None)] * 2

    def store(self, meta, refs, grads):
        for slot in range(2 * self.chips):
            place = place_of(slot, meta[ME], self.chips)
            for t in range(2):
                refs[slot // self.chips][slot % self.chips, 0, t] = grads(self.rows(place, t))

    def cores(self, outs):
        near, far = outs
        other = swap_with(far, "seq", 1)
        self.sums = [add_up(near[m], other[m]) for m in range(self.chips)]
        return self.sums

    def finish(self):
        self.parts = [self.sums[0]] + [swap_with(part, "seq", 2 * m) for m, part in enumerate(self.sums) if m]

    def last_inputs(self, step):
        return [(a, seq_block(step, self.span, PACKED)) for a in self.parts]

    def collect(self, meta, refs, step):
        return sum(ref[...].reshape(step * 2 * self.span, PACKED).astype(f32) for ref in refs)


class Ragged(Dense):
    def __init__(self, packed, messages):
        self.seqs, _, self.span, _ = packed.shape
        self.full = 2 * self.span * lax.axis_size("seq")
        chips = [swap_with(a, "seq", 2 * m + 2) for m, a in enumerate(messages[:3])]
        chips += [self.between(messages[3], 1, -1), self.between(messages[3], 2, -1)]
        near = [packed] + chips
        self.sets = [near, [swap_with(a, "seq", 1) for a in near]]

    def between(self, value, far, way):
        pairs = ((3, 2), (2, 1)) if far == 1 else ((3, 1),)
        pairs = [p if way < 0 else p[::-1] for p in pairs]
        return lax.ppermute(value, "seq", [(2 * p + c, 2 * q + c) for p, q in pairs for c in range(2)])

    def inputs(self):
        return [(a, whole()) for arrays in self.sets for a in arrays]

    def fill(self, meta, refs, kv_scr):
        s = pl.program_id(0)
        chip, rank = meta[CHIP], rank_of(meta, s)
        for j in range(2):
            own, *mains, near_extra, far_extra = refs[6 * j : 6 * j + 6]
            core = meta[CORE] ^ j

            def put(y, t, value):
                kv_scr[self.rows(2 * y + core, t), :] = value

            for t in range(2):
                put(chip, t, own[s, t])
            for m in range(1, 4):
                y = chip ^ m
                main = mains[m - 1]

                @pl.when(y < chip)
                def _():
                    put(y, 0, main[rank])

                @pl.when((y > chip) & (rank < LONG))
                def _():
                    put(y, 0, main[2 * rank])
                    put(y, 1, main[2 * rank + 1])

                for far, extra in ((1, near_extra), (2, far_extra)):
                    @pl.when((y == chip + far) & (rank >= LONG) & (rank < LONGER))
                    def _():
                        for t in range(2):
                            put(y, t, extra[2 * (rank - LONG) + t])

    def outputs(self):
        own = (like((self.seqs, 2, self.span, PACKED), bf16), seq_block(1, self.span, PACKED), None)
        shape = (32, self.span, PACKED)
        message = (like(shape, bf16), pl.BlockSpec(shape, lambda s, meta: (0, 0, 0)), None)
        return [own, own, message, message]

    def store(self, meta, refs, grads):
        chip, rank = meta[CHIP], rank_of(meta, pl.program_id(0))
        for j in range(2):
            own, out = refs[j], refs[2 + j]
            core = meta[CORE] ^ j
            value = lambda y, t: grads(self.rows(2 * y + core, t))
            for t in range(2):
                own[0, t] = value(chip, t)
            for m in range(1, 4):
                y = chip ^ m
                start = 8 * (m - 1)

                @pl.when(y < chip)
                def _():
                    out[start + rank] = value(y, 0)

                @pl.when((y > chip) & (rank < LONG))
                def _():
                    out[start + 2 * rank] = value(y, 0)
                    out[start + 2 * rank + 1] = value(y, 1)

                for far in (1, 2):
                    @pl.when((y == chip + far) & (rank >= LONG) & (rank < LONGER))
                    def _():
                        for t in range(2):
                            out[20 + 4 * far + 2 * (rank - LONG) + t] = value(y, t)

    def cores(self, outs):
        own, own_far, near, far = outs
        other_own, other = (swap_with(own_far, "seq", 1), swap_with(far, "seq", 1))
        cut = [(0, 8), (8, 16), (16, 24), (24, 28), (28, 32)]
        self.sums = [add_up(own, other_own)] + [add_up(near[a:b], other[a:b]) for a, b in cut]
        return self.sums

    def finish(self):
        own, *rest = self.sums
        self.parts = [own] + [swap_with(a, "seq", 2 * m + 2) for m, a in enumerate(rest[:3])]
        self.parts += [self.between(rest[3], 1, 1), self.between(rest[4], 2, 1)]

    def last_inputs(self, step):
        own, *rest = self.parts
        out = [(own, seq_block(step, self.span, PACKED))]
        for e in range(step):
            s_of = lambda s, e=e: step * s + e
            for m in range(1, 4):
                out += message_specs(rest[m - 1], m, self.span, False, s_of)
            out += [extra_spec(a, self.span, s_of) for a in rest[3:]]
        return out

    def collect(self, meta, refs, step):
        own, *rest = refs
        chip = meta[CHIP]
        out = []
        for e in range(step):
            rank = rank_of(meta, step * pl.program_id(0) + e)
            mine = rest[8 * e : 8 * e + 8]
            both = [own[e, t].astype(f32) for t in range(2)]
            for m in range(1, 4):
                y = chip ^ m
                both[0] += jnp.where((y > chip) | (rank < LONG), mine[2 * m - 2][0].astype(f32), 0.0)
                both[1] += jnp.where((y < chip) & (rank < LONG), mine[2 * m - 1][0].astype(f32), 0.0)
            extra = (rank >= LONG) & (rank < LONGER)
            for t in range(2):
                both[t] += jnp.where(extra, mine[6][t].astype(f32) + mine[7][t].astype(f32), 0.0)
            out += both
        return jnp.concatenate(out, axis=0)


def head_rows(chunks, offset, scale):
    span = chunks[0].shape[0]
    zero = jnp.zeros((span, 128), bf16)
    lower = lane_of((span, 128)) < HEAD_DIM
    out = []
    for h in range(HEADS):
        place = h // GROUP + offset
        chunk = chunks[h // 2]
        if h % 2 != place % 2:
            chunk = pltpu.roll(chunk, HEAD_DIM, 1)
        keep = lower if place % 2 == 0 else jnp.logical_not(lower)
        piece = jnp.where(keep, chunk * scale, 0.0).astype(bf16)
        out.append(jnp.concatenate([piece, zero] if place < 2 else [zero, piece], axis=1))
    out.append(jnp.zeros((LANES - HEADS * span, 256), bf16))
    return jnp.concatenate(out, axis=0)


def chunks_of(rows):
    full = [rows[:, 128 * c : 128 * c + 128].astype(f32) for c in range(4)]
    last = rows[:, 512:576].astype(f32)
    return full + [jnp.concatenate([last, jnp.zeros_like(last)], axis=1)]


def heads_apart(turned):
    lane = lane_of((HEAD_DIM, LANES))
    width = GROUP * HEAD_DIM
    picked = jnp.where(
        lane < width,
        turned[:HEAD_DIM],
        jnp.where(lane < 2 * width, turned[HEAD_DIM : 2 * HEAD_DIM], turned[2 * HEAD_DIM :]),
    )
    out = []
    for c in range(5):
        flipped = picked[:, 128 * c : 128 * c + 128].T
        out.append(jnp.concatenate([flipped[:HEAD_DIM], flipped[HEAD_DIM:]], axis=1))
    return out


def score_bias(tile, place, length, full, t, span):
    row = tile * TILE + lax.broadcasted_iota(jnp.int32, (TILE, 128), 0)
    inner = row % span
    pos = jnp.where(row < full // 2, row, row - inner + (span - 1) - inner)
    own = place * span + lane_of((TILE, 128)) % span
    own = own if t == 0 else full - 1 - own
    return jnp.where((pos <= own) & (pos < length), 0.0, -1e30)


def place_of(slot, me, chips):
    m, j = slot % chips, slot // chips
    return ((me // 2) ^ m) * 2 + ((me % 2) ^ j)


def tiles_for(t, me, length, full, span):
    last = (me + 1) * span if t == 0 else full - me * span
    return pl.cdiv(jnp.minimum(last, length), TILE)


def row_bias(tile, place, length, full, t, span):
    column = tile * TILE + lane_of((span, TILE))
    inner = column % span
    pos = jnp.where(column < full // 2, column, column - inner + (span - 1) - inner)
    own = place * span + lax.broadcasted_iota(jnp.int32, (span, TILE), 0)
    own = own if t == 0 else full - 1 - own
    return jnp.where((pos <= own) & (pos < length), 0.0, -1e30)


def heads_together(rows):
    span = rows.shape[0] // HEADS
    lower = lane_of((span, 128)) < HEAD_DIM
    out = []
    for pair in range(5):
        halves = []
        for h in (2 * pair, 2 * pair + 1):
            if h < HEADS:
                place = h // GROUP + 1
                piece = rows[h * span : (h + 1) * span, 128 * (place // 2) : 128 * (place // 2) + 128]
                halves.append(pltpu.roll(piece, HEAD_DIM, 1) if place % 2 != h % 2 else piece)
        out.append(jnp.where(lower, *halves) if len(halves) == 2 else halves[0])
    return jnp.concatenate(out, axis=1)[:, : HEADS * HEAD_DIM]


def each_count(t, tiles, full, work):
    half = full // 2 // TILE
    for n in range(1 + t * half, half + 1 + t * half):
        pl.when(tiles == n)(functools.partial(work, n))


def forward_kernel(keys, count, meta, q_ref, *refs):
    kv_refs = refs[:count]
    out_ref, lse_ref, kv_scr = refs[count:]
    span, full = keys.span, keys.full
    me = meta[ME]
    length = meta[LENGTHS + pl.program_id(0)]

    def block(t):
        def work(n):
            queries = head_rows(chunks_of(q_ref[0, t]), 0, HEAD_DIM**-0.5)[: HEADS * span]
            scores = []
            for tile in range(n):
                bias = row_bias(tile, me, length, full, t, span)
                raw = dot(queries, kv_scr[tile * TILE : (tile + 1) * TILE, 0:256], NT)
                scores.append(raw + jnp.concatenate([bias] * HEADS, axis=0))
            top = scores[0]
            for score in scores[1:]:
                top = jnp.maximum(top, score)
            top = jnp.max(top, axis=1, keepdims=True)
            total, out = 0.0, 0.0
            for tile, score in enumerate(scores):
                probs = jnp.exp(score - top)
                total += jnp.sum(probs, axis=1, keepdims=True)
                out += dot(probs.astype(bf16), kv_scr[tile * TILE : (tile + 1) * TILE, 128:PACKED])
            finish(out, top, total)

        def finish(out, top, total):
            out_ref[0, t] = heads_together(out / total).astype(bf16)
            column = jnp.broadcast_to(top + jnp.log(total), (HEADS * span, 128))
            row = jnp.concatenate([column, jnp.zeros((LANES - HEADS * span, 128), f32)], axis=0).T
            lse_ref[0, t : t + 1, :] = row[0:1]

        each_count(t, tiles_for(t, me, length, full, span), full, work)

    def blank(t):
        out_ref[0, t] = jnp.zeros(out_ref.shape[2:], bf16)
        lse_ref[0, t : t + 1, :] = jnp.zeros((1, LANES), f32)

    first = length > me * span
    second = length > full - (me + 1) * span

    @pl.when(pl.program_id(0) == 0)
    def _():
        kv_scr[...] = jnp.zeros_like(kv_scr)

    @pl.when(first)
    def _():
        keys.fill(meta, kv_refs, kv_scr)
        block(0)

    @pl.when(jnp.logical_not(first))
    def _():
        blank(0)

    @pl.when(second)
    def _():
        block(1)

    @pl.when(jnp.logical_not(second))
    def _():
        blank(1)


def attend(meta, queries, keys):
    seqs, _, span, features = queries.shape
    full = keys.full
    tiles = seqs * full * 5 // 4 // TILE
    inputs = keys.inputs()
    return run(
        functools.partial(forward_kernel, keys, len(inputs)), meta, (seqs,),
        [(queries, seq_block(1, span, features))] + inputs,
        [
            (like(queries.shape, bf16), seq_block(1, span, features), None),
            (like((seqs, 2, LANES), f32), pl.BlockSpec((1, 2, LANES), lambda s, meta: (s, 0, 0)), None),
        ],
        [pltpu.VMEM((full, PACKED), bf16)],
        60, (tiles * 2 * 2 * 256 * TILE * LANES, seqs * full * PACKED * 2, tiles * TILE * LANES), "attend",
    )


def backward_kernel(keys, count, meta, q_ref, o_ref, g_ref, lse_ref, cos_ref, sin_ref, *refs):
    kv_refs = refs[:count]
    dq_ref, *store_refs, kv_scr, turned_scr, dkv_scr, sum_scr = refs[count:]
    span, full = keys.span, keys.full
    me = meta[ME]
    length = meta[LENGTHS + pl.program_id(0)]

    def block(t):
        queries = head_rows(chunks_of(q_ref[0, t]), 0, HEAD_DIM**-0.5)
        grad_chunks = chunks_of(g_ref[0, t])
        grads = head_rows(grad_chunks, 1, 1.0)
        inner = []
        for g, o in zip(grad_chunks, chunks_of(o_ref[0, t])):
            product = (g * o).T
            inner.append(jnp.sum(product[:HEAD_DIM], axis=0, keepdims=True))
            inner.append(jnp.sum(product[HEAD_DIM:], axis=0, keepdims=True))
        inner = jnp.concatenate(inner, axis=1)
        log_total = lse_ref[0, t : t + 1, :]

        def one(tile):
            rows = slice(tile * TILE, (tile + 1) * TILE)
            bias = score_bias(tile, me, length, full, t, span)
            raw = dot(kv_scr[rows, 0:256], queries, NT) + jnp.concatenate([bias] * 5, axis=1)
            probs = jnp.exp(raw - log_total)
            grad_probs = dot(kv_scr[rows, 128:PACKED], grads, NT)
            grad_raw = (probs * (grad_probs - inner)).astype(bf16)
            grad_values = dot(probs.astype(bf16), grads)
            grad_keys = dot(grad_raw, queries)
            dkv_scr[rows, 0:128] += grad_keys[:, :128]
            dkv_scr[rows, 128:256] += grad_keys[:, 128:] + grad_values[:, :128]
            dkv_scr[rows, 256:384] += grad_values[:, 128:]
            return dot(turned_scr[tile], grad_raw)

        def work(n):
            sum_scr[...] = sum(one(tile) for tile in range(n))

        each_count(t, tiles_for(t, me, length, full, span), full, work)
        cos = cos_ref[pl.ds(t * span, span), :]
        sin = sin_ref[pl.ds(t * span, span), :]
        out = [
            chunk * cos - swap_halves(chunk) * sin
            for chunk in heads_apart(sum_scr[...] * HEAD_DIM**-0.5)
        ]
        dq_ref[0, t] = jnp.concatenate(out, axis=1)[:, : dq_ref.shape[3]].astype(bf16)

    def blank(t):
        dq_ref[0, t] = jnp.zeros(dq_ref.shape[2:], bf16)

    first = length > me * span
    second = length > full - (me + 1) * span

    @pl.when(pl.program_id(0) == 0)
    def _():
        kv_scr[...] = jnp.zeros_like(kv_scr)

    @pl.when(first)
    def _():
        keys.fill(meta, kv_refs, kv_scr)
        dkv_scr[...] = jnp.zeros_like(dkv_scr)

        def turn(tile, carry):
            rows = pl.ds(pl.multiple_of(tile * TILE, TILE), TILE)
            turned_scr[tile] = kv_scr[rows, 0:256].T[:KEY_WIDTH]
            return carry

        most = jnp.where(second, tiles_for(1, me, length, full, span), tiles_for(0, me, length, full, span))
        lax.fori_loop(0, most, turn, 0)
        block(0)

    @pl.when(second)
    def _():
        block(1)

    @pl.when(jnp.logical_not(second))
    def _():
        blank(1)

    @pl.when(first)
    def _():
        keys.store(meta, store_refs, lambda rows: dkv_scr[rows, :].astype(bf16))

    @pl.when(jnp.logical_not(first))
    def _():
        blank(0)
        keys.store(meta, store_refs, lambda rows: jnp.zeros((span, PACKED), bf16))


def attend_back(meta, queries, attended, grads, lse, cos, sin, keys, after):
    seqs, _, span, features = queries.shape
    full = keys.full
    tiles = seqs * full * 5 // 4 // TILE
    block = seq_block(1, span, features)
    inputs = keys.inputs()
    return run(
        functools.partial(backward_kernel, keys, len(inputs)), meta, (seqs,),
        [(queries, block), (attended, block), (grads, block)]
        + [(lse, pl.BlockSpec((1, 2, LANES), lambda s, meta: (s, 0, 0))), (cos, whole()), (sin, whole())]
        + inputs,
        [(like(attended.shape, bf16), block, None)] + keys.outputs(),
        [
            pltpu.VMEM((full, PACKED), bf16),
            pltpu.VMEM((full // TILE, KEY_WIDTH, TILE), bf16),
            pltpu.VMEM((full, PACKED), f32),
            pltpu.VMEM((KEY_WIDTH, LANES), f32),
        ],
        60, (tiles * 2 * 5 * 256 * TILE * LANES, seqs * full * PACKED * 4, tiles * TILE * LANES), "attend_back", after,
    )


def middle_kernel(
    meta, tok_ref, att_ref, cot_ref, gain_ref, wo_ref, wg_ref, wu_ref, wd_ref,
    out_ref, act_ref, cut_ref, gate_ref, up_ref, n_ref, dmid_ref, datt_ref, dhead_ref, dgain_ref,
):
    seqs, _, span, features = tok_ref.shape
    rows = seqs * 2 * span
    step = pl.program_id(0)
    flat = lambda ref: ref[...].reshape(rows, features)
    inner = lax.broadcasted_iota(jnp.int32, (2, span, 1), 1) + meta[ME] * span
    second = lax.broadcasted_iota(jnp.int32, (2, span, 1), 0) == 1
    pos = jnp.where(second, meta[FULL] - 1 - inner, inner).reshape(2 * span, 1)
    valid = jnp.concatenate(
        [(pos < meta[LENGTHS + seqs * step + s]).astype(f32) for s in range(seqs)], axis=0
    )
    gain = gain_ref[...].astype(f32)
    middle = flat(tok_ref).astype(f32) + dot(flat(att_ref), wo_ref[...])
    unit = unit_rows(middle)
    scaled = middle * unit
    normed = (scaled * gain).astype(bf16)
    cut = flat(cot_ref).astype(f32) * valid
    cut_low = cut.astype(bf16)
    n_ref[...] = normed
    cut_ref[...] = cut_low
    hidden = wg_ref.shape[1]
    mlp, d_normed = 0.0, 0.0
    for at in range(2):
        part = slice(at * hidden // 2, (at + 1) * hidden // 2)
        gate = dot(normed, wg_ref[:, part])
        up = dot(normed, wu_ref[:, part])
        d_act = dot(cut_low, wd_ref[:, part])
        sig = 0.5 * jnp.tanh(0.5 * gate) + 0.5
        silu = gate * sig
        act = (silu * up).astype(bf16)
        d_gate = (d_act * up * (sig + silu * (1.0 - sig))).astype(bf16)
        d_up = (d_act * silu).astype(bf16)
        act_ref[:, part] = act
        gate_ref[:, part] = d_gate
        up_ref[:, part] = d_up
        mlp += dot(act, wd_ref[:, part], NT)
        d_normed += dot(d_gate, wg_ref[:, part], NT) + dot(d_up, wu_ref[:, part], NT)
    out_ref[...] = (valid * (middle + mlp)).astype(bf16).reshape(out_ref.shape)
    dgain_ref[0:1] = jnp.sum(d_normed * scaled, axis=0, keepdims=True)
    dg = d_normed * gain
    d_middle = cut + unit * (dg - scaled * jnp.mean(dg * scaled, axis=-1, keepdims=True))
    d_att = d_middle.astype(bf16)
    dhead_ref[...] = dot(d_att, wo_ref[...], NT).astype(bf16).reshape(dhead_ref.shape)
    dmid_ref[...] = d_middle.reshape(dmid_ref.shape)
    datt_ref[...] = d_att


def middle(meta, tokens, attended, cotangent, gain, wo, wg, wu, wd):
    seqs, _, span, features = tokens.shape
    hidden = wg.shape[1]
    step = 2
    block = seq_block(step, span, features)
    low = lambda width: (like((seqs * 2 * span, width), bf16), flat_block(step, span, width), None)
    work = seqs * 2 * span * features
    return run(
        middle_kernel, meta, (seqs // step,),
        [(a, block) for a in (tokens, attended, cotangent)] + [(a, whole()) for a in (gain, wo, wg, wu, wd)],
        [
            (like(tokens.shape, bf16), block, None), low(hidden), low(features), low(hidden), low(hidden), low(features),
            (like(tokens.shape, f32), block, None), low(features), (like(tokens.shape, bf16), block, None),
            (like((seqs // step * 8, features), f32), pl.BlockSpec((8, features), lambda s, meta: (s, 0)), None),
        ],
        [], 60, (4 * work * (2 * features + 6 * hidden), 32 * work, work * 3), "middle",
    )


def last_kernel(
    keys, count, parted, meta, tok_ref, n_ref, dmid_ref, dq_ref, gain_ref, wq_ref, wk_ref, wv_ref, cos_ref, sin_ref, *refs
):
    part_refs, refs = refs[:count], refs[count:]
    in_ref, *out_refs, grad_scr, gain_scr = refs
    step, steps = pl.program_id(0), pl.num_programs(0)
    seqs, _, span, features = tok_ref.shape
    rows = seqs * 2 * span
    packed = keys.collect(meta, part_refs, seqs)
    cos = jnp.concatenate([cos_ref[...]] * seqs, axis=0)
    sin = jnp.concatenate([sin_ref[...]] * seqs, axis=0)
    chunks = [packed[:, 128 * c : 128 * c + 128] for c in range(3)]
    turned = [c * cos - swap_halves(c) * sin for c in chunks[:2]]
    turned[1] = jnp.where(lane_of((rows, 128)) < HEAD_DIM, turned[1], chunks[1])
    dkv = jnp.concatenate(turned + [chunks[2]], axis=1).astype(bf16)
    dq = dq_ref[...].reshape(rows, features)
    weights = jnp.concatenate([wk_ref[...], wv_ref[...]], axis=0)
    d_normed = dot(dq, wq_ref[...], NT) + dot(dkv, weights)
    values = tok_ref[...].reshape(rows, features).astype(f32)
    unit = unit_rows(values)
    scaled = values * unit
    gain_part = jnp.sum(d_normed * scaled, axis=0, keepdims=True)
    fill = jnp.zeros((rows, grad_scr.shape[1] - features - PACKED), bf16)
    grad_part = dot(n_ref[...].reshape(rows, features), jnp.concatenate([dq, dkv, fill], axis=1), TN)

    @pl.when(step == 0)
    def _():
        grad_scr[...] = grad_part
        gain_scr[...] = jnp.zeros_like(gain_scr)
        gain_scr[0:1, :] = gain_part

    @pl.when(step > 0)
    def _():
        grad_scr[...] += grad_part
        gain_scr[0:1, :] += gain_part

    dg = d_normed * gain_ref[...].astype(f32)
    back = unit * (dg - scaled * jnp.mean(dg * scaled, axis=-1, keepdims=True))
    in_ref[...] = dmid_ref[...] + back.reshape(in_ref.shape)

    @pl.when(step == steps - 1)
    def _():
        if parted:
            used = features + PACKED
            both = jnp.concatenate(
                [grad_scr[:, :used], gain_scr[...].T[:, : grad_scr.shape[1] - used]], axis=1
            )
            width = both.shape[1] // 4
            for c in range(4):
                place = lambda ref, f, s: ref.at[f, s, c]
                put_parts(meta, both[:, width * c : width * c + width], place, *out_refs)
        else:
            out_refs[0][...] = grad_scr[...]
            out_refs[1][...] = gain_scr[...]


def last(meta, parted, tokens, normed, d_middle, dq, gain, wq, wk, wv, cos, sin, keys, after):
    seqs, _, span, features = tokens.shape
    step = 2
    rows = seqs * 2 * span
    block = seq_block(step, span, features)
    if parted:
        shape = (2, 2, 4, features // 8, 256)
        more = [(like(shape, bf16), pl.BlockSpec(shape, lambda s, meta: (0,) * 5), None)] * 2
    else:
        more = [
            (like((height, width), f32), pl.BlockSpec((height, width), lambda s, meta: (0, 0)), None)
            for height, width in ((features, 1024), (128, features))
        ]
    inputs = keys.last_inputs(step)
    return run(
        functools.partial(last_kernel, keys, len(inputs), parted), meta, (seqs // step,),
        [(a, block) for a in (tokens, normed, d_middle, dq)]
        + [(a, whole()) for a in (gain, wq, wk, wv, cos, sin)] + inputs,
        [(like(tokens.shape, f32), block, None)] + more,
        [pltpu.VMEM((features, 1024), f32), pltpu.VMEM((128, features), f32)],
        60, (2 * rows * features * 2048, rows * 13000, rows), "last", after,
    )


def put_parts(meta, value, place, keep_ref, send_ref):
    core, low, high = meta[CORE], meta[LOW], meta[HIGH]
    rows = value.shape[0] // 8
    for owner in range(2):
        def write(ref):
            for at in range(4):
                x, y = (at % 2) ^ low, (at // 2) ^ high
                first, second = (x, y) if owner == 0 else (y, x)
                start = (owner * 4 + at) * rows
                place(ref, first, second)[...] = value[start : start + rows].astype(bf16)

        pl.when(core == owner)(lambda: write(keep_ref))
        pl.when(core != owner)(lambda: write(send_ref))


def down_gate_kernel(meta, cut_ref, act_ref, n_ref, gate_ref, keep_ref, send_ref, turned_scr):
    step = pl.program_id(0)
    place = lambda ref, f, s: ref.at[f, s, 0]

    @pl.when(step == 0)
    def _():
        turned_scr[...] = cut_ref[...].T

    @pl.when(step == 2)
    def _():
        turned_scr[...] = n_ref[...].T

    @pl.when(step < 2)
    def _():
        put_parts(meta, dot(turned_scr[...], act_ref[...]), place, keep_ref, send_ref)

    @pl.when(step >= 2)
    def _():
        put_parts(meta, dot(turned_scr[...], gate_ref[...]), place, keep_ref, send_ref)


def up_out_kernel(meta, n_ref, up_ref, att_ref, datt_ref, gain_ref, keep_ref, send_ref, turned_scr):
    step = pl.program_id(0)
    width = keep_ref.shape[-1]
    features = turned_scr.shape[0]
    place = lambda ref, f, s: ref.at[f, s, 0]

    @pl.when(step == 0)
    def _():
        turned_scr[...] = n_ref[...].T

    @pl.when(step < 3)
    def _():
        value = dot(turned_scr[...], up_ref[...])
        value = jnp.concatenate([value, jnp.zeros((features, width - value.shape[1]), f32)], axis=1)
        put_parts(meta, value, place, keep_ref, send_ref)

    @pl.when(step == 3)
    def _():
        value = dot(att_ref[...].T, datt_ref[...])
        gains = jnp.sum(gain_ref[...].reshape(-1, 8, features)[:, 0], axis=0, keepdims=True)
        gains = jnp.broadcast_to(gains, (128, features)).T
        value = jnp.concatenate([value, gains[:, : width - features]], axis=1)
        put_parts(meta, value, place, keep_ref, send_ref)


def grads_in_parts(kernel, meta, width, inputs, name, after):
    rows, features = inputs[0][0].shape
    shape = (2, 2, 4, features // 8, width)
    block = pl.BlockSpec((2, 2, 1) + shape[3:], lambda s, meta: (0, 0, s ^ meta[CHIP], 0, 0))
    return run(
        kernel, meta, (4,), inputs, [(like(shape, bf16), block, None)] * 2,
        [pltpu.VMEM((features, rows), bf16)], 60,
        (8 * rows * features * width, 8 * (rows + features) * width, 0), name, after,
    )


def columns(rows, width, index):
    return pl.BlockSpec((rows, width), lambda s, meta: (0, index(s)))


def across(value, kind):
    seq, batch = lax.axis_size("seq"), lax.axis_size("batch")
    pairs = []
    for s in range(seq):
        mask = 3 if kind == 2 else 1 + (s % 2 ^ kind)
        pairs += [(s * batch + b, s * batch + (b ^ mask)) for b in range(batch)]
    return lax.ppermute(value, ("seq", "batch"), pairs)


def add_up(*values):
    return sum(v.astype(f32) for v in values).astype(bf16)


class Total:
    def __init__(self, meta, *pieces):
        self.meta, self.pieces = meta, pieces

    def held(self, arrays, after):
        return hold(self.meta, arrays, after) if after else arrays

    def mine(self, at):
        sums = [keep[at].astype(f32) + got[at].astype(f32) for (keep, _), got in zip(self.pieces, self.got)]
        return jnp.concatenate(sums, axis=-1)

    def core(self):
        self.got = [swap_with(send, "seq", 1) for _, send in self.pieces]

    def toward_first(self):
        self.now = self.mine(1).astype(bf16)

    def first(self, after=()):
        (self.one,) = self.held([across(self.now, 0)], after)
        self.now = (self.mine((0, 1)) + self.one[1].astype(f32)).astype(bf16)

    def second(self, after=()):
        (self.two,) = self.held([across(self.now, 1)], after)
        self.now = [self.third(z).astype(bf16) for z in range(1, 4)]

    def third(self, z):
        return self.mine((0, 0, z)) + self.one[0, z].astype(f32) + self.two[z].astype(f32)

    def chips(self, after=()):
        there = self.held([swap_with(self.now[z - 1], "seq", 2 * z) for z in range(1, 4)], after)
        done = self.third(0) + sum(part.astype(f32) for part in there)
        self.now = done.astype(bf16)

    def back_chips(self, after=()):
        done = [self.now] + self.held([swap_with(self.now, "seq", 2 * z) for z in range(1, 4)], after)
        self.now = jnp.stack(done)

    def batch_at_once(self):
        there = [across(self.mine(at).astype(bf16), kind) for kind, at in ((2, (1, 1)), (0, (1, 0)), (1, (0, 1)))]
        self.now = (self.mine((0, 0)) + sum(part.astype(f32) for part in there)).astype(bf16)

    def all_chips(self):
        there = [self.now] + [swap_with(self.now, "seq", 2 * z) for z in range(1, 4)]
        there = [part.astype(f32) for part in there]
        self.now = ((there[0] + there[1]) + (there[2] + there[3])).astype(bf16)


def spread(meta, value):
    both = jnp.stack([value, across(value, 1)])
    ours = [both, across(both, 0)]
    return ours + [swap_with(part, "seq", 1) for part in ours]


def row_block(meta, j):
    core = meta[CORE] if j < 4 else 1 - meta[CORE]
    first, second = (j % 4) // 2, j % 2
    x = jnp.where(core == 0, first, second) ^ meta[LOW]
    y = jnp.where(core == 0, second, first) ^ meta[HIGH]
    return core * 4 + y * 2 + x


def place_rows(meta, refs, out_ref, start, width):
    for j in range(8):
        part = refs[j // 2]
        rows = part.shape[-2]
        row = pl.multiple_of(row_block(meta, j) * rows, 8)
        out_ref[pl.ds(row, rows), :] = part[j % 2, 0, :, start : start + width].astype(f32)


def join_kernel(meta, *refs):
    step = pl.program_id(0)
    refs, (down_ref, gate_ref, up_ref, out_ref, query_ref, key_ref, value_ref, mlp_ref, att_ref, scr, last_scr) = (
        refs[:4], refs[4:]
    )
    wide, third, features = down_ref.shape[1], up_ref.shape[1], out_ref.shape[1]
    narrow = wide + features + 64
    pl.when(step < 2)(lambda: place_rows(meta, refs, down_ref, 0, wide))
    pl.when(step >= 2)(lambda: place_rows(meta, refs, gate_ref, 0, wide))
    pl.when(step < 3)(lambda: place_rows(meta, refs, up_ref, wide, third))
    place_rows(meta, refs, last_scr.at[step ^ meta[CHIP]], narrow, last_scr.shape[2])

    @pl.when(step == 3)
    def _():
        place_rows(meta, refs, scr, wide, scr.shape[1])
        out_ref[...] = scr[:, :features]
        mlp_ref[...] = scr[:, features - 64 :].T[64:65]
        query_ref[...] = jnp.concatenate([last_scr[z] for z in range(3)], axis=1)[:, :features]
        turned = jnp.concatenate([last_scr[2], last_scr[3]], axis=1).T
        start = features - 512
        key_ref[...] = turned[start : start + KEY_WIDTH]
        value_ref[...] = turned[start + KEY_WIDTH : start + PACKED]
        att_ref[...] = turned[start + PACKED : start + PACKED + 1]


def join(meta, parts, outs, scratch):
    _, _, rows, width = parts[0].shape
    spec = pl.BlockSpec((2, 1, rows, width), lambda s, meta: (0, s ^ meta[CHIP], 0, 0))
    return run(
        join_kernel, meta, (4,), [(a, spec) for a in parts], [(like(shape, f32), out, None) for shape, out in outs],
        scratch, 60, (0, 8 * 4 * rows * width * 6, 0), "join",
    )


def swap_with(value, axis, mask):
    size = lax.axis_size(axis)
    return lax.ppermute(value, axis, [(s, s ^ mask) for s in range(size)])


def shards(
    tokens, assign, lengths, gain_attn, query_weight, key_weight, value_weight, out_weight,
    gain_mlp, gate_weight, up_weight, down_weight, cotangent,
):
    seqs, _, span, features = tokens.shape
    half = span * lax.axis_size("seq")
    full = 2 * half
    me = lax.axis_index("seq")
    matches = assign[:, None] == jnp.arange(lengths.shape[0], dtype=jnp.int32)[None, :]
    seq_lens = jnp.sum(jnp.where(matches, lengths[None, :], 0), axis=1)
    column = lax.axis_index("batch")
    head = jnp.stack([me, me % 2, column % 2, column // 2, me // 2, jnp.full_like(me, full)])
    index = jnp.arange(seqs)
    longer = (seq_lens[None, :] > seq_lens[:, None]) | (
        (seq_lens[None, :] == seq_lens[:, None]) & (index[None, :] < index[:, None])
    )
    ranks = jnp.sum(longer, axis=1, dtype=jnp.int32)
    meta = jnp.concatenate([head.astype(jnp.int32), seq_lens, ranks])
    parted = lax.axis_size("batch") == 4 and lax.axis_size("seq") == 8
    key_weight, value_weight, down_weight = key_weight.T, value_weight.T, down_weight.T
    row = me * span + jnp.arange(span, dtype=jnp.int32)
    pos = jnp.concatenate([row, full - 1 - row]).astype(f32)
    frequency = jnp.power(rope_base, -2.0 * jnp.arange(HEAD_DIM // 2, dtype=f32) / HEAD_DIM)
    angles = pos[:, None] * frequency
    cos, sin = jnp.cos(angles), jnp.sin(angles)
    cos = jnp.concatenate([cos] * 4, axis=1)
    sin = jnp.concatenate([-sin, sin] * 2, axis=1)
    gain_attn = gain_attn.reshape(1, -1)
    gain_mlp = gain_mlp.reshape(1, -1)

    first_weights = (gain_attn, query_weight, key_weight, value_weight, cos, sin)
    mlp_weights = (gain_mlp, out_weight, gate_weight, up_weight, down_weight)
    parted = parted and seqs == 8
    queries, packed, normed, *messages = front(meta, parted, tokens, *first_weights)
    given = (meta, tokens, cotangent, queries, packed, normed, messages, first_weights, mlp_weights)
    if not parted:
        return whole_layer(False, False, *given)
    many = jnp.sum(seq_lens > full - 2 * span) > LONG
    many = many | (jnp.sum(seq_lens > full - 6 * span) > LONGER)
    many = jnp.full((8, 128), many, f32)
    for other in [swap_with(many, "batch", m) for m in range(1, lax.axis_size("batch"))]:
        many = jnp.maximum(many, other)
    return lax.cond(
        many[0, 0] > 0.5, functools.partial(whole_layer, True, False), functools.partial(whole_layer, True, True), *given
    )


def whole_layer(parted, ragged, meta, tokens, cotangent, queries, packed, normed, messages, first_weights, mlp_weights):
    features = tokens.shape[3]
    cos, sin = first_weights[4:]
    keys = Ragged(packed, messages) if ragged else Dense(packed)
    attended, lse = attend(meta, queries, keys)
    block_out, act, cut, d_gate, d_up, n_mlp, d_middle, d_att, d_heads, gain_parts = middle(
        meta, tokens, attended, cotangent, *mlp_weights
    )
    flat_attended = attended.reshape(-1, features)
    rows, hidden = act.shape
    wide, third = hidden // 2, hidden // 3
    after = []
    if parted:
        one = grads_in_parts(
            down_gate_kernel, meta, wide,
            [
                (cut, whole()), (act, columns(rows, wide, lambda s: jnp.minimum(s, 1))),
                (n_mlp, whole()), (d_gate, columns(rows, wide, lambda s: jnp.maximum(s - 2, 0))),
            ],
            "down_gate", (),
        )
        two = grads_in_parts(
            up_out_kernel, meta, features + 64,
            [
                (n_mlp, whole()), (d_up, columns(rows, third, lambda s: jnp.minimum(s, 2))),
                (flat_attended, whole()), (d_att, whole()), (gain_parts, whole()),
            ],
            "up_out", one[:1],
        )
        large = Total(meta, one, two)
        large.core()
        large.toward_first()
        after = [large.now]
    dq, *sent = attend_back(meta, queries, attended, d_heads, lse, cos, sin, keys, after)
    after = []
    if parted:
        large.first()
        sent = sent[:-1] + hold(meta, sent[-1:], [large.one])
        large.second()
    keys.cores(sent)
    keys.finish()
    if parted:
        after = large.now = hold(meta, large.now, keys.parts[1:])
    input_grad, *tail = last(
        meta, parted, tokens, normed, d_middle, dq, *first_weights, keys, after
    )
    if parted:
        large.chips([input_grad])
        small = Total(meta, hold(meta, tail, [large.now]))
        small.core()
        small.batch_at_once()
        large.back_chips([small.now])
        small.all_chips()
        block = lambda width, index: ((features, hidden), columns(features, width, index))
        fixed = lambda height: ((height, features), columns(height, features, lambda s: 0))
        grad_down, grad_gate, grad_up, grad_out, grad_query, grad_key, grad_value, d_gain_mlp, d_gain_attn = join(
            meta, spread(meta, jnp.concatenate([large.now, small.now], axis=-1)),
            [
                block(wide, lambda s: jnp.minimum(s, 1)), block(wide, lambda s: jnp.maximum(s - 2, 0)),
                block(third, lambda s: jnp.minimum(s, 2)),
                fixed(features), fixed(features), fixed(KEY_WIDTH), fixed(KEY_WIDTH), fixed(1), fixed(1),
            ],
            [pltpu.VMEM((features, features + 64), f32), pltpu.VMEM((4, features, 256), f32)],
        )
    else:
        gain_rows = gain_parts.reshape(-1, 8, features)[:, 0].sum(axis=0, keepdims=True)
        grad_down, grad_gate, grad_up, grad_out, grad_packed, d_gain_attn, d_gain_mlp = lax.psum(
            (
                dot(cut, act, TN), dot(n_mlp, d_gate, TN), dot(n_mlp, d_up, TN),
                dot(flat_attended, d_att, TN), tail[0], tail[1][0], gain_rows,
            ),
            ("seq", "batch"),
        )
        grad_query = grad_packed[:, :features]
        grad_key = grad_packed[:, features : features + KEY_WIDTH].T
        grad_value = grad_packed[:, features + KEY_WIDTH : features + PACKED].T
    return (
        block_out,
        input_grad,
        d_gain_attn.reshape(-1),
        grad_query,
        grad_key.T,
        grad_value.T,
        grad_out,
        d_gain_mlp.reshape(-1),
        grad_gate,
        grad_up,
        grad_down.T,
    )


def solution(mesh):
    rows = P("batch", None, "seq", None)
    return jax.shard_map(
        shards,
        mesh=mesh,
        in_specs=(rows, P("batch")) + (P(),) * 10 + (rows,),
        out_specs=(rows, rows) + (P(),) * 9,
        check_vma=False,
    )
```
